32 devices in a mesh: replica: 2 (over x), shard: 4 (over z), seq: 4 (over y, core).
Axes of the slice: x: 2, y: 2, z: 4, core: 2. Of those that a mesh axis runs over, the one named last changes fastest.
Arguments:
- activations: bfloat16 [8, 2, 1024, 1024], P(('replica', 'shard'), None, 'seq'), may hold values from -6 to 6
- cotangent: bfloat16 [8, 2, 1024, 1024], P(('replica', 'shard'), None, 'seq'), may hold values from -6 to 6
- clip_loads: int32 [8], P(('replica', 'shard')), may hold values from 1 to 2, as said below
- attn_gain: bfloat16 [1024], P('shard'), may hold values from 0.5 to 1.5
- attn_shift: bfloat16 [1024], P('shard'), may hold values from -1.5 to 1.5
- w_qkv: bfloat16 [1024, 3072], P('shard'), may hold values from -0.1875 to 0.1875
- q_bias: bfloat16 [1024], P('shard'), may hold values from -1.5 to 1.5
- v_bias: bfloat16 [1024], P('shard'), may hold values from -1.5 to 1.5
- w_out: bfloat16 [1024, 1024], P('shard'), may hold values from -0.75 to 0.75
- out_bias: bfloat16 [1024], P('shard'), may hold values from -1.5 to 1.5
- mlp_gain: bfloat16 [1024], P('shard'), may hold values from 0.5 to 1.5
- mlp_shift: bfloat16 [1024], P('shard'), may hold values from -1.5 to 1.5
- w_up: bfloat16 [1024, 4096], P('shard'), may hold values from -0.1875 to 0.1875
- up_bias: bfloat16 [4096], P('shard'), may hold values from -1.5 to 1.5
- w_down: bfloat16 [4096, 1024], P('shard'), may hold values from -0.09375 to 0.09375
- down_bias: bfloat16 [1024], P('shard'), may hold values from -1.5 to 1.5
Outputs:
- layer_out: bfloat16 [8, 2, 1024, 1024], P(('replica', 'shard'), None, 'seq')
- input_grad: bfloat16 [8, 2, 1024, 1024], P(('replica', 'shard'), None, 'seq')
- grad_attn_gain: float32 [1024], P(('shard', 'seq'))
- grad_attn_shift: float32 [1024], P(('shard', 'seq'))
- grad_w_qkv: float32 [1024, 3072], P(('shard', 'seq'))
- grad_q_bias: float32 [1024], P(('shard', 'seq'))
- grad_v_bias: float32 [1024], P(('shard', 'seq'))
- grad_w_out: float32 [1024, 1024], P(('shard', 'seq'))
- grad_out_bias: float32 [1024], P(('shard', 'seq'))
- grad_mlp_gain: float32 [1024], P(('shard', 'seq'))
- grad_mlp_shift: float32 [1024], P(('shard', 'seq'))
- grad_w_up: float32 [1024, 4096], P(('shard', 'seq'))
- grad_up_bias: float32 [4096], P(('shard', 'seq'))
- grad_w_down: float32 [4096, 1024], P(('shard', 'seq'))
- grad_down_bias: float32 [1024], P(('shard', 'seq'))
The draws below stay inside these ranges and needn't reach their ends.
Inputs may be any that keep to these rules, and one draw needn't show every extreme that they name: Group g holds live clips in its first clip_loads[g] of 2 slots; the remaining slots are empty.
All inputs are finite; a program needn't handle non-finite values.
Results may differ from the reference program's by a relative error of at most 0.014.
Values may be sent and summed in bfloat16 or wider, within the bound.
A program may use at most 256 MiB of HBM per device.

```python
import jax
import jax.numpy as jnp
from jax import lax

HEADS = 16
HEAD_DIM = 64
D = 1024
FF = 4096
MB = 2
CLIP = 1024
GROUPS = 8


def draw_clip_loads(key, part):
    key = jax.random.fold_in(key, 11)
    pick_key, heavy_key, ranking_key = jax.random.split(key, 3)
    heavier = jax.random.randint(heavy_key, (GROUPS,), 2, MB + 1)
    choose = jax.random.randint(pick_key, (GROUPS,), 0, 2)
    loads_drawn = jnp.where(choose == 0, 1, heavier)
    ranking = jax.random.permutation(ranking_key, GROUPS)
    loads_drawn = loads_drawn.at[ranking[0]].set(MB).at[ranking[1]].set(1)
    return loads_drawn.astype(jnp.int32)


def shard_levels(stream_key, extent, cuts, low, largest):
    loudness, own = 1.0, jax.random.fold_in(stream_key, 6)
    for axis_at, parts in cuts:
        steps = jnp.exp(jax.random.uniform(jax.random.fold_in(own, axis_at), (parts,), jnp.float32, low / len(cuts), largest / len(cuts)))
        loudness = loudness * jnp.repeat(steps, extent[axis_at] // parts).reshape([-1 if axis == axis_at else 1 for axis in range(len(extent))])
    return loudness


def noise(stream_key, shape, scale, reach, shards=(), held_as=jnp.bfloat16):
    result = jax.random.normal(stream_key, shape, jnp.float32) * scale
    if len(shards) > 0:
        result = shard_levels(stream_key, shape, shards, -0.22, 0.18) * result
    return jnp.clip(result, min=-reach, max=reach).astype(held_as)


def setup_inputs(seed: int = 0) -> dict:
    key_of = jax.random.split(jax.random.key(seed), 17)
    return {
        "activations": noise(key_of[0], (GROUPS, MB, CLIP, D), 1.0, 6.0, ((0, 8), (2, 4))),
        "cotangent": noise(key_of[1], (GROUPS, MB, CLIP, D), 1.0, 6.0, ((0, 8), (2, 4))),
        "clip_loads": draw_clip_loads(jax.random.fold_in(key_of[16], 71), 0),
        "attn_gain": jnp.clip(1.0 + 0.1 * jax.random.normal(key_of[3], (D,), jnp.float32), 0.5, 1.5).astype(jnp.bfloat16),
        "attn_shift": noise(key_of[4], (D,), 0.3, 1.5, ((0, 4),)),
        "w_qkv": noise(key_of[5], (D, 3 * D), D ** -0.5, 0.1875, ((0, 4),)),
        "q_bias": noise(key_of[6], (D,), 0.3, 1.5, ((0, 4),)),
        "v_bias": noise(key_of[7], (D,), 0.3, 1.5, ((0, 4),)),
        "w_out": noise(key_of[8], (D, D), (D // 16) ** -0.5, 0.75, ((0, 4),)),
        "out_bias": noise(key_of[9], (D,), 0.3, 1.5, ((0, 4),)),
        "mlp_gain": jnp.clip(1.0 + 0.1 * jax.random.normal(key_of[10], (D,), jnp.float32), 0.5, 1.5).astype(jnp.bfloat16),
        "mlp_shift": noise(key_of[11], (D,), 0.3, 1.5, ((0, 4),)),
        "w_up": noise(key_of[12], (D, FF), D ** -0.5, 0.1875, ((0, 4),)),
        "up_bias": noise(key_of[13], (FF,), 0.3, 1.5, ((0, 4),)),
        "w_down": noise(key_of[14], (FF, D), FF ** -0.5, 0.09375, ((0, 4),)),
        "down_bias": noise(key_of[15], (D,), 0.3, 1.5, ((0, 4),)),
    }


@jax.custom_vjp
def low(v):
    return lax.optimization_barrier(v.astype(jnp.bfloat16)).astype(jnp.float32)

@jax.custom_vjp
def low_back(v):
    return v

def low_keep(v):
    return (low(v), None)

def low_pass(kept, grad):
    return (grad,)

def back_keep(v):
    return (v, None)

def back_low(kept, grad):
    return (low(grad),)
low.defvjp(low_keep, low_pass)
low_back.defvjp(back_keep, back_low)
EPSILON = 1e-06

def layer_norm(values, gain, shift):
    center = values - lax.optimization_barrier(jnp.mean(values, axis=-1, keepdims=True))
    spread = lax.optimization_barrier(jnp.mean(center * center, axis=-1, keepdims=True))
    return center * lax.rsqrt(spread + EPSILON) * gain + shift

def matmul_high(left, right):
    return jnp.dot(left, right, precision=lax.Precision.HIGHEST, preferred_element_type=jnp.float32)

def clip_forward(params, clip):
    attn_gain, attn_shift, w_qkv, q_bias, v_bias, w_out, out_bias, mlp_gain, mlp_shift, w_up, up_bias, w_down, down_bias = params
    length = clip.shape[0]
    width = clip.shape[1]
    score_scale = HEAD_DIM ** (-0.5)
    normed = low(layer_norm(clip, attn_gain, attn_shift))
    bias_row = jnp.concatenate([q_bias, jnp.zeros_like(q_bias), v_bias])
    project = low(low_back(matmul_high(normed, w_qkv) + bias_row))
    queries = project[:, :width].reshape(length, HEADS, HEAD_DIM)
    key_rows = project[:, width:2 * width].reshape(length, HEADS, HEAD_DIM)
    value_rows = project[:, 2 * width:].reshape(length, HEADS, HEAD_DIM)
    scores = low_back(jnp.einsum('thd,lhd->htl', queries, key_rows, precision=lax.Precision.HIGHEST) * score_scale)
    softmax_low = low(jax.nn.softmax(scores, axis=-1))
    attended = jnp.einsum('htl,lhd->thd', softmax_low, value_rows, precision=lax.Precision.HIGHEST).reshape(length, width)
    attended = low(low_back(attended))
    residual = clip + low_back(matmul_high(attended, w_out) + out_bias)
    normed_mlp = low(layer_norm(residual, mlp_gain, mlp_shift))
    pre_act = low_back(matmul_high(normed_mlp, w_up) + up_bias)
    activated = low(jax.nn.gelu(pre_act, approximate=False))
    return residual + low_back(matmul_high(activated, w_down) + down_bias)

def reference(activations, cotangent, clip_loads, attn_gain, attn_shift, w_qkv, q_bias, v_bias, w_out, out_bias, mlp_gain, mlp_shift, w_up, up_bias, w_down, down_bias):
    params = tuple((weight.astype(jnp.float32) for weight in (attn_gain, attn_shift, w_qkv, q_bias, v_bias, w_out, out_bias, mlp_gain, mlp_shift, w_up, up_bias, w_down, down_bias)))
    width = activations.shape[3]
    clips = activations.astype(jnp.float32).reshape(GROUPS * MB, CLIP, width)
    is_live = (jnp.arange(MB, dtype=jnp.int32)[None, :] < clip_loads[:, None]).astype(jnp.float32)
    is_live = is_live.reshape(GROUPS * MB, 1, 1)
    step_fn = jax.checkpoint(clip_forward)

    def run_layer(weights, inputs):

        def scan_step(carry, clip):
            return (carry, step_fn(weights, clip))
        _, outputs = lax.scan(scan_step, jnp.float32(0.0), inputs)
        return outputs
    outputs, pull = jax.vjp(run_layer, params, clips)
    out_grads = cotangent.astype(jnp.float32).reshape(GROUPS * MB, CLIP, width) * is_live
    weight_grads, input_grads = pull(out_grads)
    layer_out = (outputs * is_live).astype(jnp.bfloat16).reshape(activations.shape)
    input_grad = input_grads.astype(jnp.bfloat16).reshape(activations.shape)
    return (layer_out, input_grad, weight_grads[0], weight_grads[1], weight_grads[2], weight_grads[3], weight_grads[4], weight_grads[5], weight_grads[6], weight_grads[7], weight_grads[8], weight_grads[9], weight_grads[10], weight_grads[11], weight_grads[12])
```

```python
import functools

import jax
import jax.numpy as jnp
from jax import lax
from jax.experimental import pallas as pl
from jax.experimental.pallas import tpu as pltpu
from jax.sharding import PartitionSpec as P

MESH = pl.DeviceIdType.MESH
BF = jnp.bfloat16
F32 = jnp.float32
HEAD_DIM = 64
PAIR = 2 * HEAD_DIM
EPSILON = 1e-06
NN = (((1,), (0,)), ((), ()))
NT = (((1,), (1,)), ((), ()))
TN = (((0,), (0,)), ((), ()))
MIB = 2**20


def dot(a, b, dims=NN):
    return lax.dot_general(a, b, dims, preferred_element_type=F32)


class Place:
    def __init__(self, shards):
        self.shards = shards
        r, self.z, q = (lax.axis_index(a) for a in ("replica", "shard", "seq"))
        self.x, self.y, self.c = r % 2, q // 2, q % 2
        self.q = q
        self.to_x = {"replica": r + 1 - 2 * self.x}
        self.to_y = {"seq": q + 2 - 4 * self.y}
        self.to_c = {"seq": q + 1 - 2 * self.c}

    def to_z(self, shift):
        return {"shard": (self.z + shift) % self.shards}

    def behind(self, shift):
        return (self.z + self.shards - shift) % self.shards

    def greet(self):
        barrier = pltpu.get_barrier_semaphore()
        peers = [self.to_x, self.to_y, self.to_c]
        peers += [self.to_z(shift) for shift in range(1, self.shards)]
        for peer in peers:
            pl.semaphore_signal(barrier, inc=1, device_id=peer, device_id_type=MESH)
        pl.semaphore_wait(barrier, len(peers))


class Copies:
    def __init__(self, send_sems, recv_sems, local_sems):
        self.send_sems, self.recv_sems, self.local_sems = send_sems, recv_sems, local_sems
        self.remote, self.local = [], []

    def send(self, src, dst, peer):
        at = len(self.remote)
        copy = pltpu.make_async_remote_copy(
            src_ref=src, dst_ref=dst, send_sem=self.send_sems.at[at], recv_sem=self.recv_sems.at[at],
            device_id=peer, device_id_type=MESH,
        )
        copy.start()
        self.remote.append(copy)
        return copy

    def move(self, src, dst):
        at = len(self.local)
        copy = pltpu.make_async_copy(src, dst, self.local_sems.at[at])
        copy.start()
        self.local.append([copy, False])
        return self.local[-1]

    def wait(self, moves):
        for entry in moves:
            if not entry[1]:
                entry[0].wait()
                entry[1] = True

    def finish(self):
        for copy in self.remote:
            copy.wait_send()
        self.wait(self.local)


def normalized(values, gain, shift):
    center = values - jnp.mean(values, axis=-1, keepdims=True)
    spread = jnp.mean(center * center, axis=-1, keepdims=True)
    return center * lax.rsqrt(spread + EPSILON) * gain + shift


def head_masks(rows):
    lane = lax.broadcasted_iota(jnp.int32, (rows, PAIR), 1)
    first = (lane < HEAD_DIM).astype(F32).astype(BF)
    return first, (lane >= HEAD_DIM).astype(F32).astype(BF)


def both_heads(values, masks):
    return jnp.concatenate([values * masks[0], values * masks[1]], axis=0)


N_REMOTE1, N_LOCAL1 = 128, 80


def forward_kernel(
    shards,
    x_in, small_in, wq_in, wo_in, wu_in, wd_in,
    wq_all, wo_all, wu_all, wd_all,
    normed_out, q_out, kv_out, lse_out, att_out, res_out, nm_out, act_out, slope_out, small_out,
    xv, smv, normed, qv, kvb, lsev, att, res, nm, act, slope, wq, wo, wu,
    send_sems, recv_sems, local_sems,
):
    place = Place(shards)
    net = Copies(send_sems, recv_sems, local_sems)
    x, y, z, c = place.x, place.y, place.z, place.c
    slots, length, width = x_in.shape
    tokens = slots * length
    hidden = wu_in.shape[1]
    shard_rows = wq_in.shape[0]
    place.greet()

    small_moves = [net.move(small_in, smv.at[z])]
    small_sends = [net.send(small_in, smv.at[z], place.to_z(s)) for s in range(1, shards)]
    x_moves = [net.move(x_in, xv.at[0])]
    x_send = net.send(x_in, xv.at[1], place.to_y)

    def piece_rows(chunk, px, py, pc, lo=0, n=None):
        _, _, _, _, piece, rows, at = chunk
        n = rows if n is None else n
        return pl.ds(pl.multiple_of(((px * 2 + py) * 2 + pc) * piece + at + lo, 16), n)

    half = hidden // 2
    p32, pdn = shard_rows // 8, wd_in.shape[0] // 8
    chunks = [
        (wq_in, wq_all, width, width, p32, p32, 0),
        (wq_in, wq_all, 2 * width, width, p32, p32, 0),
        (wq_in, wq_all, 0, width, p32, p32, 0),
        (wo_in, wo_all, 0, width, p32, p32, 0),
        (wu_in, wu_all, 0, half, p32, p32, 0),
        (wu_in, wu_all, half, half, p32, p32, 0),
        (wd_in, wd_all, 0, width, pdn, pdn // 2, 0),
        (wd_in, wd_all, 0, width, pdn, pdn // 2, pdn // 2),
    ]
    state = [dict() for _ in chunks]
    others = pl.ds(1, shards - 1)

    def start_z(i):
        src, all_, col, cols, *_ = ch = chunks[i]
        rows = piece_rows(ch, x, y, c)
        cs = pl.ds(col, cols)
        state[i]["z"] = [
            net.send(src.at[rows, cs], all_.at[s, rows, cs], place.to_z(s)) for s in range(1, shards)
        ]

    def pass_piece(i, px, py, pc, lo, n, peer):
        _, all_, col, cols, *_ = ch = chunks[i]
        ref = all_.at[others, piece_rows(ch, px, py, pc, lo, n), pl.ds(col, cols)]
        return net.send(ref, ref, peer)

    def plane_one(i):
        rows = chunks[i][5]
        st = state[i]
        for copy in st["z"]:
            copy.wait_recv()
        st["x"] = pass_piece(i, x, y, c, 0, rows, place.to_x)
        st["y"] = pass_piece(i, x, y, c, 0, rows, place.to_y)
        st["core"] = [pass_piece(i, x, y, c, 0, rows, place.to_c)]

    def plane_two(i):
        rows = chunks[i][5]
        st = state[i]
        st["x"].wait_recv()
        st["xy"] = pass_piece(i, 1 - x, y, c, 0, rows // 2, place.to_y)
        st["core"].append(pass_piece(i, 1 - x, y, c, 0, rows, place.to_c))
        st["y"].wait_recv()
        st["yx"] = pass_piece(i, x, 1 - y, c, rows // 2, rows // 2, place.to_x)
        st["core"].append(pass_piece(i, x, 1 - y, c, 0, rows, place.to_c))

    def plane_three(i):
        rows = chunks[i][5]
        st = state[i]
        st["xy"].wait_recv()
        st["core"].append(pass_piece(i, 1 - x, 1 - y, c, 0, rows // 2, place.to_c))
        st["yx"].wait_recv()
        st["core"].append(pass_piece(i, 1 - x, 1 - y, c, rows // 2, rows // 2, place.to_c))

    def arrived(i):
        for copy in state[i]["core"]:
            copy.wait_recv()

    def load(i, dst):
        src, all_, col, cols, *_ = chunks[i]
        moves = []
        for s in range(shards):
            rows = pl.ds(pl.multiple_of(place.behind(s) * shard_rows, shard_rows), shard_rows)
            cs = pl.ds(col, cols)
            from_ = src.at[:, cs] if s == 0 else all_.at[s, :, cs]
            moves.append(net.move(from_, dst.at[rows, cs]))
        return moves

    start_z(0)
    start_z(1)

    net.wait(small_moves)
    for copy in small_sends:
        copy.wait_recv()
    small_moves = [net.move(smv, small_out)]

    def small(row, count=1):
        return jnp.concatenate([smv[s] for s in range(shards)], axis=1)[row : row + count].astype(F32)

    def norm_first(which):
        gain, shift = small(0), small(1)
        for slot in range(slots):
            rows = pl.ds(slot * length, length)
            normed[which, rows, :] = normalized(xv[which, slot].astype(F32), gain, shift).astype(BF)

    net.wait(x_moves)
    norm_first(0)
    plane_one(0)
    start_z(2)
    plane_one(1)
    plane_two(0)
    start_z(3)
    x_send.wait_recv()
    norm_first(1)
    moves_out = [net.move(normed, normed_out)]
    plane_one(2)
    plane_two(1)
    plane_three(0)
    start_z(4)
    arrived(0)
    k_moves = load(0, wq)
    plane_one(3)
    plane_two(2)
    plane_three(1)
    start_z(5)
    arrived(1)
    v_moves = load(1, wq)
    net.wait(k_moves)

    v_bias = small(3)

    def project_kv(which, part):
        lanes = pl.ds((part + 1) * width, width)
        rows = normed[which]
        out = dot(rows, wq[:, lanes])
        if part:
            out = out + v_bias
        out = out.astype(BF)
        at = (y if which == 0 else 1 - y) * 2 + c
        for slot in range(slots):
            kvb[slot, at, :, pl.ds(part * width, width)] = out[slot * length : (slot + 1) * length]

    shares = []

    def share(part):
        for which in range(2):
            at = (y if which == 0 else 1 - y) * 2 + c
            ref = kvb.at[:, at, :, pl.ds(part * width, width)]
            shares.append(net.send(ref, ref, place.to_c))

    project_kv(0, 0)
    project_kv(1, 0)
    share(0)
    plane_one(4)
    plane_two(3)
    plane_three(2)
    start_z(6)
    arrived(2)
    q_moves = load(2, wq)
    net.wait(v_moves)
    project_kv(0, 1)
    project_kv(1, 1)
    share(1)
    plane_three(3)
    arrived(3)
    o_moves = load(3, wo)
    net.wait(q_moves)
    qv[...] = (dot(normed[0], wq[:, :width]) + small(2)).astype(BF)
    moves_out.append(net.move(qv, q_out))
    plane_one(5)
    plane_two(4)
    start_z(7)
    for copy in shares:
        copy.wait_recv()
    moves_out.append(net.move(kvb, kv_out))

    def attend(slot, lo, hi):
        masks = head_masks(length)

        @pl.loop(lo, hi)
        def _(p):
            lanes = pl.ds(pl.multiple_of(p * PAIR, PAIR), PAIR)
            v_lanes = pl.ds(pl.multiple_of(width + p * PAIR, PAIR), PAIR)
            rows = pl.ds(slot * length, length)
            queries = both_heads(qv[rows, lanes] * BF(HEAD_DIM**-0.5), masks)
            keys = kvb[slot, :, :, lanes].reshape(-1, PAIR)
            values = kvb[slot, :, :, v_lanes].reshape(-1, PAIR)
            scores = dot(keys, queries, NT)
            top = jnp.max(scores, axis=0, keepdims=True)
            terms = jnp.exp(scores - top)
            total = jnp.sum(terms, axis=0, keepdims=True)
            lsev[slot, p] = top + jnp.log(total)
            out = dot(values, terms.astype(BF), TN) * (1.0 / total)
            out = jnp.concatenate([out[:HEAD_DIM, :length], out[HEAD_DIM:, length:]], axis=0)
            att[rows, lanes] = out.T.astype(BF)

    pairs = width // PAIR
    attend(0, 0, pairs)
    plane_one(6)
    plane_two(5)
    plane_three(4)
    arrived(4)
    up_moves = [load(4, wu)]
    attend(1, 0, pairs)
    moves_out += [net.move(lsev, lse_out), net.move(att, att_out)]
    plane_one(7)
    plane_two(6)
    plane_three(5)
    arrived(5)
    up_moves.append(load(5, wu))

    net.wait(o_moves)
    out_bias, mlp_gain, mlp_shift = small(4), small(5), small(6)
    for slot in range(slots):
        rows = pl.ds(slot * length, length)
        value = xv[0, slot].astype(F32) + dot(att[rows], wo[...]) + out_bias
        res[rows] = value
        nm[rows] = normalized(value, mlp_gain, mlp_shift).astype(BF)
    moves_out += [net.move(res, res_out), net.move(nm, nm_out)]

    up_block = 512

    def up(part):
        @pl.loop(part * (half // up_block), (part + 1) * (half // up_block))
        def _(j):
            lanes = pl.ds(pl.multiple_of(j * up_block, up_block), up_block)
            s, inner = j // (wd_in.shape[0] // up_block), j % (wd_in.shape[0] // up_block)
            first = 8 + inner * (up_block // shard_rows)
            sm = smv[s].astype(F32)
            row = jnp.concatenate([sm[8:9], sm[9:10]], axis=1)
            row2 = jnp.concatenate([sm[10:11], sm[11:12]], axis=1)
            bias = jnp.where(inner == 0, row, row2)
            pre = dot(nm[...], wu[:, lanes]) + bias
            phi = 0.5 + 0.5 * lax.erf(pre * (0.5**0.5))
            density = jnp.exp(pre * pre * -0.5) * 0.3989422804014327
            act[:, lanes] = (pre * phi).astype(BF)
            slope[:, lanes] = (phi + pre * density).astype(BF)

    net.wait(up_moves[0])
    up(0)
    plane_two(7)
    plane_three(6)
    net.wait(up_moves[1])
    up(1)
    moves_out += [net.move(act, act_out), net.move(slope, slope_out)]
    plane_three(7)
    arrived(6)
    arrived(7)
    net.finish()


def forward(shards, x, small, wq, wo, wu, wd):
    slots, length, width = x.shape
    tokens = slots * length
    rows = wq.shape[0]
    hidden = wu.shape[1]
    pairs = width // PAIR
    clip = 4 * length
    any_ = pl.BlockSpec(memory_space=pl.ANY)
    sd = jax.ShapeDtypeStruct
    outs = (
        sd((shards,) + wq.shape, BF), sd((shards,) + wo.shape, BF), sd((shards,) + wu.shape, BF), sd((shards,) + wd.shape, BF),
        sd((2, tokens, width), BF), sd((tokens, width), BF), sd((slots, 4, length, 2 * width), BF),
        sd((slots, pairs, 1, 2 * length), F32), sd((tokens, width), BF), sd((tokens, width), F32),
        sd((tokens, width), BF), sd((tokens, hidden), BF), sd((tokens, hidden), BF), sd((shards,) + small.shape, BF),
    )
    return pl.pallas_call(
        functools.partial(forward_kernel, shards),
        out_shape=outs,
        in_specs=[any_] * 6,
        out_specs=(any_,) * len(outs),
        scratch_shapes=[
            pltpu.VMEM((2, slots, length, width), BF),
            pltpu.VMEM((shards,) + small.shape, BF),
            pltpu.VMEM((2, tokens, width), BF),
            pltpu.VMEM((tokens, width), BF),
            pltpu.VMEM((slots, 4, length, 2 * width), BF),
            pltpu.VMEM((slots, pairs, 1, 2 * length), F32),
            pltpu.VMEM((tokens, width), BF),
            pltpu.VMEM((tokens, width), F32),
            pltpu.VMEM((tokens, width), BF),
            pltpu.VMEM((tokens, hidden), BF),
            pltpu.VMEM((tokens, hidden), BF),
            pltpu.VMEM((width, 3 * width), BF),
            pltpu.VMEM((width, width), BF),
            pltpu.VMEM((width, hidden), BF),
            pltpu.SemaphoreType.DMA((N_REMOTE1,)),
            pltpu.SemaphoreType.DMA((N_REMOTE1,)),
            pltpu.SemaphoreType.DMA((N_LOCAL1,)),
        ],
        compiler_params=pltpu.CompilerParams(collective_id=1, has_side_effects=True, vmem_limit_bytes=62 * MIB),
    )(x, small, wq, wo, wu, wd)


def contract_rows(left, right):
    return lax.dot_general(left, right, TN, preferred_element_type=F32)


def contract_cols(left, right):
    return lax.dot_general(left, right, NT, preferred_element_type=F32)


def row_total(values):
    return jnp.sum(values.astype(F32), axis=0)


def norm_pull(values, gain, shift, incoming):
    _, pull = jax.vjp(normalized, values, gain, shift)
    return pull(incoming)


def local(
    activations, cotangent, clip_loads, attn_gain, attn_shift, w_qkv, q_bias, v_bias, w_out, out_bias,
    mlp_gain, mlp_shift, w_up, up_bias, w_down, down_bias,
):
    shards = lax.axis_size("shard")
    z = lax.axis_index("shard")
    x = activations[0]
    slots, length, width = x.shape
    tokens = slots * length
    heads = width // HEAD_DIM
    rows = w_qkv.shape[0]
    vectors = [attn_gain, attn_shift, q_bias, v_bias, out_bias, mlp_gain, mlp_shift, down_bias]
    small = jnp.concatenate([jnp.stack(vectors), up_bias.reshape(-1, rows)], axis=0)
    small = jnp.pad(small, ((0, 16 - small.shape[0]), (0, 0)))
    (wq, wo, wu, wd, normed, q, kv, lse, att, res, nm, act, slope, smalls) = forward(
        shards, x, small, w_qkv, w_out, w_up, w_down
    )
    order = (z - jnp.arange(shards)) % shards

    def whole(gathered, own):
        return gathered.at[0].set(own)[order].reshape((-1,) + own.shape[1:])

    wq, wo, wu, wd = whole(wq, w_qkv), whole(wo, w_out), whole(wu, w_up), whole(wd, w_down)
    full = jnp.concatenate([smalls[s] for s in range(shards)], axis=1).astype(F32)
    live = (jnp.arange(slots) < clip_loads[0]).astype(F32)[:, None, None]
    live = jnp.broadcast_to(live, (slots, length, 1)).reshape(tokens, 1)
    out_grad = cotangent[0].reshape(tokens, width).astype(F32) * live
    layer_out = (live * (res + jnp.dot(act, wd, preferred_element_type=F32) + full[7:8])).astype(BF)
    d_mlp = out_grad.astype(BF)
    grad_w_down = contract_rows(act, d_mlp)
    grad_down_bias = row_total(d_mlp)
    d_pre = (contract_cols(d_mlp, wd) * slope.astype(F32)).astype(BF)
    grad_w_up = contract_rows(nm, d_pre)
    grad_up_bias = row_total(d_pre)
    d_norm = contract_cols(d_pre, wu)
    d_res_norm, grad_mlp_gain, grad_mlp_shift = norm_pull(res, full[5], full[6], d_norm)
    d_residual = out_grad + d_res_norm
    d_branch = d_residual.astype(BF)
    grad_w_out = contract_rows(att, d_branch)
    grad_out_bias = row_total(d_branch)
    d_att = contract_cols(d_branch, wo).astype(BF)
    scale = HEAD_DIM**-0.5
    d_q, d_kv = [], []
    for slot in range(slots):
        span = slice(slot * length, (slot + 1) * length)
        queries = q[span].reshape(length, heads, HEAD_DIM)
        keys = kv[slot, :, :, :width].reshape(-1, heads, HEAD_DIM)
        values = kv[slot, :, :, width:].reshape(-1, heads, HEAD_DIM)
        d_a = d_att[span].reshape(length, heads, HEAD_DIM)
        logs = lse[slot].reshape(heads, length)
        scores = jnp.einsum("thd,lhd->htl", queries, keys, preferred_element_type=F32) * scale
        probs = jnp.exp(scores - logs[:, :, None])
        d_probs = jnp.einsum("thd,lhd->htl", d_a, values, preferred_element_type=F32)
        d_scores = (probs * (d_probs - jnp.sum(probs * d_probs, axis=-1, keepdims=True))).astype(BF)
        d_q.append(jnp.einsum("htl,lhd->thd", d_scores, keys, preferred_element_type=F32).reshape(length, width) * scale)
        d_k = jnp.einsum("htl,thd->lhd", d_scores, queries, preferred_element_type=F32) * scale
        d_v = jnp.einsum("htl,thd->lhd", probs.astype(BF), d_a, preferred_element_type=F32)
        d_kv.append(jnp.concatenate([d_k.reshape(-1, width), d_v.reshape(-1, width)], axis=1).astype(BF))
    d_q = jnp.concatenate(d_q).astype(BF)
    d_kv = jnp.stack(d_kv).reshape(slots, 4, length, 2 * width)
    d_kv = lax.psum_scatter(d_kv, "seq", scatter_dimension=1, tiled=True).reshape(tokens, 2 * width)
    d_project = jnp.concatenate([d_q, d_kv], axis=1)
    grad_w_qkv = contract_rows(normed[0], d_project)
    grad_q_bias = row_total(d_q)
    grad_v_bias = row_total(d_kv[:, width:])
    d_norm1 = contract_cols(d_project, wq)
    d_in, grad_attn_gain, grad_attn_shift = norm_pull(x.reshape(tokens, width).astype(F32), full[0], full[1], d_norm1)
    input_grad = (d_residual + d_in).astype(BF)

    def scatter(value):
        value = lax.psum_scatter(value.astype(BF), ("shard", "seq"), scatter_dimension=0, tiled=True)
        return lax.psum(value, "replica").astype(F32)

    def total(value):
        value = lax.psum(value, ("replica", "shard", "seq"))
        n = value.shape[0] // (shards * lax.axis_size("seq"))
        at = z * lax.axis_size("seq") + lax.axis_index("seq")
        return lax.dynamic_slice_in_dim(value, at * n, n)

    shape = activations.shape
    return (
        layer_out.reshape(shape), input_grad.reshape(shape), total(grad_attn_gain), total(grad_attn_shift),
        scatter(grad_w_qkv), total(grad_q_bias), total(grad_v_bias), scatter(grad_w_out), total(grad_out_bias),
        total(grad_mlp_gain), total(grad_mlp_shift), scatter(grad_w_up), total(grad_up_bias),
        scatter(grad_w_down), total(grad_down_bias),
    )


def solution(mesh):
    rows = P("shard")
    full = P("shard", None)
    clips = P(("replica", "shard"), None, "seq", None)
    vec = P(("shard", "seq"))
    mat = P(("shard", "seq"), None)
    return jax.shard_map(
        local,
        mesh=mesh,
        in_specs=(
            clips, clips, P(("replica", "shard")), rows, rows, full, rows, rows, full, rows, rows, rows, full, rows, full, rows,
        ),
        out_specs=(clips, clips, vec, vec, mat, vec, vec, mat, vec, vec, vec, mat, vec, mat, vec),
        check_vma=False,
    )
```

```python
import functools
import jax
import jax.numpy as jnp
from jax import lax
from jax.experimental import pallas as pl
from jax.experimental.pallas import tpu as pltpu
from jax.sharding import PartitionSpec as P

MESH = pl.DeviceIdType.MESH
BF = jnp.bfloat16
F32 = jnp.float32
HEAD_DIM = 64
PAIR = 2 * HEAD_DIM
EPSILON = 1e-06
NN = (((1,), (0,)), ((), ()))
NT = (((1,), (1,)), ((), ()))
TN = (((0,), (0,)), ((), ()))
MIB = 2**20


def dot(a, b, dims=NN):
    return lax.dot_general(a, b, dims, preferred_element_type=F32)


class Place:
    def __init__(self, shards):
        self.shards = shards
        r, self.z, q = (lax.axis_index(a) for a in ("replica", "shard", "seq"))
        self.x, self.y, self.c = r % 2, q // 2, q % 2
        self.q = q
        self.to_x = {"replica": r + 1 - 2 * self.x}
        self.to_y = {"seq": q + 2 - 4 * self.y}
        self.to_c = {"seq": q + 1 - 2 * self.c}

    def to_z(self, shift):
        return {"shard": (self.z + shift) % self.shards}

    def behind(self, shift):
        return (self.z + self.shards - shift) % self.shards

    def greet(self):
        barrier = pltpu.get_barrier_semaphore()
        peers = [self.to_x, self.to_y, self.to_c]
        peers += [self.to_z(shift) for shift in range(1, self.shards)]
        for peer in peers:
            pl.semaphore_signal(barrier, inc=1, device_id=peer, device_id_type=MESH)
        pl.semaphore_wait(barrier, len(peers))


class Copies:
    def __init__(self, send_sems, recv_sems, local_sems):
        self.send_sems, self.recv_sems, self.local_sems = send_sems, recv_sems, local_sems
        self.remote, self.local = [], []

    def send(self, src, dst, peer):
        at = len(self.remote)
        copy = pltpu.make_async_remote_copy(
            src_ref=src, dst_ref=dst, send_sem=self.send_sems.at[at], recv_sem=self.recv_sems.at[at],
            device_id=peer, device_id_type=MESH,
        )
        copy.start()
        self.remote.append(copy)
        return copy

    def move(self, src, dst):
        at = len(self.local)
        copy = pltpu.make_async_copy(src, dst, self.local_sems.at[at])
        copy.start()
        self.local.append([copy, False])
        return self.local[-1]

    def wait(self, moves):
        for entry in moves:
            if not entry[1]:
                entry[0].wait()
                entry[1] = True

    def finish(self):
        for copy in self.remote:
            copy.wait_send()
        self.wait(self.local)


def normalized(values, gain, shift):
    center = values - jnp.mean(values, axis=-1, keepdims=True)
    spread = jnp.mean(center * center, axis=-1, keepdims=True)
    return center * lax.rsqrt(spread + EPSILON) * gain + shift


def head_masks(rows):
    lane = lax.broadcasted_iota(jnp.int32, (rows, PAIR), 1)
    first = (lane < HEAD_DIM).astype(F32).astype(BF)
    return first, (lane >= HEAD_DIM).astype(F32).astype(BF)


def both_heads(values, masks):
    return jnp.concatenate([values * masks[0], values * masks[1]], axis=0)


N_REMOTE1, N_LOCAL1 = 128, 80


def forward_kernel(
    shards,
    x_in, small_in, wq_in, wo_in, wu_in, wd_in,
    wq_all, wo_all, wu_all, wd_all,
    normed_out, q_out, kv_out, lse_out, att_out, res_out, nm_out, act_out, slope_out, small_out,
    xv, smv, normed, qv, kvb, lsev, att, res, nm, act, slope, wq, wo, wu,
    send_sems, recv_sems, local_sems,
):
    place = Place(shards)
    net = Copies(send_sems, recv_sems, local_sems)
    x, y, z, c = place.x, place.y, place.z, place.c
    slots, length, width = x_in.shape
    tokens = slots * length
    hidden = wu_in.shape[1]
    shard_rows = wq_in.shape[0]
    place.greet()

    small_moves = [net.move(small_in, smv.at[z])]
    small_sends = [net.send(small_in, smv.at[z], place.to_z(s)) for s in range(1, shards)]
    x_moves = [net.move(x_in, xv.at[0])]
    x_send = net.send(x_in, xv.at[1], place.to_y)

    def piece_rows(chunk, px, py, pc, lo=0, n=None):
        _, _, _, _, piece, rows, at = chunk
        n = rows if n is None else n
        return pl.ds(pl.multiple_of(((px * 2 + py) * 2 + pc) * piece + at + lo, 16), n)

    half = hidden // 2
    p32, pdn = shard_rows // 8, wd_in.shape[0] // 8
    chunks = [
        (wq_in, wq_all, width, width, p32, p32, 0),
        (wq_in, wq_all, 2 * width, width, p32, p32, 0),
        (wq_in, wq_all, 0, width, p32, p32, 0),
        (wo_in, wo_all, 0, width, p32, p32, 0),
        (wu_in, wu_all, 0, half, p32, p32, 0),
        (wu_in, wu_all, half, half, p32, p32, 0),
        (wd_in, wd_all, 0, width, pdn, pdn // 2, 0),
        (wd_in, wd_all, 0, width, pdn, pdn // 2, pdn // 2),
    ]
    state = [dict() for _ in chunks]
    others = pl.ds(1, shards - 1)

    def start_z(i):
        src, all_, col, cols, *_ = ch = chunks[i]
        rows = piece_rows(ch, x, y, c)
        cs = pl.ds(col, cols)
        state[i]["z"] = [
            net.send(src.at[rows, cs], all_.at[s, rows, cs], place.to_z(s)) for s in range(1, shards)
        ]

    def pass_piece(i, px, py, pc, lo, n, peer):
        _, all_, col, cols, *_ = ch = chunks[i]
        ref = all_.at[others, piece_rows(ch, px, py, pc, lo, n), pl.ds(col, cols)]
        return net.send(ref, ref, peer)

    def plane_one(i):
        rows = chunks[i][5]
        st = state[i]
        for copy in st["z"]:
            copy.wait_recv()
        st["x"] = pass_piece(i, x, y, c, 0, rows, place.to_x)
        st["y"] = pass_piece(i, x, y, c, 0, rows, place.to_y)
        st["core"] = [pass_piece(i, x, y, c, 0, rows, place.to_c)]

    def plane_two(i):
        rows = chunks[i][5]
        st = state[i]
        st["x"].wait_recv()
        st["xy"] = pass_piece(i, 1 - x, y, c, 0, rows // 2, place.to_y)
        st["core"].append(pass_piece(i, 1 - x, y, c, 0, rows, place.to_c))
        st["y"].wait_recv()
        st["yx"] = pass_piece(i, x, 1 - y, c, rows // 2, rows // 2, place.to_x)
        st["core"].append(pass_piece(i, x, 1 - y, c, 0, rows, place.to_c))

    def plane_three(i):
        rows = chunks[i][5]
        st = state[i]
        st["xy"].wait_recv()
        st["core"].append(pass_piece(i, 1 - x, 1 - y, c, 0, rows // 2, place.to_c))
        st["yx"].wait_recv()
        st["core"].append(pass_piece(i, 1 - x, 1 - y, c, rows // 2, rows // 2, place.to_c))

    def arrived(i):
        for copy in state[i]["core"]:
            copy.wait_recv()

    def load(i, dst):
        src, all_, col, cols, *_ = chunks[i]
        moves = []
        for s in range(shards):
            rows = pl.ds(pl.multiple_of(place.behind(s) * shard_rows, shard_rows), shard_rows)
            cs = pl.ds(col, cols)
            from_ = src.at[:, cs] if s == 0 else all_.at[s, :, cs]
            moves.append(net.move(from_, dst.at[rows, cs]))
        return moves

    start_z(0)
    start_z(1)

    net.wait(small_moves)
    for copy in small_sends:
        copy.wait_recv()
    small_moves = [net.move(smv, small_out)]

    def small(row, count=1):
        return jnp.concatenate([smv[s] for s in range(shards)], axis=1)[row : row + count].astype(F32)

    def norm_first(which):
        gain, shift = small(0), small(1)
        for slot in range(slots):
            rows = pl.ds(slot * length, length)
            normed[which, rows, :] = normalized(xv[which, slot].astype(F32), gain, shift).astype(BF)

    net.wait(x_moves)
    norm_first(0)
    plane_one(0)
    start_z(2)
    plane_one(1)
    plane_two(0)
    start_z(3)
    x_send.wait_recv()
    norm_first(1)
    moves_out = [net.move(normed, normed_out)]
    plane_one(2)
    plane_two(1)
    plane_three(0)
    start_z(4)
    arrived(0)
    k_moves = load(0, wq)
    plane_one(3)
    plane_two(2)
    plane_three(1)
    start_z(5)
    arrived(1)
    v_moves = load(1, wq)
    net.wait(k_moves)

    v_bias = small(3)

    def project_kv(which, part):
        lanes = pl.ds((part + 1) * width, width)
        rows = normed[which]
        out = dot(rows, wq[:, lanes])
        if part:
            out = out + v_bias
        out = out.astype(BF)
        at = (y if which == 0 else 1 - y) * 2 + c
        for slot in range(slots):
            kvb[slot, part, at] = out[slot * length : (slot + 1) * length]

    shares = []

    def share(part):
        for which in range(2):
            at = (y if which == 0 else 1 - y) * 2 + c
            ref = kvb.at[:, part, at]
            shares.append(net.send(ref, ref, place.to_c))

    project_kv(0, 0)
    project_kv(1, 0)
    share(0)
    plane_one(4)
    plane_two(3)
    plane_three(2)
    start_z(6)
    arrived(2)
    q_moves = load(2, wq)
    net.wait(v_moves)
    project_kv(0, 1)
    project_kv(1, 1)
    share(1)
    plane_three(3)
    arrived(3)
    o_moves = load(3, wo)
    net.wait(q_moves)
    qv[...] = (dot(normed[0], wq[:, :width]) + small(2)).astype(BF)
    moves_out.append(net.move(qv, q_out))
    plane_one(5)
    plane_two(4)
    start_z(7)
    for copy in shares:
        copy.wait_recv()
    moves_out.append(net.move(kvb, kv_out))

    def attend(slot, lo, hi):
        masks = head_masks(length)

        @pl.loop(lo, hi)
        def _(p):
            lanes = pl.ds(pl.multiple_of(p * PAIR, PAIR), PAIR)
            rows = pl.ds(slot * length, length)
            queries = both_heads(qv[rows, lanes] * BF(HEAD_DIM**-0.5), masks)
            keys = kvb[slot, 0, :, :, lanes].reshape(-1, PAIR)
            values = kvb[slot, 1, :, :, lanes].reshape(-1, PAIR)
            scores = dot(keys, queries, NT)
            top = jnp.max(scores, axis=0, keepdims=True)
            terms = jnp.exp(scores - top)
            total = jnp.sum(terms, axis=0, keepdims=True)
            lsev[slot, p] = top + jnp.log(total)
            out = dot(values, terms.astype(BF), TN) * (1.0 / total)
            out = jnp.concatenate([out[:HEAD_DIM, :length], out[HEAD_DIM:, length:]], axis=0)
            att[rows, lanes] = out.T.astype(BF)

    pairs = width // PAIR
    attend(0, 0, pairs)
    plane_one(6)
    plane_two(5)
    plane_three(4)
    arrived(4)
    up_moves = [load(4, wu)]
    attend(1, 0, pairs)
    moves_out += [net.move(lsev, lse_out), net.move(att, att_out)]
    plane_one(7)
    plane_two(6)
    plane_three(5)
    arrived(5)
    up_moves.append(load(5, wu))

    net.wait(o_moves)
    out_bias, mlp_gain, mlp_shift = small(4), small(5), small(6)
    for slot in range(slots):
        rows = pl.ds(slot * length, length)
        value = xv[0, slot].astype(F32) + dot(att[rows], wo[...]) + out_bias
        res[rows] = value
        nm[rows] = normalized(value, mlp_gain, mlp_shift).astype(BF)
    moves_out += [net.move(res, res_out), net.move(nm, nm_out)]

    up_block = 512

    def up(part):
        @pl.loop(part * (half // up_block), (part + 1) * (half // up_block))
        def _(j):
            lanes = pl.ds(pl.multiple_of(j * up_block, up_block), up_block)
            s, inner = j // (wd_in.shape[0] // up_block), j % (wd_in.shape[0] // up_block)
            first = 8 + inner * (up_block // shard_rows)
            sm = smv[s].astype(F32)
            row = jnp.concatenate([sm[8:9], sm[9:10]], axis=1)
            row2 = jnp.concatenate([sm[10:11], sm[11:12]], axis=1)
            bias = jnp.where(inner == 0, row, row2)
            pre = dot(nm[...], wu[:, lanes]) + bias
            phi = 0.5 + 0.5 * lax.erf(pre * (0.5**0.5))
            density = jnp.exp(pre * pre * -0.5) * 0.3989422804014327
            act[:, lanes] = (pre * phi).astype(BF)
            slope[:, lanes] = (phi + pre * density).astype(BF)

    net.wait(up_moves[0])
    up(0)
    plane_two(7)
    plane_three(6)
    net.wait(up_moves[1])
    up(1)
    moves_out += [net.move(act, act_out), net.move(slope, slope_out)]
    plane_three(7)
    arrived(6)
    arrived(7)
    net.finish()


def forward(shards, x, small, wq, wo, wu, wd):
    slots, length, width = x.shape
    tokens = slots * length
    hidden = wu.shape[1]
    pairs = width // PAIR
    any_ = pl.BlockSpec(memory_space=pl.ANY)
    sd = jax.ShapeDtypeStruct
    outs = (
        sd((shards,) + wq.shape, BF), sd((shards,) + wo.shape, BF), sd((shards,) + wu.shape, BF), sd((shards,) + wd.shape, BF),
        sd((2, tokens, width), BF), sd((tokens, width), BF), sd((slots, 2, 4, length, width), BF),
        sd((slots, pairs, 1, 2 * length), F32), sd((tokens, width), BF), sd((tokens, width), F32),
        sd((tokens, width), BF), sd((tokens, hidden), BF), sd((tokens, hidden), BF), sd((shards,) + small.shape, BF),
    )
    return pl.pallas_call(
        functools.partial(forward_kernel, shards),
        out_shape=outs,
        in_specs=[any_] * 6,
        out_specs=(any_,) * len(outs),
        scratch_shapes=[
            pltpu.VMEM((2, slots, length, width), BF),
            pltpu.VMEM((shards,) + small.shape, BF),
            pltpu.VMEM((2, tokens, width), BF),
            pltpu.VMEM((tokens, width), BF),
            pltpu.VMEM((slots, 2, 4, length, width), BF),
            pltpu.VMEM((slots, pairs, 1, 2 * length), F32),
            pltpu.VMEM((tokens, width), BF),
            pltpu.VMEM((tokens, width), F32),
            pltpu.VMEM((tokens, width), BF),
            pltpu.VMEM((tokens, hidden), BF),
            pltpu.VMEM((tokens, hidden), BF),
            pltpu.VMEM((width, 3 * width), BF),
            pltpu.VMEM((width, width), BF),
            pltpu.VMEM((width, hidden), BF),
            pltpu.SemaphoreType.DMA((N_REMOTE1,)),
            pltpu.SemaphoreType.DMA((N_REMOTE1,)),
            pltpu.SemaphoreType.DMA((N_LOCAL1,)),
        ],
        compiler_params=pltpu.CompilerParams(collective_id=1, has_side_effects=True, vmem_limit_bytes=62 * MIB),
    )(x, small, wq, wo, wu, wd)


N_REMOTE2, N_LOCAL2 = 160, 80
RING_A, RING_B = 3, 5


def norm_back(values, gain, incoming):
    center = values - jnp.mean(values, axis=-1, keepdims=True)
    spread = jnp.mean(center * center, axis=-1, keepdims=True)
    r = lax.rsqrt(spread + EPSILON)
    xhat = center * r
    e = incoming * gain
    back = r * (e - jnp.mean(e, axis=-1, keepdims=True) - xhat * jnp.mean(e * xhat, axis=-1, keepdims=True))
    return back, incoming * xhat


def col_sum(values):
    return jnp.sum(values.astype(F32), axis=0, keepdims=True)


def backward_kernel(
    shards,
    x_in, cot_in, live_in, small_in, wq_in, wo_in, wu_in, wd_in, wq_all, wo_all, wu_all, wd_all,
    normed_in, q_in, kv_in, lse_in, att_in, res_in, nm_in, act_in, slope_in,
    layer_out, input_out, gq_out, go_out, gu_out, gd_out, sg_out,
    wa, wb, ad, nm, att, res, dm, dbr, qv, normed, xv, dn, lsev,
    gq, go, gu, gd, sg, ub, sr,
    gbuf, r0, r1x, r1y, r2x, r2y, r3, r4, fbuf, tbuf,
    send_sems, recv_sems, local_sems, free_sems, act_free,
):
    place = Place(shards)
    net = Copies(send_sems, recv_sems, local_sems)
    x, y, z, c = place.x, place.y, place.z, place.c
    slots, length, width = x_in.shape
    tokens = slots * length
    hidden = wu_in.shape[1]
    shard_rows = wq_in.shape[0]
    down_rows = wd_in.shape[0]
    block = 256
    clip = 4 * length

    def span(slot):
        return pl.ds(slot * length, length)

    cot_moves = [net.move(cot_in.at[slot], dm.at[span(slot)]) for slot in range(slots)]
    act_moves = [net.move(act_in, ad.at[0])]

    def blocks_of(own, gathered, cols, dst_of):
        moves = []
        for s in range(shards):
            src = own.at[:, cols] if s == 0 else gathered.at[s, :, cols]
            moves.append(net.move(src, dst_of(place.behind(s))))
        return moves

    every = pl.ds(0, width)
    wd_moves = blocks_of(
        wd_in, wd_all, every, lambda a: wa.at[pl.ds(pl.multiple_of(a * down_rows, down_rows), down_rows)]
    )
    place.greet()

    net.wait(cot_moves)
    for slot in range(slots):
        dm[span(slot)] = dm[span(slot)] * live_in[slot].astype(BF)
    net.wait(act_moves)

    chunks = []
    flights = []

    def advance_zero(k):
        st, a = chunks[k], k % RING_A
        st["s0"].wait_recv()

        @pl.loop(0, 4)
        def _(i):
            gbuf[a, c, i] = gbuf[a, c, i] + r0[a, i]

        pl.semaphore_signal(free_sems.at[0], inc=1, device_id=place.to_c, device_id_type=MESH)
        b = k % RING_B
        if k >= RING_B:
            pl.semaphore_wait(free_sems.at[1], 1)
            pl.semaphore_wait(free_sems.at[2], 1)
        st["s1y"] = net.send(gbuf.at[a, c, pl.ds(0, 2), 1 - y], r1y.at[b], place.to_y)
        st["s1x"] = net.send(gbuf.at[a, c, 3 - x], r1x.at[b], place.to_x)

    def advance_one(k):
        st, a, b = chunks[k], k % RING_A, k % RING_B
        st["s1y"].wait_recv()
        for i in range(2):
            gbuf[a, c, i, y] = gbuf[a, c, i, y] + r1y[b, i]
        st["s2x"] = net.send(gbuf.at[a, c, 1 - x, y], r2x.at[b], place.to_x)
        st["s1x"].wait_recv()
        for i in range(2):
            gbuf[a, c, 2 + x, i] = gbuf[a, c, 2 + x, i] + r1x[b, i]
        st["s2y"] = net.send(gbuf.at[a, c, 2 + x, 1 - y], r2y.at[b], place.to_y)

    def advance_two(k):
        st, a, b = chunks[k], k % RING_A, k % RING_B
        st["s2x"].wait_recv()
        fbuf[b, :, 0] = gbuf[a, c, x, y] + r2x[b]
        st["s2y"].wait_recv()
        fbuf[b, :, 1] = gbuf[a, c, 2 + x, y] + r2y[b]
        if k >= RING_B:
            for shift in range(1, shards):
                pl.semaphore_wait(free_sems.at[2 + shift], 1)
        st["s3"] = [
            net.send(fbuf.at[b, (z + shift) % shards], r3.at[b, shift - 1], place.to_z(shift))
            for shift in range(1, shards)
        ]
        for name in ("s0", "s1x", "s1y", "s2x", "s2y"):
            st[name].wait_send()

    def advance_three(k):
        st, b = chunks[k], k % RING_B
        for copy in st["s3"]:
            copy.wait_recv()
        total = fbuf[b, z].astype(F32)
        for shift in range(1, shards):
            total = total + r3[b, shift - 1].astype(F32)
        tbuf[b] = total.astype(BF)
        st["s4"] = net.send(tbuf.at[b], r4.at[b], place.to_x)

    def advance_four(k, total_chunks=12):
        st, b = chunks[k], k % RING_B
        st["s4"].wait_recv()
        out, kind, col = st["out"]
        for source, at in ((tbuf, x), (r4, 1 - x)):
            for p in range(2):
                value = source[b, p].astype(F32)
                if kind == "cols":
                    lanes = pl.ds(pl.multiple_of(col + p * 2 * block + at * block, block), block)
                    out[:, lanes] = value
                else:
                    rows = pl.ds(pl.multiple_of((p * 2 + at) * 64, 64), 64)
                    out[rows, pl.ds(col, block)] = value
        for copy in st["s3"]:
            copy.wait_send()
        st["s4"].wait_send()
        if k + RING_B < total_chunks:
            pl.semaphore_signal(free_sems.at[1], inc=1, device_id=place.to_x, device_id_type=MESH)
            pl.semaphore_signal(free_sems.at[2], inc=1, device_id=place.to_y, device_id_type=MESH)
            for shift in range(1, shards):
                peer = {"shard": place.behind(shift)}
                pl.semaphore_signal(free_sems.at[2 + shift], inc=1, device_id=peer, device_id_type=MESH)

    stages = (advance_zero, advance_one, advance_two, advance_three, advance_four)

    def pump():
        for flight in flights:
            if flight[1] < len(stages):
                stages[flight[1]](flight[0])
                flight[1] += 1

    def launch(out, kind, col):
        k = len(chunks)
        a = k % RING_A
        if k >= RING_A:
            pl.semaphore_wait(free_sems.at[0], 1)
        chunks.append({"out": (out, kind, col)})
        chunks[k]["s0"] = net.send(gbuf.at[a, 1 - c], r0.at[a], place.to_c)
        flights.append([k, 0])

    def grad_cols(pairs, out, col):
        a = len(chunks) % RING_A

        @pl.loop(0, 4)
        def _(i):
            total = None
            for left, right in pairs:
                term = dot(left[...], right(i), TN)
                total = term if total is None else total + term
            value = total.astype(BF).reshape(shards, 2, 2, 64, block)
            for cc in range(2):
                for yy in range(2):
                    gbuf[a, cc, i, yy] = value[:, yy, cc]

        launch(out, "cols", col)

    def grad_down(j):
        a = len(chunks) % RING_A
        right = dm[:, pl.ds(j * block, block)]

        @pl.loop(0, shards)
        def _(i):
            left = ad[0, :, pl.ds(pl.multiple_of(i * down_rows, down_rows), down_rows)]
            value = dot(left, right, TN).astype(BF).reshape(2, 2, 4, 64, block)
            for cc in range(2):
                for yy in range(2):
                    gbuf[a, cc, :, yy, i] = value[yy, cc]

        launch(gd, "rows", j * block)

    def lanes_at(start, n=block):
        return pl.ds(pl.multiple_of(start, block), n)

    grad_down(0)
    slope_moves = [net.move(slope_in, ad.at[1])]
    nm_moves = [net.move(nm_in, nm), net.move(res_in, res)]
    half_rows = width // 2
    per = half_rows // shard_rows
    wu_moves = blocks_of(
        wu_in, wu_all, pl.ds(0, hidden),
        lambda a: wb.at[a // per, pl.ds(pl.multiple_of((a % per) * shard_rows, shard_rows), shard_rows)],
    )
    late_moves = [
        net.move(att_in, att), net.move(q_in, qv), net.move(normed_in, normed), net.move(x_in, xv),
        net.move(lse_in, lsev),
    ]
    pump()
    grad_down(1)
    net.wait(wd_moves)
    net.wait(slope_moves)
    wide = 512

    def d_pre(lo, hi):
        @pl.loop(lo, hi)
        def _(j):
            lanes = pl.ds(pl.multiple_of(j * wide, wide), wide)
            value = dot(dm[...], wa[lanes, :], NT) * ad[1, :, lanes].astype(F32)
            value = value.astype(BF)
            ad[1, :, lanes] = value
            ub[j] = col_sum(value)

    n_wide = hidden // wide
    d_pre(0, n_wide // 2)
    pump()
    grad_down(2)
    d_pre(n_wide // 2, n_wide)
    pump()
    grad_down(3)

    def full(row):
        return jnp.concatenate([small_in[s, row : row + 1] for s in range(shards)], axis=1).astype(F32)

    net.wait(nm_moves)
    down_bias = full(7)
    for slot in range(slots):
        value = res[span(slot)] + dot(ad[0, span(slot)], wa[...]) + down_bias
        value = (value * live_in[slot]).astype(BF)
        dbr[span(slot)] = value
    layer_moves = [net.move(dbr.at[span(slot)], layer_out.at[slot]) for slot in range(slots)]
    sg[7:8] = col_sum(dm[...])
    pump()

    kv_moves = [net.move(kv_in, wa)]
    wo_moves = []
    for s in range(shards):
        at = place.behind(s)
        src = wo_in if s == 0 else wo_all.at[s]
        rows = pl.ds(pl.multiple_of((at % per) * shard_rows, shard_rows), shard_rows)
        wo_moves.append(net.move(src, ad.at[0, rows, pl.ds(pl.multiple_of((at // per) * width, width), width)]))

    def up_pairs(j):
        return [(nm, lambda i: ad[1, :, lanes_at(j * width + i * block)])]

    grad_cols(up_pairs(0), gu, 0)
    net.wait(wu_moves)
    net.wait(layer_moves)
    gain = full(5)
    gain_terms, shift_terms = None, None
    for slot in range(slots):
        rows = span(slot)
        incoming = jnp.concatenate([dot(ad[1, rows], wb[i], NT) for i in range(2)], axis=1)
        back, terms = norm_back(res[rows], gain, incoming)
        back = back + dm[rows].astype(F32)
        res[rows] = back
        dbr[rows] = back.astype(BF)
        terms, shifts = col_sum(terms), col_sum(incoming)
        gain_terms = terms if slot == 0 else gain_terms + terms
        shift_terms = shifts if slot == 0 else shift_terms + shifts
    sg[5:6] = gain_terms
    sg[6:7] = shift_terms
    sg[4:5] = col_sum(dbr[...])
    pump()
    grad_cols(up_pairs(1), gu, width)
    net.wait(wo_moves)
    for i in range(2):
        dm[:, i * half_rows : (i + 1) * half_rows] = dot(
            dbr[...], ad[0, :, i * width : (i + 1) * width], NT
        ).astype(BF)
    pl.semaphore_signal(act_free, inc=1, device_id=place.to_c, device_id_type=MESH)
    pump()
    grad_cols(up_pairs(2), gu, 2 * width)
    net.wait(late_moves)
    net.wait(kv_moves)
    scale = HEAD_DIM**-0.5

    def attend(slot, lo, hi):
        masks = head_masks(length)

        @pl.loop(lo, hi)
        def _(p):
            lanes = pl.ds(pl.multiple_of(p * PAIR, PAIR), PAIR)
            rows = span(slot)
            keys = wa[pl.ds(slot * 2 * clip, clip), lanes]
            values = wa[pl.ds((slot * 2 + 1) * clip, clip), lanes]
            queries = qv[rows, lanes] * BF(scale)
            d_out = dm[rows, lanes]
            along = (att[rows, lanes].astype(F32) * d_out.astype(F32)).T
            logs = lsev[slot, p]
            d_k, d_v, d_q = None, None, []
            for h in range(2):
                half = slice(h * HEAD_DIM, (h + 1) * HEAD_DIM)
                q_h, d_h = queries * masks[h], d_out * masks[h]
                probs = jnp.exp(dot(keys, q_h, NT) - logs[:, h * length : (h + 1) * length])
                mean = jnp.sum(along[half], axis=0, keepdims=True)
                d_scores = (probs * (dot(values, d_h, NT) - mean)).astype(BF)
                term_v = dot(probs.astype(BF), d_h)
                term_k = dot(d_scores, q_h)
                d_v = term_v if h == 0 else d_v + term_v
                d_k = term_k if h == 0 else d_k + term_k
                d_q.append(dot(keys, d_scores, TN)[half])
            qv[rows, lanes] = (jnp.concatenate(d_q, axis=0).T * scale).astype(BF)
            for part, value in ((0, d_k), (1, d_v)):
                value = value.astype(BF)
                for yy in range(2):
                    to = pl.ds(pl.multiple_of((yy * 2 + part) * width + p * PAIR, PAIR), PAIR)
                    for cc in range(2):
                        at = (yy * 2 + cc) * length
                        wb[cc, rows, to] = value[at : at + length]

    pairs = width // PAIR

    def share(slot):
        if slot == 0:
            pl.semaphore_wait(act_free, 1)
        return net.send(wb.at[1 - c, span(slot)], ad.at[0, span(slot)], place.to_c)

    attend(0, 0, pairs // 2)
    pump()
    grad_cols(up_pairs(3), gu, 3 * width)
    attend(0, pairs // 2, pairs)
    shares = [share(0)]
    pump()
    grad_cols([(att, lambda i: dbr[:, lanes_at(i * block)])], go, 0)
    attend(1, 0, pairs // 2)
    pump()
    attend(1, pairs // 2, pairs)
    shares.append(share(1))
    wq_moves = []
    for part in (1, 2, 0):
        wq_moves.append(
            blocks_of(
                wq_in, wq_all, pl.ds(part * width, width),
                lambda a: wa.at[pl.ds(pl.multiple_of(part * width + a * shard_rows, shard_rows), shard_rows)],
            )
        )
    pump()
    grad_cols([(normed.at[0], lambda i: qv[:, lanes_at(i * block)])], gq, 0)
    sg[2:3] = col_sum(qv[...])

    for slot in range(slots):
        shares[slot].wait_recv()

        @pl.loop(0, 2 * 2)
        def _(i):
            lanes = pl.ds(pl.multiple_of(i * width, width), width)
            wb[c, span(slot), lanes] = wb[c, span(slot), lanes] + ad[0, span(slot), lanes]

    def d_part(part, which, lanes_from=0, n=None):
        side = y if which == 0 else 1 - y
        n = width if n is None else n
        return wb[c, :, lanes_at((side * 2 + part) * width + lanes_from, n)]

    net.wait(wq_moves[0])
    net.wait(wq_moves[1])
    back = dot(d_part(0, 1), wa[pl.ds(width, width)], NT) + dot(d_part(1, 1), wa[pl.ds(2 * width, width)], NT)
    dm[...] = back.astype(BF)
    back_sends = [net.send(dm.at[span(slot)], dn.at[slot], place.to_y) for slot in range(slots)]
    pump()

    def kv_pairs(part):
        return [
            (normed.at[which], lambda i, which=which: d_part(part, which, i * block, block)) for which in range(2)
        ]

    grad_cols(kv_pairs(0), gq, width)
    sg[3:4] = col_sum(d_part(1, 0)) + col_sum(d_part(1, 1))
    pump()
    grad_cols(kv_pairs(1), gq, 2 * width)
    pump()
    net.wait(wq_moves[2])
    gain = full(0)
    for slot in range(slots):
        rows = span(slot)
        incoming = dot(qv[rows], wa[pl.ds(0, width)], NT)
        side = [wb[c, rows, lanes_at((y * 2 + part) * width, width)] for part in range(2)]
        incoming = incoming + dot(side[0], wa[pl.ds(width, width)], NT)
        incoming = incoming + dot(side[1], wa[pl.ds(2 * width, width)], NT)
        back_sends[slot].wait_recv()
        incoming = incoming + dn[slot].astype(F32)
        back, terms = norm_back(xv[slot].astype(F32), gain, incoming)
        xv[slot] = (res[rows] + back).astype(BF)
        terms, shifts = col_sum(terms), col_sum(incoming)
        gain_terms = terms if slot == 0 else gain_terms + terms
        shift_terms = shifts if slot == 0 else shift_terms + shifts
        if slot == 0:
            pump()
    out_moves = [net.move(xv, input_out)]
    sg[0:1] = gain_terms
    sg[1:2] = shift_terms
    per_row = width // wide
    for j in range(n_wide):
        sg[8 + j // per_row : 9 + j // per_row, (j % per_row) * wide : (j % per_row + 1) * wide] = ub[j]
    sg[12:16] = jnp.zeros((4, width), F32)

    sums = [net.send(sg, sr.at[0], place.to_c)]
    pump()
    sums[0].wait_recv()
    sr[4] = sg[...] + sr[0]
    sums.append(net.send(sr.at[4], sr.at[1], place.to_y))
    pump()
    sums[1].wait_recv()
    sr[5] = sr[4] + sr[1]
    sums += [net.send(sr.at[5], sr.at[7 + shift], place.to_z(shift)) for shift in range(1, shards)]
    pump()
    for copy in sums[2:]:
        copy.wait_recv()
    total = sr[5]
    for shift in range(1, shards):
        total = total + sr[7 + shift]
    sr[6] = total
    sums.append(net.send(sr.at[6], sr.at[2], place.to_x))
    pump()
    sums[-1].wait_recv()
    sr[3] = sr[6] + sr[2]
    out_moves.append(net.move(sr.at[3], sg_out))
    while any(flight[1] < len(stages) for flight in flights):
        pump()
    for _ in range(RING_A):
        pl.semaphore_wait(free_sems.at[0], 1)
    out_moves += [net.move(a, b) for a, b in ((gq, gq_out), (go, go_out), (gu, gu_out), (gd, gd_out))]
    finish(net, chunks)


def finish(net, chunks):
    done = set()
    for st in chunks:
        for name, value in st.items():
            if name.startswith("s"):
                done.update(id(copy) for copy in (value if isinstance(value, list) else [value]))
    for copy in net.remote:
        if id(copy) not in done:
            copy.wait_send()
    net.wait(net.local)


def backward(shards, x, cot, live, small, weights, gathered, kept):
    slots, length, width = x.shape
    tokens = slots * length
    hidden = weights[2].shape[1]
    down_rows = weights[3].shape[0]
    pairs = width // PAIR
    owned = weights[0].shape[0] // 4
    any_ = pl.BlockSpec(memory_space=pl.ANY)
    vmem = pl.BlockSpec(memory_space=pltpu.VMEM)
    sd = jax.ShapeDtypeStruct
    outs = (
        sd((slots, length, width), BF), sd((slots, length, width), BF), sd((owned, 3 * width), F32), sd((owned, width), F32),
        sd((owned, hidden), F32), sd((down_rows // 4, width), F32), sd((16, width), F32),
    )
    tile = (64, 256)
    return pl.pallas_call(
        functools.partial(backward_kernel, shards),
        out_shape=outs,
        in_specs=[any_] * 2 + [vmem] * 2 + [any_] * 17,
        out_specs=(any_,) * len(outs),
        scratch_shapes=[
            pltpu.VMEM((hidden, width), BF),
            pltpu.VMEM((2, width // 2, hidden), BF),
            pltpu.VMEM((2, tokens, hidden), BF),
            pltpu.VMEM((tokens, width), BF),
            pltpu.VMEM((tokens, width), BF),
            pltpu.VMEM((tokens, width), F32),
            pltpu.VMEM((tokens, width), BF),
            pltpu.VMEM((tokens, width), BF),
            pltpu.VMEM((tokens, width), BF),
            pltpu.VMEM((2, tokens, width), BF),
            pltpu.VMEM((slots, length, width), BF),
            pltpu.VMEM((slots, length, width), BF),
            pltpu.VMEM((slots, pairs, 1, 2 * length), F32),
            pltpu.VMEM((owned, 3 * width), F32),
            pltpu.VMEM((owned, width), F32),
            pltpu.VMEM((owned, hidden), F32),
            pltpu.VMEM((down_rows // 4, width), F32),
            pltpu.VMEM((16, width), F32),
            pltpu.VMEM((hidden // 512, 1, 512), F32),
            pltpu.VMEM((7 + shards, 16, width), F32),
            pltpu.VMEM((RING_A, 2, 4, 2, shards) + tile, BF),
            pltpu.VMEM((RING_A, 4, 2, shards) + tile, BF),
            pltpu.VMEM((RING_B, 2, shards) + tile, BF),
            pltpu.VMEM((RING_B, 2, shards) + tile, BF),
            pltpu.VMEM((RING_B, shards) + tile, BF),
            pltpu.VMEM((RING_B, shards) + tile, BF),
            pltpu.VMEM((RING_B, shards - 1, 2) + tile, BF),
            pltpu.VMEM((RING_B, 2) + tile, BF),
            pltpu.VMEM((RING_B, shards, 2) + tile, BF),
            pltpu.VMEM((RING_B, 2) + tile, BF),
            pltpu.SemaphoreType.DMA((N_REMOTE2,)),
            pltpu.SemaphoreType.DMA((N_REMOTE2,)),
            pltpu.SemaphoreType.DMA((N_LOCAL2,)),
            pltpu.SemaphoreType.REGULAR((2 + shards,)),
            pltpu.SemaphoreType.REGULAR,
        ],
        compiler_params=pltpu.CompilerParams(collective_id=2, has_side_effects=True, vmem_limit_bytes=63 * MIB),
    )(x, cot, live, small, *weights, *gathered, *kept)


def local(
    activations, cotangent, clip_loads, attn_gain, attn_shift, w_qkv, q_bias, v_bias, w_out, out_bias,
    mlp_gain, mlp_shift, w_up, up_bias, w_down, down_bias,
):
    shards, seats = lax.axis_size("shard"), lax.axis_size("seq")
    x, cot = activations[0], cotangent[0]
    slots, length, width = x.shape
    rows = w_qkv.shape[0]
    vectors = [attn_gain, attn_shift, q_bias, v_bias, out_bias, mlp_gain, mlp_shift, down_bias]
    small = jnp.concatenate([jnp.stack(vectors), up_bias.reshape(-1, rows)], axis=0)
    small = jnp.pad(small, ((0, 16 - small.shape[0]), (0, 0)))
    weights = (w_qkv, w_out, w_up, w_down)
    *gathered, normed, q, kv, lse, att, res, nm, act, slope, small = forward(shards, x, small, *weights)
    live = (jnp.arange(slots) < clip_loads[0]).astype(F32)
    live = jnp.broadcast_to(live[:, None, None], (slots, 1, width))
    kept = (normed, q, kv.reshape(-1, width), lse, att, res, nm, act, slope)
    layer_out, input_grad, gq, go, gu, gd, sums = backward(shards, x, cot, live, small, weights, gathered, kept)
    pods = lax.axis_size("replica")
    if pods > 2:
        ends = [[p for p in range(pods) if p % 2 == side] for side in range(2)]
        gq, go, gu, gd = (
            lax.psum(g.astype(BF), "replica", axis_index_groups=ends).astype(F32) for g in (gq, go, gu, gd)
        )
        sums = lax.psum(sums, "replica", axis_index_groups=ends)
    at = lax.axis_index("shard") * seats + lax.axis_index("seq")
    n = width // (shards * seats)
    vec = lax.dynamic_slice_in_dim(sums[:8], at * n, n, axis=1)
    n_up = n * 4
    up = lax.dynamic_slice_in_dim(sums[8:12].reshape(-1), at * n_up, n_up)
    return (
        layer_out[None], input_grad[None], vec[0], vec[1], gq, vec[2], vec[3], go, vec[4], vec[5], vec[6], gu, up, gd, vec[7],
    )


def solution(mesh):
    rows = P("shard")
    full = P("shard", None)
    clips = P(("replica", "shard"), None, "seq", None)
    vec = P(("shard", "seq"))
    mat = P(("shard", "seq"), None)
    return jax.shard_map(
        local,
        mesh=mesh,
        in_specs=(
            clips, clips, P(("replica", "shard")), rows, rows, full, rows, rows, full, rows, rows, rows, full, rows, full, rows,
        ),
        out_specs=(clips, clips, vec, vec, mat, vec, vec, mat, vec, vec, vec, mat, vec, mat, vec),
        check_vma=False,
    )
```

```python
import functools
import jax
import jax.numpy as jnp
from jax import lax
from jax.experimental import pallas as pl
from jax.experimental.pallas import tpu as pltpu
from jax.sharding import PartitionSpec as P

MESH = pl.DeviceIdType.MESH
BF = jnp.bfloat16
F32 = jnp.float32
HEAD_DIM = 64
PAIR = 2 * HEAD_DIM
EPSILON = 1e-06
NN = (((1,), (0,)), ((), ()))
NT = (((1,), (1,)), ((), ()))
TN = (((0,), (0,)), ((), ()))
MIB = 2**20


def dot(a, b, dims=NN):
    return lax.dot_general(a, b, dims, preferred_element_type=F32)


class Place:
    def __init__(self, shards):
        self.shards = shards
        r, self.z, q = (lax.axis_index(a) for a in ("replica", "shard", "seq"))
        self.x, self.y, self.c = r % 2, q // 2, q % 2
        self.q = q
        self.to_x = {"replica": r + 1 - 2 * self.x}
        self.to_y = {"seq": q + 2 - 4 * self.y}
        self.to_c = {"seq": q + 1 - 2 * self.c}

    def to_z(self, shift):
        return {"shard": (self.z + shift) % self.shards}

    def behind(self, shift):
        return (self.z + self.shards - shift) % self.shards

    def greet(self):
        barrier = pltpu.get_barrier_semaphore()
        peers = [self.to_x, self.to_y, self.to_c]
        peers += [self.to_z(shift) for shift in range(1, self.shards)]
        for peer in peers:
            pl.semaphore_signal(barrier, inc=1, device_id=peer, device_id_type=MESH)
        pl.semaphore_wait(barrier, len(peers))


class Copies:
    def __init__(self, send_sems, recv_sems, local_sems):
        self.send_sems, self.recv_sems, self.local_sems = send_sems, recv_sems, local_sems
        self.remote, self.local = [], []

    def send(self, src, dst, peer):
        at = len(self.remote)
        copy = pltpu.make_async_remote_copy(
            src_ref=src, dst_ref=dst, send_sem=self.send_sems.at[at], recv_sem=self.recv_sems.at[at],
            device_id=peer, device_id_type=MESH,
        )
        copy.start()
        self.remote.append(copy)
        return copy

    def move(self, src, dst):
        at = len(self.local)
        copy = pltpu.make_async_copy(src, dst, self.local_sems.at[at])
        copy.start()
        self.local.append([copy, False])
        return self.local[-1]

    def wait(self, moves):
        for entry in moves:
            if not entry[1]:
                entry[0].wait()
                entry[1] = True

    def finish(self):
        for copy in self.remote:
            copy.wait_send()
        self.wait(self.local)


def normalized(values, gain, shift):
    center = values - jnp.mean(values, axis=-1, keepdims=True)
    spread = jnp.mean(center * center, axis=-1, keepdims=True)
    return center * lax.rsqrt(spread + EPSILON) * gain + shift


def head_masks(rows):
    lane = lax.broadcasted_iota(jnp.int32, (rows, PAIR), 1)
    first = (lane < HEAD_DIM).astype(F32).astype(BF)
    return first, (lane >= HEAD_DIM).astype(F32).astype(BF)


def both_heads(values, masks):
    return jnp.concatenate([values * masks[0], values * masks[1]], axis=0)


N_REMOTE1, N_LOCAL1 = 176, 80
AHEAD = 2
IN_HALVES = (3, 5, 7)


def forward_kernel(
    shards,
    x_in, small_in, wq_in, wo_in, wu_in, wd_in,
    wq_all, wo_all, wu_all, wd_all,
    normed_out, q_out, kv_out, lse_out, att_out, res_out, nm_out, act_out, slope_out, small_out,
    xv, smv, normed, qv, kvb, lsev, att, res, nm, act, slope, wq, wo, wu,
    send_sems, recv_sems, local_sems,
):
    place = Place(shards)
    net = Copies(send_sems, recv_sems, local_sems)
    x, y, z, c = place.x, place.y, place.z, place.c
    slots, length, width = x_in.shape
    tokens = slots * length
    hidden = wu_in.shape[1]
    shard_rows = wq_in.shape[0]
    place.greet()

    small_moves = [net.move(small_in, smv.at[z])]
    small_sends = [net.send(small_in, smv.at[z], place.to_z(s)) for s in range(1, shards)]
    x_moves = [net.move(x_in, xv.at[0])]
    x_sends = [net.send(x_in.at[0], xv.at[1, 0], place.to_y)]

    chunks = [(wq_in, wq_all, part * width, 0, False) for part in (1, 2, 0)]
    chunks.append((wo_in, wo_all, 0, 0, False))
    chunks += [(wu_in, wu_all, j * width, 0, False) for j in range(hidden // width)]
    chunks += [(wd_in, wd_all, 0, j * shard_rows, True) for j in range(wd_in.shape[0] // shard_rows)]
    chunks = [chunk[:4] + (chunk[4] or i in IN_HALVES,) for i, chunk in enumerate(chunks)]
    state = [dict() for _ in chunks]
    others = pl.ds(1, shards - 1)
    eighth, quarter = shard_rows // 8, shard_rows // 4
    near, far = {"shard": z + 1 - 2 * (z % 2)}, {"shard": z + 2 - 4 * (z // 2)}
    at_near = 1 + 2 * (z % 2)

    def region(i, px, py, pc, side=None):
        _, _, col, row, halves = chunks[i]
        if halves:
            h = (px + py) % 2
            at, n = {None: (0, 2 * quarter), "x": (0, quarter), "y": (quarter, quarter)}[side]
            rows = pl.ds(pl.multiple_of(row + pc * 2 * quarter + at, 16), n)
            return rows, pl.ds(pl.multiple_of(col + h * (width // 2), 128), width // 2)
        cut = width // 4
        at, n = {None: (0, width), "y": (0, cut), "x": (cut, width - cut)}[side]
        rows = pl.ds(pl.multiple_of(row + ((px * 2 + py) * 2 + pc) * eighth, 16), eighth)
        return rows, pl.ds(col + at, n)

    def start_z(i):
        src, all_, *_ = chunks[i]
        at = region(i, x, y, c)
        state[i]["far"] = net.send(src.at[at], all_.at[(2,) + at], far)
        state[i]["near"] = net.send(src.at[at], all_.at[(at_near,) + at], near)

    def relay(i):
        all_ = chunks[i][1]
        at = region(i, x, y, c)
        state[i]["far"].wait_recv()
        state[i]["relay"] = net.send(all_.at[(2,) + at], all_.at[(4 - at_near,) + at], near)
        if i + AHEAD < len(chunks):
            start_z(i + AHEAD)

    def pass_piece(i, px, py, pc, peer, side=None):
        ref = chunks[i][1].at[(others,) + region(i, px, py, pc, side)]
        return net.send(ref, ref, peer)

    def plane_one(i):
        st = state[i]
        st["near"].wait_recv()
        st["relay"].wait_recv()
        halves = chunks[i][4]
        st["x"] = pass_piece(i, x, y, c, place.to_x, "x" if halves else None)
        st["y"] = pass_piece(i, x, y, c, place.to_y, "y" if halves else None)
        st["core"] = [pass_piece(i, x, y, c, place.to_c)]

    def plane_two(i):
        st = state[i]
        halves = chunks[i][4]
        st["y"].wait_recv()
        if not halves:
            st["yx"] = pass_piece(i, x, 1 - y, c, place.to_x, "x")
        st["core"].append(pass_piece(i, x, 1 - y, c, place.to_c, "y" if halves else None))
        st["x"].wait_recv()
        if not halves:
            st["xy"] = pass_piece(i, 1 - x, y, c, place.to_y, "y")
        st["core"].append(pass_piece(i, 1 - x, y, c, place.to_c, "x" if halves else None))

    def plane_three(i):
        st = state[i]
        if chunks[i][4]:
            return
        for name, side in (("yx", "x"), ("xy", "y")):
            st[name].wait_recv()
            st["core"].append(pass_piece(i, 1 - x, 1 - y, c, place.to_c, side))

    def arrived(i):
        for copy in state[i]["core"]:
            copy.wait_recv()

    def load(i, dst):
        src, all_, col, *_ = chunks[i]
        moves = []
        for s in range(shards):
            rows = pl.ds(pl.multiple_of(place.behind(s) * shard_rows, shard_rows), shard_rows)
            cs = pl.ds(col, width)
            from_ = src.at[:, cs] if s == 0 else all_.at[s, :, cs]
            moves.append(net.move(from_, dst.at[rows, cs]))
        return moves

    for i in range(AHEAD):
        start_z(i)

    net.wait(small_moves)
    for copy in small_sends:
        copy.wait_recv()
    small_moves = [net.move(smv, small_out)]

    def small(row, count=1):
        return jnp.concatenate([smv[s] for s in range(shards)], axis=1)[row : row + count].astype(F32)

    def norm_first(which, slot):
        rows = pl.ds(slot * length, length)
        normed[which, rows, :] = normalized(xv[which, slot].astype(F32), small(0), small(1)).astype(BF)

    loads = {}

    def step(i):
        if i + 4 < len(chunks):
            relay(i + 4)
        if i + 2 < len(chunks):
            plane_one(i + 2)
        if 0 <= i + 1 < len(chunks):
            plane_two(i + 1)
        if 0 <= i < len(chunks):
            plane_three(i)
        if 0 <= i - 1:
            arrived(i - 1)
            if i - 1 < len(targets):
                loads[i - 1] = load(i - 1, targets[i - 1])

    targets = [wq] * 3 + [wo] + [wu] * (hidden // width)

    net.wait(x_moves)
    norm_first(0, 0)
    relay(0)
    relay(1)
    step(-2)
    x_sends.append(net.send(x_in.at[1], xv.at[1, 1], place.to_y))
    norm_first(0, 1)
    step(-1)
    x_sends[0].wait_recv()
    norm_first(1, 0)
    step(0)
    x_sends[1].wait_recv()
    norm_first(1, 1)
    moves_out = [net.move(normed, normed_out)]
    step(1)
    v_bias = small(3)

    def project_kv(which, part):
        lanes = pl.ds((part + 1) * width, width)
        rows = normed[which]
        out = dot(rows, wq[:, lanes])
        if part:
            out = out + v_bias
        out = out.astype(BF)
        at = (y if which == 0 else 1 - y) * 2 + c
        for slot in range(slots):
            kvb[slot, part, at] = out[slot * length : (slot + 1) * length]

    shares = []

    def share(part):
        for which in range(2):
            at = (y if which == 0 else 1 - y) * 2 + c
            ref = kvb.at[:, part, at]
            shares.append(net.send(ref, ref, place.to_c))

    net.wait(loads[0])
    project_kv(0, 0)
    project_kv(1, 0)
    share(0)
    step(2)
    net.wait(loads[1])
    project_kv(0, 1)
    project_kv(1, 1)
    share(1)
    step(3)
    net.wait(loads[2])
    qv[...] = (dot(normed[0], wq[:, :width]) + small(2)).astype(BF)
    moves_out.append(net.move(qv, q_out))
    for copy in shares:
        copy.wait_recv()
    moves_out.append(net.move(kvb, kv_out))

    def attend(slot, lo, hi):
        masks = head_masks(length)

        @pl.loop(lo, hi)
        def _(p):
            lanes = pl.ds(pl.multiple_of(p * PAIR, PAIR), PAIR)
            rows = pl.ds(slot * length, length)
            queries = both_heads(qv[rows, lanes] * BF(HEAD_DIM**-0.5), masks)
            keys = kvb[slot, 0, :, :, lanes].reshape(-1, PAIR)
            values = kvb[slot, 1, :, :, lanes].reshape(-1, PAIR)
            scores = dot(keys, queries, NT)
            top = jnp.max(scores, axis=0, keepdims=True)
            terms = jnp.exp(scores - top)
            total = jnp.sum(terms, axis=0, keepdims=True)
            lsev[slot, p] = top + jnp.log(total)
            out = dot(values, terms.astype(BF), TN) * (1.0 / total)
            out = jnp.concatenate([out[:HEAD_DIM, :length], out[HEAD_DIM:, length:]], axis=0)
            att[rows, lanes] = out.T.astype(BF)

    pairs = width // PAIR
    attend(0, 0, pairs // 2)
    step(4)
    attend(0, pairs // 2, pairs)
    step(5)
    attend(1, 0, pairs // 2)
    step(6)
    attend(1, pairs // 2, pairs)
    moves_out += [net.move(lsev, lse_out), net.move(att, att_out)]
    step(7)
    net.wait(loads[3])
    out_bias, mlp_gain, mlp_shift = small(4), small(5), small(6)
    for slot in range(slots):
        rows = pl.ds(slot * length, length)
        value = xv[0, slot].astype(F32) + dot(att[rows], wo[...]) + out_bias
        res[rows] = value
        nm[rows] = normalized(value, mlp_gain, mlp_shift).astype(BF)
    moves_out += [net.move(res, res_out), net.move(nm, nm_out)]

    up_block = 512

    def up(part):
        @pl.loop(part * (width // up_block), (part + 1) * (width // up_block))
        def _(j):
            lanes = pl.ds(pl.multiple_of(j * up_block, up_block), up_block)
            s, inner = j // (wd_in.shape[0] // up_block), j % (wd_in.shape[0] // up_block)
            first = 8 + inner * (up_block // shard_rows)
            sm = smv[s].astype(F32)
            row = jnp.concatenate([sm[8:9], sm[9:10]], axis=1)
            row2 = jnp.concatenate([sm[10:11], sm[11:12]], axis=1)
            bias = jnp.where(inner == 0, row, row2)
            pre = dot(nm[...], wu[:, lanes]) + bias
            phi = 0.5 + 0.5 * lax.erf(pre * (0.5**0.5))
            density = jnp.exp(pre * pre * -0.5) * 0.3989422804014327
            act[:, lanes] = (pre * phi).astype(BF)
            slope[:, lanes] = (phi + pre * density).astype(BF)

    for j in range(hidden // width):
        if 4 + j not in loads:
            step(5 + j)
        net.wait(loads[4 + j])
        up(j)
        if j % 2:
            lanes = pl.ds((j - 1) * width, 2 * width)
            moves_out += [net.move(act.at[:, lanes], act_out.at[:, lanes]), net.move(slope.at[:, lanes], slope_out.at[:, lanes])]
    for i in range(9, len(chunks) + 1):
        step(i)
    net.finish()


def forward(shards, x, small, wq, wo, wu, wd):
    slots, length, width = x.shape
    tokens = slots * length
    hidden = wu.shape[1]
    pairs = width // PAIR
    any_ = pl.BlockSpec(memory_space=pl.ANY)
    sd = jax.ShapeDtypeStruct
    outs = (
        sd((shards,) + wq.shape, BF), sd((shards,) + wo.shape, BF), sd((shards,) + wu.shape, BF), sd((shards,) + wd.shape, BF),
        sd((2, tokens, width), BF), sd((tokens, width), BF), sd((slots, 2, 4, length, width), BF),
        sd((slots, pairs, 1, 2 * length), F32), sd((tokens, width), BF), sd((tokens, width), F32),
        sd((tokens, width), BF), sd((tokens, hidden), BF), sd((tokens, hidden), BF), sd((shards,) + small.shape, BF),
    )
    return pl.pallas_call(
        functools.partial(forward_kernel, shards),
        out_shape=outs,
        in_specs=[any_] * 6,
        out_specs=(any_,) * len(outs),
        scratch_shapes=[
            pltpu.VMEM((2, slots, length, width), BF),
            pltpu.VMEM((shards,) + small.shape, BF),
            pltpu.VMEM((2, tokens, width), BF),
            pltpu.VMEM((tokens, width), BF),
            pltpu.VMEM((slots, 2, 4, length, width), BF),
            pltpu.VMEM((slots, pairs, 1, 2 * length), F32),
            pltpu.VMEM((tokens, width), BF),
            pltpu.VMEM((tokens, width), F32),
            pltpu.VMEM((tokens, width), BF),
            pltpu.VMEM((tokens, hidden), BF),
            pltpu.VMEM((tokens, hidden), BF),
            pltpu.VMEM((width, 3 * width), BF),
            pltpu.VMEM((width, width), BF),
            pltpu.VMEM((width, hidden), BF),
            pltpu.SemaphoreType.DMA((N_REMOTE1,)),
            pltpu.SemaphoreType.DMA((N_REMOTE1,)),
            pltpu.SemaphoreType.DMA((N_LOCAL1,)),
        ],
        compiler_params=pltpu.CompilerParams(collective_id=1, has_side_effects=True, vmem_limit_bytes=62 * MIB),
    )(x, small, wq, wo, wu, wd)


N_REMOTE2, N_LOCAL2 = 160, 80
RING_A, RING_B, N_CHUNKS = 3, 3, 12
X_ONLY = (8, 9)


def norm_back(values, gain, incoming):
    center = values - jnp.mean(values, axis=-1, keepdims=True)
    spread = jnp.mean(center * center, axis=-1, keepdims=True)
    r = lax.rsqrt(spread + EPSILON)
    xhat = center * r
    e = incoming * gain
    back = r * (e - jnp.mean(e, axis=-1, keepdims=True) - xhat * jnp.mean(e * xhat, axis=-1, keepdims=True))
    return back, incoming * xhat


def col_sum(values):
    return jnp.sum(values.astype(F32), axis=0, keepdims=True)


def backward_kernel(
    shards,
    x_in, cot_in, live_in, small_in, wq_in, wo_in, wu_in, wd_in, wq_all, wo_all, wu_all, wd_all,
    normed_in, q_in, kv_in, lse_in, att_in, res_in, nm_in, act_in, slope_in,
    layer_out, input_out, gq_out, go_out, gu_out, gd_out, sg_out,
    wa, wb, ad, nm, att, res, dm, dbr, qv, normed, xv, dn, lsev,
    gq, go, gu, gd, sg, ub, sr,
    gbuf, r0, r1, ra, rb, r2, r4, fbuf, gb, tsum, tbuf,
    send_sems, recv_sems, local_sems, free_sems, act_free,
):
    place = Place(shards)
    net = Copies(send_sems, recv_sems, local_sems)
    x, y, z, c = place.x, place.y, place.z, place.c
    slots, length, width = x_in.shape
    tokens = slots * length
    hidden = wu_in.shape[1]
    shard_rows = wq_in.shape[0]
    down_rows = wd_in.shape[0]
    block = 256
    clip = 4 * length

    def span(slot):
        return pl.ds(slot * length, length)

    cot_moves = [net.move(cot_in.at[slot], dm.at[span(slot)]) for slot in range(slots)]
    act_moves = [net.move(act_in, ad.at[0])]

    def blocks_of(own, gathered, cols, dst_of):
        moves = []
        for s in range(shards):
            src = own.at[:, cols] if s == 0 else gathered.at[s, :, cols]
            moves.append(net.move(src, dst_of(place.behind(s))))
        return moves

    every = pl.ds(0, width)
    wd_moves = blocks_of(
        wd_in, wd_all, every, lambda a: wa.at[pl.ds(pl.multiple_of(a * down_rows, down_rows), down_rows)]
    )
    place.greet()

    net.wait(cot_moves)
    for slot in range(slots):
        dm[span(slot)] = dm[span(slot)] * live_in[slot].astype(BF)
    net.wait(act_moves)

    chunks = []
    flights = []

    def first_peer(k, p):
        return place.to_x if p or k in X_ONLY else place.to_y

    def credit(k, p):
        return free_sems.at[2 if p else 3 if k in X_ONLY else 1]

    def advance_zero(k):
        st, a, b = chunks[k], k % RING_A, k % RING_B
        st["s0"].wait_recv()

        @pl.loop(0, 4)
        def _(i):
            gbuf[a, c, i] = gbuf[a, c, i] + r0[a, i]

        pl.semaphore_signal(free_sems.at[0], inc=1, device_id=place.to_c, device_id_type=MESH)
        st["s1"] = []
        for p in range(2):
            if k >= RING_B:
                pl.semaphore_wait(credit(k, p), 1)
            peer = first_peer(k, p)
            src = gbuf.at[a, c, 2 * p + 1 - x] if peer is place.to_x else gbuf.at[a, c, pl.ds(2 * p, 2), 1 - y]
            st["s1"].append(net.send(src, r1.at[b, p], peer))

    def advance_one(k):
        st, a, b = chunks[k], k % RING_A, k % RING_B
        for p in range(2):
            st["s1"][p].wait_recv()
            for i in range(2):
                kept = gbuf[a, c, 2 * p + x, i] if first_peer(k, p) is place.to_x else gbuf[a, c, 2 * p + i, y]
                value = kept + r1[b, p, i]
                for zz in range(shards):
                    fbuf[b, zz % 2, zz // 2, 2 * p + i] = value[zz]
            if k + RING_B < N_CHUNKS:
                peer = first_peer(k + RING_B, p)
                pl.semaphore_signal(credit(k + RING_B, p), inc=1, device_id=peer, device_id_type=MESH)
        st["sa"] = net.send(fbuf.at[b, 1 - z % 2], ra.at[k], {"shard": z + 1 - 2 * (z % 2)})
        for copy in [st["s0"]] + st["s1"]:
            copy.wait_send()

    def advance_two(k):
        st, b = chunks[k], k % RING_B
        st["sa"].wait_recv()
        for i in range(2):
            gb[b, i] = fbuf[b, z % 2, i] + ra[k, i]
        st["sb"] = net.send(gb.at[b, 1 - z // 2], rb.at[k], {"shard": z + 2 - 4 * (z // 2)})
        st["sa"].wait_send()

    def advance_three(k):
        st, b = chunks[k], k % RING_B
        st["sb"].wait_recv()
        tsum[b] = gb[b, z // 2] + rb[k]
        st["s2"] = []
        for p in range(2):
            over_y = first_peer(k, p) is place.to_x
            src = tsum.at[b, 2 * p + 1 - (y if over_y else x)]
            st["s2"].append(net.send(src, r2.at[k, p], place.to_y if over_y else place.to_x))
        st["sb"].wait_send()

    def advance_four(k):
        st, b = chunks[k], k % RING_B
        for p in range(2):
            st["s2"][p].wait_recv()
            at = y if first_peer(k, p) is place.to_x else x
            tbuf[b, p] = tsum[b, 2 * p + at] + r2[k, p]
        st["s4"] = net.send(tbuf.at[b], r4.at[k], place.to_x)
        for copy in st["s2"]:
            copy.wait_send()

    def advance_five(k):
        st, b = chunks[k], k % RING_B
        st["s4"].wait_recv()
        out, kind, col = st["out"]
        for source, slot, at in ((tbuf, b, x), (r4, k, 1 - x)):
            for p in range(2):
                value = source[slot, p]
                if kind == "cols":
                    lanes = pl.ds(pl.multiple_of(col + p * 2 * block + at * block, block), block)
                    out[:, lanes] = value
                else:
                    rows = pl.ds(pl.multiple_of((p * 2 + at) * 64, 64), 64)
                    out[rows, pl.ds(col, block)] = value
        st["s4"].wait_send()

    stages = (advance_zero, advance_one, advance_two, advance_three, advance_four, advance_five)

    def pump():
        for flight in reversed(flights):
            if flight[1] < len(stages):
                stages[flight[1]](flight[0])
                flight[1] += 1

    def launch(out, kind, col):
        k = len(chunks)
        a = k % RING_A
        if k >= RING_A:
            pl.semaphore_wait(free_sems.at[0], 1)
        chunks.append({"out": (out, kind, col)})
        chunks[k]["s0"] = net.send(gbuf.at[a, 1 - c], r0.at[a], place.to_c)
        flights.append([k, 0])

    def grad_cols(pairs, out, col):
        a = len(chunks) % RING_A

        @pl.loop(0, 4)
        def _(i):
            total = None
            for left, right in pairs:
                term = dot(left[...], right(i), TN)
                total = term if total is None else total + term
            value = total.astype(BF).reshape(shards, 2, 2, 64, block)
            for cc in range(2):
                for yy in range(2):
                    gbuf[a, cc, i, yy] = value[:, yy, cc]

        launch(out, "cols", col)

    def grad_down(j):
        a = len(chunks) % RING_A
        right = dm[:, pl.ds(j * block, block)]

        @pl.loop(0, shards)
        def _(i):
            left = ad[0, :, pl.ds(pl.multiple_of(i * down_rows, down_rows), down_rows)]
            value = dot(left, right, TN).astype(BF).reshape(2, 2, 4, 64, block)
            for cc in range(2):
                for yy in range(2):
                    gbuf[a, cc, :, yy, i] = value[yy, cc]

        launch(gd, "rows", j * block)

    def lanes_at(start, n=block):
        return pl.ds(pl.multiple_of(start, block), n)

    slope_moves = [net.move(slope_in, ad.at[1])]
    grad_down(0)
    half_rows = width // 2
    per = half_rows // shard_rows
    wu_moves = blocks_of(
        wu_in, wu_all, pl.ds(0, hidden),
        lambda a: wb.at[a // per, pl.ds(pl.multiple_of((a % per) * shard_rows, shard_rows), shard_rows)],
    )
    nm_moves = [net.move(res_in, res), net.move(nm_in, nm)]
    wo_moves = blocks_of(
        wo_in, wo_all, every,
        lambda a: normed.at[a // per, pl.ds(pl.multiple_of((a % per) * shard_rows, shard_rows), shard_rows)],
    )
    late_moves = [net.move(att_in, att), net.move(q_in, qv), net.move(lse_in, lsev)]
    net.wait(wd_moves)
    net.wait(slope_moves)
    wide = 512

    def d_pre(lo, hi):
        @pl.loop(lo, hi)
        def _(j):
            lanes = pl.ds(pl.multiple_of(j * wide, wide), wide)
            value = dot(dm[...], wa[lanes, :], NT) * ad[1, :, lanes].astype(F32)
            value = value.astype(BF)
            ad[1, :, lanes] = value
            ub[j] = col_sum(value)

    def full(row):
        return jnp.concatenate([small_in[s, row : row + 1] for s in range(shards)], axis=1).astype(F32)

    n_wide = hidden // wide
    d_pre(0, n_wide // 4)
    pump()
    grad_down(1)
    d_pre(n_wide // 4, n_wide)
    pump()
    grad_down(2)
    net.wait(wu_moves)
    net.wait(nm_moves)
    down_bias = full(7)
    gain = full(5)
    gain_terms, shift_terms = None, None
    for slot in range(slots):
        rows = span(slot)
        value = res[rows] + dot(ad[0, rows], wa[...]) + down_bias
        xv[slot] = (value * live_in[slot]).astype(BF)
        incoming = jnp.concatenate([dot(ad[1, rows], wb[i], NT) for i in range(2)], axis=1)
        back, terms = norm_back(res[rows], gain, incoming)
        back = back + dm[rows].astype(F32)
        res[rows] = back
        dbr[rows] = back.astype(BF)
        terms, shifts = col_sum(terms), col_sum(incoming)
        gain_terms = terms if slot == 0 else gain_terms + terms
        shift_terms = shifts if slot == 0 else shift_terms + shifts
        if slot == 0:
            pump()
            grad_down(3)
    layer_moves = [net.move(xv, layer_out)]
    kv_moves = [net.move(kv_in, wa)]
    sg[5:6] = gain_terms
    sg[6:7] = shift_terms
    sg[4:5] = col_sum(dbr[...])
    sg[7:8] = col_sum(dm[...])
    net.wait(wo_moves)
    for i in range(2):
        dm[:, i * half_rows : (i + 1) * half_rows] = dot(dbr[...], normed[i], NT).astype(BF)
    normed_moves = [net.move(normed_in, normed)]
    pl.semaphore_signal(act_free, inc=1, device_id=place.to_c, device_id_type=MESH)

    def up_pairs(j):
        return [(nm, lambda i: ad[1, :, lanes_at(j * width + i * block)])]

    pump()
    grad_cols(up_pairs(0), gu, 0)
    net.wait(layer_moves)
    late_moves.append(net.move(x_in, xv))
    net.wait(late_moves)
    net.wait(kv_moves)
    scale = HEAD_DIM**-0.5

    def attend(slot, lo, hi):
        masks = head_masks(length)

        @pl.loop(lo, hi)
        def _(p):
            lanes = pl.ds(pl.multiple_of(p * PAIR, PAIR), PAIR)
            rows = span(slot)
            keys = wa[pl.ds(slot * 2 * clip, clip), lanes]
            values = wa[pl.ds((slot * 2 + 1) * clip, clip), lanes]
            queries = qv[rows, lanes] * BF(scale)
            d_out = dm[rows, lanes]
            along = (att[rows, lanes].astype(F32) * d_out.astype(F32)).T
            logs = lsev[slot, p]
            d_k, d_v, d_q = None, None, []
            for h in range(2):
                half = slice(h * HEAD_DIM, (h + 1) * HEAD_DIM)
                q_h, d_h = queries * masks[h], d_out * masks[h]
                probs = jnp.exp(dot(keys, q_h, NT) - logs[:, h * length : (h + 1) * length])
                mean = jnp.sum(along[half], axis=0, keepdims=True)
                d_scores = (probs * (dot(values, d_h, NT) - mean)).astype(BF)
                term_v = dot(probs.astype(BF), d_h)
                term_k = dot(d_scores, q_h)
                d_v = term_v if h == 0 else d_v + term_v
                d_k = term_k if h == 0 else d_k + term_k
                d_q.append(dot(keys, d_scores, TN)[half])
            qv[rows, lanes] = (jnp.concatenate(d_q, axis=0).T * scale).astype(BF)
            for part, value in ((0, d_k), (1, d_v)):
                value = value.astype(BF)
                for yy in range(2):
                    to = pl.ds(pl.multiple_of((yy * 2 + part) * width + p * PAIR, PAIR), PAIR)
                    for cc in range(2):
                        at = (yy * 2 + cc) * length
                        wb[cc, rows, to] = value[at : at + length]

    pairs = width // PAIR

    def share(slot):
        if slot == 0:
            pl.semaphore_wait(act_free, 1)
        return net.send(wb.at[1 - c, span(slot)], ad.at[0, span(slot)], place.to_c)

    attend(0, 0, pairs // 2)
    pump()
    grad_cols(up_pairs(1), gu, width)
    attend(0, pairs // 2, pairs)
    shares = [share(0)]
    pump()
    grad_cols(up_pairs(2), gu, 2 * width)
    attend(1, 0, pairs // 2)
    pump()
    grad_cols(up_pairs(3), gu, 3 * width)
    attend(1, pairs // 2, pairs)
    shares.append(share(1))
    wq_moves = []
    for part in (1, 2, 0):
        wq_moves.append(
            blocks_of(
                wq_in, wq_all, pl.ds(part * width, width),
                lambda a: wa.at[pl.ds(pl.multiple_of(part * width + a * shard_rows, shard_rows), shard_rows)],
            )
        )
    pump()
    grad_cols([(att, lambda i: dbr[:, lanes_at(i * block)])], go, 0)
    sg[2:3] = col_sum(qv[...])

    for slot in range(slots):
        shares[slot].wait_recv()

        @pl.loop(0, 2 * 2)
        def _(i):
            lanes = pl.ds(pl.multiple_of(i * width, width), width)
            wb[c, span(slot), lanes] = wb[c, span(slot), lanes] + ad[0, span(slot), lanes]

    def d_part(part, which, lanes_from=0, n=None):
        side = y if which == 0 else 1 - y
        n = width if n is None else n
        return wb[c, :, lanes_at((side * 2 + part) * width + lanes_from, n)]

    net.wait(wq_moves[0])
    net.wait(wq_moves[1])
    back = dot(d_part(0, 1), wa[pl.ds(width, width)], NT) + dot(d_part(1, 1), wa[pl.ds(2 * width, width)], NT)
    dm[...] = back.astype(BF)
    back_sends = [net.send(dm.at[span(slot)], dn.at[slot], place.to_y) for slot in range(slots)]
    pump()
    net.wait(normed_moves)
    grad_cols([(normed.at[0], lambda i: qv[:, lanes_at(i * block)])], gq, 0)
    sg[3:4] = col_sum(d_part(1, 0)) + col_sum(d_part(1, 1))
    pump()

    def kv_pairs(part):
        return [
            (normed.at[which], lambda i, which=which: d_part(part, which, i * block, block)) for which in range(2)
        ]

    grad_cols(kv_pairs(0), gq, width)
    pump()
    grad_cols(kv_pairs(1), gq, 2 * width)
    pump()
    net.wait(wq_moves[2])
    gain = full(0)
    for slot in range(slots):
        rows = span(slot)
        incoming = dot(qv[rows], wa[pl.ds(0, width)], NT)
        side = [wb[c, rows, lanes_at((y * 2 + part) * width, width)] for part in range(2)]
        incoming = incoming + dot(side[0], wa[pl.ds(width, width)], NT)
        incoming = incoming + dot(side[1], wa[pl.ds(2 * width, width)], NT)
        back_sends[slot].wait_recv()
        incoming = incoming + dn[slot].astype(F32)
        back, terms = norm_back(xv[slot].astype(F32), gain, incoming)
        xv[slot] = (res[rows] + back).astype(BF)
        terms, shifts = col_sum(terms), col_sum(incoming)
        gain_terms = terms if slot == 0 else gain_terms + terms
        shift_terms = shifts if slot == 0 else shift_terms + shifts
        if slot == 0:
            pump()
    out_moves = [net.move(xv, input_out)]
    sg[0:1] = gain_terms
    sg[1:2] = shift_terms
    per_row = width // wide
    for j in range(n_wide):
        sg[8 + j // per_row : 9 + j // per_row, (j % per_row) * wide : (j % per_row + 1) * wide] = ub[j]
    sg[12:16] = jnp.zeros((4, width), F32)

    sums = [net.send(sg, sr.at[0], place.to_c)]
    pump()
    sums[0].wait_recv()
    sr[4] = sg[...] + sr[0]
    sums.append(net.send(sr.at[4], sr.at[1], place.to_y))
    pump()
    sums[1].wait_recv()
    sr[5] = sr[4] + sr[1]
    sums += [net.send(sr.at[5], sr.at[7 + shift], place.to_z(shift)) for shift in range(1, shards)]
    pump()
    for copy in sums[2:]:
        copy.wait_recv()
    total = sr[5]
    for shift in range(1, shards):
        total = total + sr[7 + shift]
    sr[6] = total
    sums.append(net.send(sr.at[6], sr.at[2], place.to_x))
    pump()
    sums[-1].wait_recv()
    sr[3] = sr[6] + sr[2]
    out_moves.append(net.move(sr.at[3], sg_out))
    while any(flight[1] < len(stages) for flight in flights):
        pump()
    for _ in range(RING_A):
        pl.semaphore_wait(free_sems.at[0], 1)
    out_moves += [net.move(a, b) for a, b in ((gq, gq_out), (go, go_out), (gu, gu_out), (gd, gd_out))]
    finish(net, chunks)


def finish(net, chunks):
    done = set()
    for st in chunks:
        for name, value in st.items():
            if name.startswith("s"):
                done.update(id(copy) for copy in (value if isinstance(value, list) else [value]))
    for copy in net.remote:
        if id(copy) not in done:
            copy.wait_send()
    net.wait(net.local)


def backward(shards, x, cot, live, small, weights, gathered, kept):
    slots, length, width = x.shape
    tokens = slots * length
    hidden = weights[2].shape[1]
    down_rows = weights[3].shape[0]
    pairs = width // PAIR
    owned = weights[0].shape[0] // 4
    any_ = pl.BlockSpec(memory_space=pl.ANY)
    vmem = pl.BlockSpec(memory_space=pltpu.VMEM)
    sd = jax.ShapeDtypeStruct
    outs = (
        sd((slots, length, width), BF), sd((slots, length, width), BF), sd((owned, 3 * width), BF), sd((owned, width), BF),
        sd((owned, hidden), BF), sd((down_rows // 4, width), BF), sd((16, width), F32),
    )
    tile = (64, 256)
    return pl.pallas_call(
        functools.partial(backward_kernel, shards),
        out_shape=outs,
        in_specs=[any_] * 2 + [vmem] * 2 + [any_] * 17,
        out_specs=(any_,) * len(outs),
        scratch_shapes=[
            pltpu.VMEM((hidden, width), BF),
            pltpu.VMEM((2, width // 2, hidden), BF),
            pltpu.VMEM((2, tokens, hidden), BF),
            pltpu.VMEM((tokens, width), BF),
            pltpu.VMEM((tokens, width), BF),
            pltpu.VMEM((tokens, width), F32),
            pltpu.VMEM((tokens, width), BF),
            pltpu.VMEM((tokens, width), BF),
            pltpu.VMEM((tokens, width), BF),
            pltpu.VMEM((2, tokens, width), BF),
            pltpu.VMEM((slots, length, width), BF),
            pltpu.VMEM((slots, length, width), BF),
            pltpu.VMEM((slots, pairs, 1, 2 * length), F32),
            pltpu.VMEM((owned, 3 * width), BF),
            pltpu.VMEM((owned, width), BF),
            pltpu.VMEM((owned, hidden), BF),
            pltpu.VMEM((down_rows // 4, width), BF),
            pltpu.VMEM((16, width), F32),
            pltpu.VMEM((hidden // 512, 1, 512), F32),
            pltpu.VMEM((7 + shards, 16, width), F32),
            pltpu.VMEM((RING_A, 2, 4, 2, shards) + tile, BF),
            pltpu.VMEM((RING_A, 4, 2, shards) + tile, BF),
            pltpu.VMEM((RING_B, 2, 2, shards) + tile, BF),
            pltpu.VMEM((N_CHUNKS, 2, 4) + tile, BF),
            pltpu.VMEM((N_CHUNKS, 4) + tile, BF),
            pltpu.VMEM((N_CHUNKS, 2) + tile, BF),
            pltpu.VMEM((N_CHUNKS, 2) + tile, BF),
            pltpu.VMEM((RING_B, 2, 2, 4) + tile, BF),
            pltpu.VMEM((RING_B, 2, 4) + tile, BF),
            pltpu.VMEM((RING_B, 4) + tile, BF),
            pltpu.VMEM((RING_B, 2) + tile, BF),
            pltpu.SemaphoreType.DMA((N_REMOTE2,)),
            pltpu.SemaphoreType.DMA((N_REMOTE2,)),
            pltpu.SemaphoreType.DMA((N_LOCAL2,)),
            pltpu.SemaphoreType.REGULAR((4,)),
            pltpu.SemaphoreType.REGULAR,
        ],
        compiler_params=pltpu.CompilerParams(collective_id=2, has_side_effects=True, vmem_limit_bytes=63 * MIB),
    )(x, cot, live, small, *weights, *gathered, *kept)


def place_kernel(n, *refs):
    srcs, dsts = refs[: n + 1], refs[n + 1 : 2 * n + 3]
    small, bufs, wide, sems = refs[2 * n + 3], refs[2 * n + 4 : 3 * n + 4], refs[3 * n + 4 : -1], refs[-1]
    loads = [pltpu.make_async_copy(src, buf, sems.at[i]) for i, (src, buf) in enumerate(zip(srcs, bufs + (small,)))]
    for copy in loads:
        copy.start()
    stores = []
    for i in range(n):
        loads[i].wait()
        buf = bufs[i]
        if i >= 2:
            buf = wide[i - 2]
            buf[...] = bufs[i][...].astype(F32)
        stores.append(pltpu.make_async_copy(buf, dsts[i], sems.at[n + 1 + i]))
        stores[-1].start()
    loads[n].wait()
    at = lax.axis_index("shard") * lax.axis_size("seq") + lax.axis_index("seq")
    vec_out, up_out = dsts[n:]
    pair = small[0:8, pl.ds(pl.multiple_of(at // 2 * 128, 128), 128)]
    vec_out[...] = jnp.where(at % 2 == 0, pair[:, :64], pair[:, 64:])
    up_out[...] = small[pl.ds(8 + at // 4, 1), pl.ds(pl.multiple_of(at % 4 * 256, 256), 256)]
    for copy in stores:
        copy.wait()


def place_results(sums, *arrays):
    any_, vmem = pl.BlockSpec(memory_space=pl.ANY), pl.BlockSpec(memory_space=pltpu.VMEM)
    n = len(arrays)
    outs = tuple(jax.ShapeDtypeStruct(a.shape, F32 if a.ndim == 2 else BF) for a in arrays)
    return pl.pallas_call(
        functools.partial(place_kernel, n),
        out_shape=outs + (jax.ShapeDtypeStruct((8, 64), F32), jax.ShapeDtypeStruct((1, 256), F32)),
        in_specs=[any_] * (n + 1),
        out_specs=(any_,) * n + (vmem, vmem),
        scratch_shapes=[pltpu.VMEM(sums.shape, F32)]
        + [pltpu.VMEM(a.shape, BF) for a in arrays]
        + [pltpu.VMEM(a.shape, F32) for a in arrays[2:]]
        + [pltpu.SemaphoreType.DMA((2 * n + 1,))],
        compiler_params=pltpu.CompilerParams(vmem_limit_bytes=60 * MIB),
    )(*arrays, sums)


def local(
    activations, cotangent, clip_loads, attn_gain, attn_shift, w_qkv, q_bias, v_bias, w_out, out_bias,
    mlp_gain, mlp_shift, w_up, up_bias, w_down, down_bias,
):
    shards = lax.axis_size("shard")
    x, cot = activations[0], cotangent[0]
    slots, length, width = x.shape
    rows = w_qkv.shape[0]
    vectors = [attn_gain, attn_shift, q_bias, v_bias, out_bias, mlp_gain, mlp_shift, down_bias]
    small = jnp.broadcast_to(up_bias.reshape(1, 4, rows), (4, 4, rows)).reshape(16, rows)
    row = lax.broadcasted_iota(jnp.int32, (16, rows), 0)
    for i, vector in enumerate(vectors):
        small = jnp.where(row == i, vector[None, :], small)
    weights = (w_qkv, w_out, w_up, w_down)
    *gathered, normed, q, kv, lse, att, res, nm, act, slope, small = forward(shards, x, small, *weights)
    live = (jnp.arange(slots) < clip_loads[0]).astype(F32)
    live = jnp.broadcast_to(live[:, None, None], (slots, 1, width))
    kept = (normed, q, kv.reshape(-1, width), lse, att, res, nm, act, slope)
    layer_out, input_grad, gq, go, gu, gd, sums = backward(shards, x, cot, live, small, weights, gathered, kept)
    pods = lax.axis_size("replica")
    if pods > 2:
        ends = [[p for p in range(pods) if p % 2 == side] for side in range(2)]
        gq, go, gu, gd, sums = (lax.psum(g, "replica", axis_index_groups=ends) for g in (gq, go, gu, gd, sums))
    layer_out, input_grad, gq, go, gu, gd, vec, up = place_results(sums, layer_out, input_grad, gq, go, gu, gd)
    return (
        layer_out[None], input_grad[None], vec[0], vec[1], gq, vec[2], vec[3], go, vec[4], vec[5], vec[6], gu, up[0], gd, vec[7],
    )


def solution(mesh):
    rows = P("shard")
    full = P("shard", None)
    clips = P(("replica", "shard"), None, "seq", None)
    vec = P(("shard", "seq"))
    mat = P(("shard", "seq"), None)
    return jax.shard_map(
        local,
        mesh=mesh,
        in_specs=(
            clips, clips, P(("replica", "shard")), rows, rows, full, rows, rows, full, rows, rows, rows, full, rows, full, rows,
        ),
        out_specs=(clips, clips, vec, vec, mat, vec, vec, mat, vec, vec, vec, mat, vec, mat, vec),
        check_vma=False,
    )
```

```python
import functools
import jax
import jax.numpy as jnp
from jax import lax
from jax.experimental import pallas as pl
from jax.experimental.pallas import tpu as pltpu
from jax.sharding import PartitionSpec as P

MESH = pl.DeviceIdType.MESH
BF = jnp.bfloat16
F32 = jnp.float32
HEAD_DIM = 64
PAIR = 2 * HEAD_DIM
EPSILON = 1e-06
NN = (((1,), (0,)), ((), ()))
NT = (((1,), (1,)), ((), ()))
TN = (((0,), (0,)), ((), ()))
MIB = 2**20


def dot(a, b, dims=NN):
    return lax.dot_general(a, b, dims, preferred_element_type=F32)


class Place:
    def __init__(self, shards):
        self.shards = shards
        r, self.z, q = (lax.axis_index(a) for a in ("replica", "shard", "seq"))
        self.x, self.y, self.c = r % 2, q // 2, q % 2
        self.q = q
        self.to_x = {"replica": r + 1 - 2 * self.x}
        self.to_y = {"seq": q + 2 - 4 * self.y}
        self.to_c = {"seq": q + 1 - 2 * self.c}

    def to_z(self, shift):
        return {"shard": (self.z + shift) % self.shards}

    def behind(self, shift):
        return (self.z + self.shards - shift) % self.shards

    def greet(self):
        barrier = pltpu.get_barrier_semaphore()
        peers = [self.to_x, self.to_y, self.to_c]
        peers += [self.to_z(shift) for shift in range(1, self.shards)]
        for peer in peers:
            pl.semaphore_signal(barrier, inc=1, device_id=peer, device_id_type=MESH)
        pl.semaphore_wait(barrier, len(peers))


class Copies:
    def __init__(self, send_sems, recv_sems, local_sems):
        self.send_sems, self.recv_sems, self.local_sems = send_sems, recv_sems, local_sems
        self.remote, self.local = [], []

    def send(self, src, dst, peer):
        at = len(self.remote)
        copy = pltpu.make_async_remote_copy(
            src_ref=src, dst_ref=dst, send_sem=self.send_sems.at[at], recv_sem=self.recv_sems.at[at],
            device_id=peer, device_id_type=MESH,
        )
        copy.start()
        self.remote.append(copy)
        return copy

    def move(self, src, dst):
        at = len(self.local)
        copy = pltpu.make_async_copy(src, dst, self.local_sems.at[at])
        copy.start()
        self.local.append([copy, False])
        return self.local[-1]

    def wait(self, moves):
        for entry in moves:
            if not entry[1]:
                entry[0].wait()
                entry[1] = True

    def finish(self):
        for copy in self.remote:
            copy.wait_send()
        self.wait(self.local)


def normalized(values, gain, shift):
    center = values - jnp.mean(values, axis=-1, keepdims=True)
    spread = jnp.mean(center * center, axis=-1, keepdims=True)
    return center * lax.rsqrt(spread + EPSILON) * gain + shift


def head_masks(rows):
    lane = lax.broadcasted_iota(jnp.int32, (rows, PAIR), 1)
    first = (lane < HEAD_DIM).astype(F32).astype(BF)
    return first, (lane >= HEAD_DIM).astype(F32).astype(BF)


def both_heads(values, masks):
    return jnp.concatenate([values * masks[0], values * masks[1]], axis=0)


N_REMOTE1, N_LOCAL1 = 176, 80
AHEAD = 2
IN_HALVES = (3, 5, 7)


def forward_kernel(
    shards,
    x_in, small_in, wq_in, wo_in, wu_in, wd_in,
    wq_all, wo_all, wu_all, wd_all,
    normed_out, q_out, kv_out, lse_out, att_out, res_out, nm_out, act_out, slope_out, small_out,
    xv, smv, normed, qv, kvb, lsev, att, res, nm, act, slope, wq, wo, wu,
    send_sems, recv_sems, local_sems,
):
    place = Place(shards)
    net = Copies(send_sems, recv_sems, local_sems)
    x, y, z, c = place.x, place.y, place.z, place.c
    slots, length, width = x_in.shape
    tokens = slots * length
    hidden = wu_in.shape[1]
    shard_rows = wq_in.shape[0]
    place.greet()

    small_moves = [net.move(small_in, smv.at[z])]
    small_sends = [net.send(small_in, smv.at[z], place.to_z(s)) for s in range(1, shards)]
    x_moves = [net.move(x_in, xv.at[0])]
    x_sends = [net.send(x_in.at[0], xv.at[1, 0], place.to_y)]

    chunks = [(wq_in, wq_all.at[part], part * width, 0, False) for part in (1, 2, 0)]
    chunks.append((wo_in, wo_all.at[0], 0, 0, False))
    chunks += [(wu_in, wu_all.at[j], j * width, 0, False) for j in range(hidden // width)]
    chunks += [(wd_in, wd_all.at[j], 0, j * shard_rows, True) for j in range(wd_in.shape[0] // shard_rows)]
    chunks = [chunk[:4] + (chunk[4] or i in IN_HALVES,) for i, chunk in enumerate(chunks)]
    state = [dict() for _ in chunks]
    others = pl.ds(1, shards - 1)
    eighth, quarter = shard_rows // 8, shard_rows // 4
    near, far = {"shard": z + 1 - 2 * (z % 2)}, {"shard": z + 2 - 4 * (z // 2)}
    at_near = 1 + 2 * (z % 2)

    def region(i, px, py, pc, side=None, first=0):
        if chunks[i][4]:
            piece = ((px + py) % 2 * 2 + pc) * quarter
            at, n = {None: (0, quarter), "x": (0, eighth), "y": (eighth, eighth)}[side]
        else:
            piece = ((px * 2 + py) * 2 + pc) * eighth
            at, n = {None: (0, eighth), "y": (0, eighth // 2), "x": (eighth // 2, eighth // 2)}[side]
        return pl.ds(pl.multiple_of(first + piece + at, 16), n)

    def start_z(i):
        src, all_, col, row, _ = chunks[i]
        rows = region(i, x, y, c)
        src = src.at[region(i, x, y, c, None, row), pl.ds(col, width)]
        state[i]["far"] = net.send(src, all_.at[2, rows], far)
        state[i]["near"] = net.send(src, all_.at[at_near, rows], near)

    def relay(i):
        all_ = chunks[i][1]
        rows = region(i, x, y, c)
        state[i]["far"].wait_recv()
        state[i]["relay"] = net.send(all_.at[2, rows], all_.at[4 - at_near, rows], near)
        if i + AHEAD < len(chunks):
            start_z(i + AHEAD)

    def pass_piece(i, px, py, pc, peer, side=None):
        ref = chunks[i][1].at[others, region(i, px, py, pc, side)]
        return net.send(ref, ref, peer)

    def plane_one(i):
        st = state[i]
        st["near"].wait_recv()
        st["relay"].wait_recv()
        halves = chunks[i][4]
        st["x"] = pass_piece(i, x, y, c, place.to_x, "x" if halves else None)
        st["y"] = pass_piece(i, x, y, c, place.to_y, "y" if halves else None)
        st["core"] = [pass_piece(i, x, y, c, place.to_c)]

    def plane_two(i):
        st = state[i]
        halves = chunks[i][4]
        st["y"].wait_recv()
        if not halves:
            st["yx"] = pass_piece(i, x, 1 - y, c, place.to_x, "x")
        st["core"].append(pass_piece(i, x, 1 - y, c, place.to_c, "y" if halves else None))
        st["x"].wait_recv()
        if not halves:
            st["xy"] = pass_piece(i, 1 - x, y, c, place.to_y, "y")
        st["core"].append(pass_piece(i, 1 - x, y, c, place.to_c, "x" if halves else None))

    def plane_three(i):
        st = state[i]
        if chunks[i][4]:
            return
        for name, side in (("yx", "x"), ("xy", "y")):
            st[name].wait_recv()
            st["core"].append(pass_piece(i, 1 - x, 1 - y, c, place.to_c, side))

    def arrived(i):
        for copy in state[i]["core"]:
            copy.wait_recv()

    def load(i, dst):
        src, all_, col, *_ = chunks[i]
        moves = []
        for s in range(shards):
            rows = pl.ds(pl.multiple_of(place.behind(s) * shard_rows, shard_rows), shard_rows)
            cs = pl.ds(col, width)
            from_ = src.at[:, cs] if s == 0 else all_.at[s]
            moves.append(net.move(from_, dst.at[rows, cs]))
        return moves

    for i in range(AHEAD):
        start_z(i)

    net.wait(small_moves)
    for copy in small_sends:
        copy.wait_recv()
    small_moves = [net.move(smv, small_out)]

    def small(row, count=1):
        return jnp.concatenate([smv[s] for s in range(shards)], axis=1)[row : row + count].astype(F32)

    def norm_first(which, slot):
        rows = pl.ds(slot * length, length)
        normed[which, rows, :] = normalized(xv[which, slot].astype(F32), small(0), small(1)).astype(BF)

    loads = {}

    def step(i):
        if i + 4 < len(chunks):
            relay(i + 4)
        if i + 2 < len(chunks):
            plane_one(i + 2)
        if 0 <= i + 1 < len(chunks):
            plane_two(i + 1)
        if 0 <= i < len(chunks):
            plane_three(i)
        if 0 <= i - 1:
            arrived(i - 1)
            if i - 1 < len(targets):
                loads[i - 1] = load(i - 1, targets[i - 1])

    targets = [wq] * 3 + [wo] + [wu] * (hidden // width)

    net.wait(x_moves)
    norm_first(0, 0)
    relay(0)
    relay(1)
    step(-2)
    x_sends.append(net.send(x_in.at[1], xv.at[1, 1], place.to_y))
    norm_first(0, 1)
    step(-1)
    x_sends[0].wait_recv()
    norm_first(1, 0)
    step(0)
    x_sends[1].wait_recv()
    norm_first(1, 1)
    moves_out = [net.move(normed, normed_out)]
    step(1)
    v_bias = small(3)

    def project_kv(which, part):
        lanes = pl.ds((part + 1) * width, width)
        rows = normed[which]
        out = dot(rows, wq[:, lanes])
        if part:
            out = out + v_bias
        out = out.astype(BF)
        at = (y if which == 0 else 1 - y) * 2 + c
        for slot in range(slots):
            kvb[slot, part, at] = out[slot * length : (slot + 1) * length]

    shares = []

    def share(part):
        for which in range(2):
            at = (y if which == 0 else 1 - y) * 2 + c
            ref = kvb.at[:, part, at]
            shares.append(net.send(ref, ref, place.to_c))

    net.wait(loads[0])
    project_kv(0, 0)
    project_kv(1, 0)
    share(0)
    step(2)
    net.wait(loads[1])
    project_kv(0, 1)
    project_kv(1, 1)
    share(1)
    step(3)
    net.wait(loads[2])
    qv[...] = (dot(normed[0], wq[:, :width]) + small(2)).astype(BF)
    moves_out.append(net.move(qv, q_out))
    for copy in shares:
        copy.wait_recv()
    moves_out.append(net.move(kvb, kv_out))

    def attend(slot, lo, hi):
        masks = head_masks(length)

        @pl.loop(lo, hi)
        def _(p):
            lanes = pl.ds(pl.multiple_of(p * PAIR, PAIR), PAIR)
            rows = pl.ds(slot * length, length)
            queries = both_heads(qv[rows, lanes] * BF(HEAD_DIM**-0.5), masks)
            keys = kvb[slot, 0, :, :, lanes].reshape(-1, PAIR)
            values = kvb[slot, 1, :, :, lanes].reshape(-1, PAIR)
            scores = dot(keys, queries, NT)
            top = jnp.max(scores, axis=0, keepdims=True)
            terms = jnp.exp(scores - top)
            total = jnp.sum(terms, axis=0, keepdims=True)
            lsev[slot, p] = top + jnp.log(total)
            out = dot(values, terms.astype(BF), TN) * (1.0 / total)
            out = jnp.concatenate([out[:HEAD_DIM, :length], out[HEAD_DIM:, length:]], axis=0)
            att[rows, lanes] = out.T.astype(BF)

    pairs = width // PAIR
    attend(0, 0, pairs // 2)
    step(4)
    attend(0, pairs // 2, pairs)
    step(5)
    attend(1, 0, pairs // 2)
    step(6)
    attend(1, pairs // 2, pairs)
    moves_out += [net.move(lsev, lse_out), net.move(att, att_out)]
    step(7)
    net.wait(loads[3])
    out_bias, mlp_gain, mlp_shift = small(4), small(5), small(6)
    for slot in range(slots):
        rows = pl.ds(slot * length, length)
        value = xv[0, slot].astype(F32) + dot(att[rows], wo[...]) + out_bias
        res[rows] = value
        nm[rows] = normalized(value, mlp_gain, mlp_shift).astype(BF)
    moves_out += [net.move(res, res_out), net.move(nm, nm_out)]

    up_block = 512

    def up(part):
        @pl.loop(part * (width // up_block), (part + 1) * (width // up_block))
        def _(j):
            lanes = pl.ds(pl.multiple_of(j * up_block, up_block), up_block)
            s, inner = j // (wd_in.shape[0] // up_block), j % (wd_in.shape[0] // up_block)
            first = 8 + inner * (up_block // shard_rows)
            sm = smv[s].astype(F32)
            row = jnp.concatenate([sm[8:9], sm[9:10]], axis=1)
            row2 = jnp.concatenate([sm[10:11], sm[11:12]], axis=1)
            bias = jnp.where(inner == 0, row, row2)
            pre = dot(nm[...], wu[:, lanes]) + bias
            phi = 0.5 + 0.5 * lax.erf(pre * (0.5**0.5))
            density = jnp.exp(pre * pre * -0.5) * 0.3989422804014327
            act[:, lanes] = (pre * phi).astype(BF)
            slope[:, lanes] = (phi + pre * density).astype(BF)

    for j in range(hidden // width):
        if 4 + j not in loads:
            step(5 + j)
        net.wait(loads[4 + j])
        up(j)
        if j % 2:
            lanes = pl.ds((j - 1) * width, 2 * width)
            moves_out += [net.move(act.at[:, lanes], act_out.at[:, lanes]), net.move(slope.at[:, lanes], slope_out.at[:, lanes])]
    for i in range(9, len(chunks) + 1):
        step(i)
    net.finish()


def forward(shards, x, small, wq, wo, wu, wd):
    slots, length, width = x.shape
    tokens = slots * length
    hidden = wu.shape[1]
    pairs = width // PAIR
    any_ = pl.BlockSpec(memory_space=pl.ANY)
    sd = jax.ShapeDtypeStruct
    square = (shards, wq.shape[0], width)
    outs = (
        sd((3,) + square, BF), sd((1,) + square, BF), sd((hidden // width,) + square, BF), sd((wd.shape[0] // wq.shape[0],) + square, BF),
        sd((2, tokens, width), BF), sd((tokens, width), BF), sd((slots, 2, 4, length, width), BF),
        sd((slots, pairs, 1, 2 * length), F32), sd((tokens, width), BF), sd((tokens, width), F32),
        sd((tokens, width), BF), sd((tokens, hidden), BF), sd((tokens, hidden), BF), sd((shards,) + small.shape, BF),
    )
    return pl.pallas_call(
        functools.partial(forward_kernel, shards),
        out_shape=outs,
        in_specs=[any_] * 6,
        out_specs=(any_,) * len(outs),
        scratch_shapes=[
            pltpu.VMEM((2, slots, length, width), BF),
            pltpu.VMEM((shards,) + small.shape, BF),
            pltpu.VMEM((2, tokens, width), BF),
            pltpu.VMEM((tokens, width), BF),
            pltpu.VMEM((slots, 2, 4, length, width), BF),
            pltpu.VMEM((slots, pairs, 1, 2 * length), F32),
            pltpu.VMEM((tokens, width), BF),
            pltpu.VMEM((tokens, width), F32),
            pltpu.VMEM((tokens, width), BF),
            pltpu.VMEM((tokens, hidden), BF),
            pltpu.VMEM((tokens, hidden), BF),
            pltpu.VMEM((width, 3 * width), BF),
            pltpu.VMEM((width, width), BF),
            pltpu.VMEM((width, hidden), BF),
            pltpu.SemaphoreType.DMA((N_REMOTE1,)),
            pltpu.SemaphoreType.DMA((N_REMOTE1,)),
            pltpu.SemaphoreType.DMA((N_LOCAL1,)),
        ],
        compiler_params=pltpu.CompilerParams(collective_id=1, has_side_effects=True, vmem_limit_bytes=62 * MIB),
    )(x, small, wq, wo, wu, wd)


N_REMOTE2, N_LOCAL2 = 160, 80
RING_A, RING_B, N_CHUNKS = 3, 3, 12
X_ONLY = (8, 9)
IN_PARTS = (11,)


def norm_back(values, gain, incoming):
    center = values - jnp.mean(values, axis=-1, keepdims=True)
    spread = jnp.mean(center * center, axis=-1, keepdims=True)
    r = lax.rsqrt(spread + EPSILON)
    xhat = center * r
    e = incoming * gain
    back = r * (e - jnp.mean(e, axis=-1, keepdims=True) - xhat * jnp.mean(e * xhat, axis=-1, keepdims=True))
    return back, incoming * xhat


def col_sum(values):
    return jnp.sum(values.astype(F32), axis=0, keepdims=True)


def backward_kernel(
    shards,
    x_in, cot_in, live_in, small_in, wq_in, wo_in, wu_in, wd_in, wq_all, wo_all, wu_all, wd_all,
    normed_in, q_in, kv_in, lse_in, att_in, res_in, nm_in, act_in, slope_in,
    layer_out, input_out, gq_out, go_out, gu_out, gd_out, sg_out,
    wa, wb, ad, nm, att, res, dm, dbr, qv, normed, xv, dn, lsev,
    gq, go, gu, gd, sg, ub, sr,
    gbuf, r0, r1, ra, rb, r2, r4, fbuf, gb, tsum, tbuf,
    send_sems, recv_sems, local_sems, free_sems, act_free,
):
    place = Place(shards)
    net = Copies(send_sems, recv_sems, local_sems)
    x, y, z, c = place.x, place.y, place.z, place.c
    slots, length, width = x_in.shape
    tokens = slots * length
    hidden = wu_in.shape[1]
    shard_rows = wq_in.shape[0]
    down_rows = wd_in.shape[0]
    block = 256
    clip = 4 * length

    def span(slot):
        return pl.ds(slot * length, length)

    cot_moves = [net.move(cot_in.at[slot], dm.at[span(slot)]) for slot in range(slots)]
    act_moves = [net.move(act_in, ad.at[0])]

    def blocks_of(own, gathered, dst_of):
        moves = []
        for s in range(shards):
            dst = dst_of(place.behind(s))
            if s == 0:
                moves.append(net.move(own, dst))
                continue
            for j, square in enumerate(gathered):
                at = (pl.ds(j * shard_rows, shard_rows),) if own.shape[0] > shard_rows else (slice(None), pl.ds(j * width, width))
                moves.append(net.move(square.at[s], dst.at[at]))
        return moves

    wd_moves = blocks_of(
        wd_in, [wd_all.at[j] for j in range(down_rows // shard_rows)],
        lambda a: wa.at[pl.ds(pl.multiple_of(a * down_rows, down_rows), down_rows)],
    )
    place.greet()

    net.wait(cot_moves)
    for slot in range(slots):
        dm[span(slot)] = dm[span(slot)] * live_in[slot].astype(BF)
    net.wait(act_moves)

    flights = []

    def first_peer(k, p):
        return place.to_x if p or k in X_ONLY else place.to_y

    def credit(k, p):
        return free_sems.at[2 if p else 3 if k in X_ONLY else 1]

    def advance_zero(st):
        k, rows = st["k"], st["rows"]
        a, b = k % RING_A, k % RING_B
        st["s0"].wait_recv()

        @pl.loop(0, 4)
        def _(i):
            gbuf[a, c, i, :, :, rows, :] = gbuf[a, c, i, :, :, rows, :] + r0[a, i, :, :, rows, :]

        if st["last"]:
            pl.semaphore_signal(free_sems.at[0], inc=1, device_id=place.to_c, device_id_type=MESH)
        st["s1"] = []
        for p in range(2):
            if k >= RING_B and st["first"]:
                pl.semaphore_wait(credit(k, p), 1)
            peer = first_peer(k, p)
            if peer is place.to_x:
                src = gbuf.at[a, c, 2 * p + 1 - x, :, :, rows, :]
            else:
                src = gbuf.at[a, c, pl.ds(2 * p, 2), 1 - y, :, rows, :]
            st["s1"].append(net.send(src, r1.at[b, p, :, :, rows, :], peer))

    def advance_one(st):
        k, rows = st["k"], st["rows"]
        a, b = k % RING_A, k % RING_B
        for p in range(2):
            st["s1"][p].wait_recv()
            for i in range(2):
                if first_peer(k, p) is place.to_x:
                    kept = gbuf[a, c, 2 * p + x, i, :, rows, :]
                else:
                    kept = gbuf[a, c, 2 * p + i, y, :, rows, :]
                value = kept + r1[b, p, i, :, rows, :]
                for zz in range(shards):
                    fbuf[b, zz % 2, zz // 2, 2 * p + i, rows, :] = value[zz]
            if k + RING_B < N_CHUNKS:
                peer = first_peer(k + RING_B, p)
                pl.semaphore_signal(credit(k + RING_B, p), inc=1, device_id=peer, device_id_type=MESH)
        near = {"shard": z + 1 - 2 * (z % 2)}
        st["sa"] = net.send(fbuf.at[b, 1 - z % 2, :, :, rows, :], ra.at[k, :, :, rows, :], near)
        for copy in [st["s0"]] + st["s1"]:
            copy.wait_send()

    def advance_two(st):
        k, rows = st["k"], st["rows"]
        b = k % RING_B
        st["sa"].wait_recv()
        for i in range(2):
            gb[b, i, :, rows, :] = fbuf[b, z % 2, i, :, rows, :] + ra[k, i, :, rows, :]
        far = {"shard": z + 2 - 4 * (z // 2)}
        st["sb"] = net.send(gb.at[b, 1 - z // 2, :, rows, :], rb.at[k, :, rows, :], far)
        st["sa"].wait_send()

    def advance_three(st):
        k, rows = st["k"], st["rows"]
        b = k % RING_B
        st["sb"].wait_recv()
        tsum[b, :, rows, :] = gb[b, z // 2, :, rows, :] + rb[k, :, rows, :]
        st["s2"] = []
        for p in range(2):
            over_y = first_peer(k, p) is place.to_x
            src = tsum.at[b, 2 * p + 1 - (y if over_y else x), rows, :]
            st["s2"].append(net.send(src, r2.at[k, p, rows, :], place.to_y if over_y else place.to_x))
        st["sb"].wait_send()

    def advance_four(st):
        k, rows = st["k"], st["rows"]
        b = k % RING_B
        for p in range(2):
            st["s2"][p].wait_recv()
            at = y if first_peer(k, p) is place.to_x else x
            tbuf[b, p, rows, :] = tsum[b, 2 * p + at, rows, :] + r2[k, p, rows, :]
        st["s4"] = net.send(tbuf.at[b, :, rows, :], r4.at[k, :, rows, :], place.to_x)
        for copy in st["s2"]:
            copy.wait_send()

    def advance_five(st):
        k, rows = st["k"], st["rows"]
        b = k % RING_B
        st["s4"].wait_recv()
        out, kind, col = st["out"]
        for source, slot, at in ((tbuf, b, x), (r4, k, 1 - x)):
            for p in range(2):
                value = source[slot, p, rows, :]
                if kind == "cols":
                    out[rows, pl.ds(pl.multiple_of(col + p * 2 * block + at * block, block), block)] = value
                else:
                    out[pl.ds(pl.multiple_of((p * 2 + at) * 64 + rows.start, 16), rows.size), pl.ds(col, block)] = value
        st["s4"].wait_send()

    stages = (advance_zero, advance_one, advance_two, advance_three, advance_four, advance_five)

    def pump():
        for st in reversed(flights):
            if st["stage"] < len(stages):
                stages[st["stage"]](st)
                st["stage"] += 1

    def next_chunk():
        return flights[-1]["k"] + 1 if flights else 0

    def launch(out, kind, col):
        k = next_chunk()
        a = k % RING_A
        if k >= RING_A:
            pl.semaphore_wait(free_sems.at[0], 1)
        parts = 2 if k in IN_PARTS else 1
        made = []
        for part in range(parts):
            rows = pl.ds(part * (64 // parts), 64 // parts)
            st = {"k": k, "stage": 0, "rows": rows, "out": (out, kind, col)}
            st["first"], st["last"] = part == 0, part == parts - 1
            st["s0"] = net.send(gbuf.at[a, 1 - c, :, :, :, rows, :], r0.at[a, :, :, :, rows, :], place.to_c)
            made.append(st)
        flights.extend(reversed(made))

    def grad_cols(pairs, out, col):
        a = next_chunk() % RING_A

        @pl.loop(0, 2)
        def _(i):
            total = None
            for left, right in pairs:
                term = dot(left[...], right(i), TN)
                total = term if total is None else total + term
            for j in range(2):
                value = total[:, j * block : (j + 1) * block].astype(BF).reshape(shards, 2, 2, 64, block)
                for cc in range(2):
                    for yy in range(2):
                        gbuf[a, cc, i * 2 + j, yy] = value[:, yy, cc]

        launch(out, "cols", col)

    def grad_down(j):
        a = next_chunk() % RING_A
        right = dm[:, pl.ds(j * block, block)]

        @pl.loop(0, shards)
        def _(i):
            left = ad[0, :, pl.ds(pl.multiple_of(i * down_rows, down_rows), down_rows)]
            value = dot(left, right, TN).astype(BF).reshape(2, 2, 4, 64, block)
            for cc in range(2):
                for yy in range(2):
                    gbuf[a, cc, :, yy, i] = value[yy, cc]

        launch(gd, "rows", j * block)

    def lanes_at(start, n=block):
        return pl.ds(pl.multiple_of(start, block), n)

    slope_moves = [net.move(slope_in, ad.at[1])]
    grad_down(0)
    half_rows = width // 2
    per = half_rows // shard_rows
    wu_moves = blocks_of(
        wu_in, [wu_all.at[j] for j in range(hidden // width)],
        lambda a: wb.at[a // per, pl.ds(pl.multiple_of((a % per) * shard_rows, shard_rows), shard_rows)],
    )
    nm_moves = [net.move(res_in, res), net.move(nm_in, nm)]
    wo_moves = blocks_of(
        wo_in, [wo_all.at[0]],
        lambda a: normed.at[a // per, pl.ds(pl.multiple_of((a % per) * shard_rows, shard_rows), shard_rows)],
    )
    late_moves = [net.move(att_in, att), net.move(q_in, qv), net.move(lse_in, lsev)]
    net.wait(wd_moves)
    net.wait(slope_moves)
    wide = 512

    def d_pre(lo, hi):
        @pl.loop(lo, hi)
        def _(j):
            lanes = pl.ds(pl.multiple_of(j * wide, wide), wide)
            value = dot(dm[...], wa[lanes, :], NT) * ad[1, :, lanes].astype(F32)
            value = value.astype(BF)
            ad[1, :, lanes] = value
            ub[j] = col_sum(value)

    def full(row):
        return jnp.concatenate([small_in[s, row : row + 1] for s in range(shards)], axis=1).astype(F32)

    n_wide = hidden // wide
    d_pre(0, n_wide // 4)
    pump()
    grad_down(1)
    d_pre(n_wide // 4, n_wide)
    pump()
    grad_down(2)
    net.wait(wu_moves)
    net.wait(nm_moves)
    down_bias = full(7)
    gain = full(5)
    gain_terms, shift_terms = None, None
    for slot in range(slots):
        rows = span(slot)
        value = res[rows] + dot(ad[0, rows], wa[...]) + down_bias
        xv[slot] = (value * live_in[slot]).astype(BF)
        incoming = jnp.concatenate([dot(ad[1, rows], wb[i], NT) for i in range(2)], axis=1)
        back, terms = norm_back(res[rows], gain, incoming)
        back = back + dm[rows].astype(F32)
        res[rows] = back
        dbr[rows] = back.astype(BF)
        terms, shifts = col_sum(terms), col_sum(incoming)
        gain_terms = terms if slot == 0 else gain_terms + terms
        shift_terms = shifts if slot == 0 else shift_terms + shifts
        if slot == 0:
            pump()
            grad_down(3)
    layer_moves = [net.move(xv, layer_out)]
    kv_moves = [net.move(kv_in, wa)]
    sg[5:6] = gain_terms
    sg[6:7] = shift_terms
    sg[4:5] = col_sum(dbr[...])
    sg[7:8] = col_sum(dm[...])
    net.wait(wo_moves)
    for i in range(2):
        dm[:, i * half_rows : (i + 1) * half_rows] = dot(dbr[...], normed[i], NT).astype(BF)
    normed_moves = [net.move(normed_in, normed)]
    pl.semaphore_signal(act_free, inc=1, device_id=place.to_c, device_id_type=MESH)

    def up_pairs(j):
        return [(nm, lambda i: ad[1, :, lanes_at(j * width + i * 2 * block, 2 * block)])]

    pump()
    grad_cols(up_pairs(0), gu, 0)
    net.wait(layer_moves)
    late_moves.append(net.move(x_in, xv))
    net.wait(late_moves)
    net.wait(kv_moves)
    scale = HEAD_DIM**-0.5

    def attend(slot, lo, hi):
        masks = head_masks(length)

        @pl.loop(lo, hi)
        def _(p):
            lanes = pl.ds(pl.multiple_of(p * PAIR, PAIR), PAIR)
            rows = span(slot)
            keys = wa[pl.ds(slot * 2 * clip, clip), lanes]
            values = wa[pl.ds((slot * 2 + 1) * clip, clip), lanes]
            queries = qv[rows, lanes] * BF(scale)
            d_out = dm[rows, lanes]
            along = (att[rows, lanes].astype(F32) * d_out.astype(F32)).T
            logs = lsev[slot, p]
            d_k, d_v, d_q = None, None, []
            for h in range(2):
                half = slice(h * HEAD_DIM, (h + 1) * HEAD_DIM)
                q_h, d_h = queries * masks[h], d_out * masks[h]
                probs = jnp.exp(dot(keys, q_h, NT) - logs[:, h * length : (h + 1) * length])
                mean = jnp.sum(along[half], axis=0, keepdims=True)
                d_scores = (probs * (dot(values, d_h, NT) - mean)).astype(BF)
                term_v = dot(probs.astype(BF), d_h)
                term_k = dot(d_scores, q_h)
                d_v = term_v if h == 0 else d_v + term_v
                d_k = term_k if h == 0 else d_k + term_k
                d_q.append(dot(keys, d_scores, TN)[half])
            qv[rows, lanes] = (jnp.concatenate(d_q, axis=0).T * scale).astype(BF)
            for part, value in ((0, d_k), (1, d_v)):
                value = value.astype(BF)
                for yy in range(2):
                    to = pl.ds(pl.multiple_of((yy * 2 + part) * width + p * PAIR, PAIR), PAIR)
                    for cc in range(2):
                        at = (yy * 2 + cc) * length
                        wb[cc, rows, to] = value[at : at + length]

    pairs = width // PAIR

    def share(slot):
        if slot == 0:
            pl.semaphore_wait(act_free, 1)
        return net.send(wb.at[1 - c, span(slot)], ad.at[0, span(slot)], place.to_c)

    attend(0, 0, pairs // 2)
    pump()
    grad_cols(up_pairs(1), gu, width)
    attend(0, pairs // 2, pairs)
    shares = [share(0)]
    pump()
    grad_cols(up_pairs(2), gu, 2 * width)
    attend(1, 0, pairs // 2)
    pump()
    grad_cols(up_pairs(3), gu, 3 * width)
    attend(1, pairs // 2, pairs)
    shares.append(share(1))
    wq_moves = []
    for part in (1, 2, 0):
        wq_moves.append(
            blocks_of(
                wq_in.at[:, pl.ds(part * width, width)], [wq_all.at[part]],
                lambda a: wa.at[pl.ds(pl.multiple_of(part * width + a * shard_rows, shard_rows), shard_rows)],
            )
        )
    pump()
    grad_cols([(att, lambda i: dbr[:, lanes_at(i * 2 * block, 2 * block)])], go, 0)
    sg[2:3] = col_sum(qv[...])

    for slot in range(slots):
        shares[slot].wait_recv()

        @pl.loop(0, 2 * 2)
        def _(i):
            lanes = pl.ds(pl.multiple_of(i * width, width), width)
            wb[c, span(slot), lanes] = wb[c, span(slot), lanes] + ad[0, span(slot), lanes]

    def d_part(part, which, lanes_from=0, n=None):
        side = y if which == 0 else 1 - y
        n = width if n is None else n
        return wb[c, :, lanes_at((side * 2 + part) * width + lanes_from, n)]

    net.wait(wq_moves[0])
    net.wait(wq_moves[1])
    back = dot(d_part(0, 1), wa[pl.ds(width, width)], NT) + dot(d_part(1, 1), wa[pl.ds(2 * width, width)], NT)
    dm[...] = back.astype(BF)
    back_sends = [net.send(dm.at[span(slot)], dn.at[slot], place.to_y) for slot in range(slots)]
    pump()
    net.wait(normed_moves)
    grad_cols([(normed.at[0], lambda i: qv[:, lanes_at(i * 2 * block, 2 * block)])], gq, 0)
    sg[3:4] = col_sum(d_part(1, 0)) + col_sum(d_part(1, 1))
    pump()

    def kv_pairs(part):
        return [
            (normed.at[which], lambda i, which=which: d_part(part, which, i * 2 * block, 2 * block)) for which in range(2)
        ]

    grad_cols(kv_pairs(0), gq, width)
    pump()
    grad_cols(kv_pairs(1), gq, 2 * width)
    pump()
    net.wait(wq_moves[2])
    gain = full(0)
    for slot in range(slots):
        rows = span(slot)
        incoming = dot(qv[rows], wa[pl.ds(0, width)], NT)
        side = [wb[c, rows, lanes_at((y * 2 + part) * width, width)] for part in range(2)]
        incoming = incoming + dot(side[0], wa[pl.ds(width, width)], NT)
        incoming = incoming + dot(side[1], wa[pl.ds(2 * width, width)], NT)
        back_sends[slot].wait_recv()
        incoming = incoming + dn[slot].astype(F32)
        back, terms = norm_back(xv[slot].astype(F32), gain, incoming)
        xv[slot] = (res[rows] + back).astype(BF)
        terms, shifts = col_sum(terms), col_sum(incoming)
        gain_terms = terms if slot == 0 else gain_terms + terms
        shift_terms = shifts if slot == 0 else shift_terms + shifts
        if slot == 0:
            pump()
    out_moves = [net.move(xv, input_out)]
    sg[0:1] = gain_terms
    sg[1:2] = shift_terms
    per_row = width // wide
    for j in range(n_wide):
        sg[8 + j // per_row : 9 + j // per_row, (j % per_row) * wide : (j % per_row + 1) * wide] = ub[j]
    sg[12:16] = jnp.zeros((4, width), F32)

    sums = [net.send(sg, sr.at[0], place.to_c)]
    pump()
    sums[0].wait_recv()
    sr[4] = sg[...] + sr[0]
    sums.append(net.send(sr.at[4], sr.at[1], place.to_y))
    pump()
    sums[1].wait_recv()
    sr[5] = sr[4] + sr[1]
    sums += [net.send(sr.at[5], sr.at[7 + shift], place.to_z(shift)) for shift in range(1, shards)]
    pump()
    for copy in sums[2:]:
        copy.wait_recv()
    total = sr[5]
    for shift in range(1, shards):
        total = total + sr[7 + shift]
    sr[6] = total
    sums.append(net.send(sr.at[6], sr.at[2], place.to_x))
    pump()
    sums[-1].wait_recv()
    sr[3] = sr[6] + sr[2]
    out_moves.append(net.move(sr.at[3], sg_out))
    while any(st["stage"] < len(stages) for st in flights):
        pump()
    for _ in range(RING_A):
        pl.semaphore_wait(free_sems.at[0], 1)
    out_moves += [net.move(a, b) for a, b in ((gq, gq_out), (go, go_out), (gu, gu_out), (gd, gd_out))]
    finish(net, flights)


def finish(net, flights):
    done = set()
    for st in flights:
        for name, value in st.items():
            if name in ("s0", "s1", "sa", "sb", "s2", "s4"):
                done.update(id(copy) for copy in (value if isinstance(value, list) else [value]))
    for copy in net.remote:
        if id(copy) not in done:
            copy.wait_send()
    net.wait(net.local)


def backward(shards, x, cot, live, small, weights, gathered, kept):
    slots, length, width = x.shape
    tokens = slots * length
    hidden = weights[2].shape[1]
    down_rows = weights[3].shape[0]
    pairs = width // PAIR
    owned = weights[0].shape[0] // 4
    any_ = pl.BlockSpec(memory_space=pl.ANY)
    vmem = pl.BlockSpec(memory_space=pltpu.VMEM)
    sd = jax.ShapeDtypeStruct
    outs = (
        sd((slots, length, width), BF), sd((slots, length, width), BF), sd((owned, 3 * width), BF), sd((owned, width), BF),
        sd((owned, hidden), BF), sd((down_rows // 4, width), BF), sd((16, width), F32),
    )
    tile = (64, 256)
    return pl.pallas_call(
        functools.partial(backward_kernel, shards),
        out_shape=outs,
        in_specs=[any_] * 2 + [vmem] * 2 + [any_] * 17,
        out_specs=(any_,) * len(outs),
        scratch_shapes=[
            pltpu.VMEM((hidden, width), BF),
            pltpu.VMEM((2, width // 2, hidden), BF),
            pltpu.VMEM((2, tokens, hidden), BF),
            pltpu.VMEM((tokens, width), BF),
            pltpu.VMEM((tokens, width), BF),
            pltpu.VMEM((tokens, width), F32),
            pltpu.VMEM((tokens, width), BF),
            pltpu.VMEM((tokens, width), BF),
            pltpu.VMEM((tokens, width), BF),
            pltpu.VMEM((2, tokens, width), BF),
            pltpu.VMEM((slots, length, width), BF),
            pltpu.VMEM((slots, length, width), BF),
            pltpu.VMEM((slots, pairs, 1, 2 * length), F32),
            pltpu.VMEM((owned, 3 * width), BF),
            pltpu.VMEM((owned, width), BF),
            pltpu.VMEM((owned, hidden), BF),
            pltpu.VMEM((down_rows // 4, width), BF),
            pltpu.VMEM((16, width), F32),
            pltpu.VMEM((hidden // 512, 1, 512), F32),
            pltpu.VMEM((7 + shards, 16, width), F32),
            pltpu.VMEM((RING_A, 2, 4, 2, shards) + tile, BF),
            pltpu.VMEM((RING_A, 4, 2, shards) + tile, BF),
            pltpu.VMEM((RING_B, 2, 2, shards) + tile, BF),
            pltpu.VMEM((N_CHUNKS, 2, 4) + tile, BF),
            pltpu.VMEM((N_CHUNKS, 4) + tile, BF),
            pltpu.VMEM((N_CHUNKS, 2) + tile, BF),
            pltpu.VMEM((N_CHUNKS, 2) + tile, BF),
            pltpu.VMEM((RING_B, 2, 2, 4) + tile, BF),
            pltpu.VMEM((RING_B, 2, 4) + tile, BF),
            pltpu.VMEM((RING_B, 4) + tile, BF),
            pltpu.VMEM((RING_B, 2) + tile, BF),
            pltpu.SemaphoreType.DMA((N_REMOTE2,)),
            pltpu.SemaphoreType.DMA((N_REMOTE2,)),
            pltpu.SemaphoreType.DMA((N_LOCAL2,)),
            pltpu.SemaphoreType.REGULAR((4,)),
            pltpu.SemaphoreType.REGULAR,
        ],
        compiler_params=pltpu.CompilerParams(collective_id=2, has_side_effects=True, vmem_limit_bytes=63 * MIB),
    )(x, cot, live, small, *weights, *gathered, *kept)


def place_kernel(n, *refs):
    srcs, dsts = refs[: n + 1], refs[n + 1 : 2 * n + 3]
    small, bufs, wide, sems = refs[2 * n + 3], refs[2 * n + 4 : 3 * n + 4], refs[3 * n + 4 : -1], refs[-1]
    loads = [pltpu.make_async_copy(src, buf, sems.at[i]) for i, (src, buf) in enumerate(zip(srcs, bufs + (small,)))]
    for copy in loads:
        copy.start()
    stores = []
    for i in range(n):
        loads[i].wait()
        buf = bufs[i]
        if i >= 2:
            buf = wide[i - 2]
            buf[...] = bufs[i][...].astype(F32)
        stores.append(pltpu.make_async_copy(buf, dsts[i], sems.at[n + 1 + i]))
        stores[-1].start()
    loads[n].wait()
    at = lax.axis_index("shard") * lax.axis_size("seq") + lax.axis_index("seq")
    vec_out, up_out = dsts[n:]
    pair = small[0:8, pl.ds(pl.multiple_of(at // 2 * 128, 128), 128)]
    vec_out[...] = jnp.where(at % 2 == 0, pair[:, :64], pair[:, 64:])
    up_out[...] = small[pl.ds(8 + at // 4, 1), pl.ds(pl.multiple_of(at % 4 * 256, 256), 256)]
    for copy in stores:
        copy.wait()


def place_results(sums, *arrays):
    any_, vmem = pl.BlockSpec(memory_space=pl.ANY), pl.BlockSpec(memory_space=pltpu.VMEM)
    n = len(arrays)
    outs = tuple(jax.ShapeDtypeStruct(a.shape, F32 if a.ndim == 2 else BF) for a in arrays)
    return pl.pallas_call(
        functools.partial(place_kernel, n),
        out_shape=outs + (jax.ShapeDtypeStruct((8, 64), F32), jax.ShapeDtypeStruct((1, 256), F32)),
        in_specs=[any_] * (n + 1),
        out_specs=(any_,) * n + (vmem, vmem),
        scratch_shapes=[pltpu.VMEM(sums.shape, F32)]
        + [pltpu.VMEM(a.shape, BF) for a in arrays]
        + [pltpu.VMEM(a.shape, F32) for a in arrays[2:]]
        + [pltpu.SemaphoreType.DMA((2 * n + 1,))],
        compiler_params=pltpu.CompilerParams(vmem_limit_bytes=60 * MIB),
    )(*arrays, sums)


def local(
    activations, cotangent, clip_loads, attn_gain, attn_shift, w_qkv, q_bias, v_bias, w_out, out_bias,
    mlp_gain, mlp_shift, w_up, up_bias, w_down, down_bias,
):
    shards = lax.axis_size("shard")
    x, cot = activations[0], cotangent[0]
    slots, length, width = x.shape
    rows = w_qkv.shape[0]
    vectors = [attn_gain, attn_shift, q_bias, v_bias, out_bias, mlp_gain, mlp_shift, down_bias]
    small = jnp.broadcast_to(up_bias.reshape(1, 4, rows), (4, 4, rows)).reshape(16, rows)
    row = lax.broadcasted_iota(jnp.int32, (16, rows), 0)
    for i, vector in enumerate(vectors):
        small = jnp.where(row == i, vector[None, :], small)
    weights = (w_qkv, w_out, w_up, w_down)
    *gathered, normed, q, kv, lse, att, res, nm, act, slope, small = forward(shards, x, small, *weights)
    live = (jnp.arange(slots) < clip_loads[0]).astype(F32)
    live = jnp.broadcast_to(live[:, None, None], (slots, 1, width))
    kept = (normed, q, kv.reshape(-1, width), lse, att, res, nm, act, slope)
    layer_out, input_grad, gq, go, gu, gd, sums = backward(shards, x, cot, live, small, weights, gathered, kept)
    pods = lax.axis_size("replica")
    if pods > 2:
        ends = [[p for p in range(pods) if p % 2 == side] for side in range(2)]
        gq, go, gu, gd, sums = (lax.psum(g, "replica", axis_index_groups=ends) for g in (gq, go, gu, gd, sums))
    layer_out, input_grad, gq, go, gu, gd, vec, up = place_results(sums, layer_out, input_grad, gq, go, gu, gd)
    return (
        layer_out[None], input_grad[None], vec[0], vec[1], gq, vec[2], vec[3], go, vec[4], vec[5], vec[6], gu, up[0], gd, vec[7],
    )


def solution(mesh):
    rows = P("shard")
    full = P("shard", None)
    clips = P(("replica", "shard"), None, "seq", None)
    vec = P(("shard", "seq"))
    mat = P(("shard", "seq"), None)
    return jax.shard_map(
        local,
        mesh=mesh,
        in_specs=(
            clips, clips, P(("replica", "shard")), rows, rows, full, rows, rows, full, rows, rows, rows, full, rows, full, rows,
        ),
        out_specs=(clips, clips, vec, vec, mat, vec, vec, mat, vec, vec, vec, mat, vec, mat, vec),
        check_vma=False,
    )
```

```python
import functools
import jax
import jax.numpy as jnp
from jax import lax
from jax.experimental import pallas as pl
from jax.experimental.pallas import tpu as pltpu
from jax.sharding import PartitionSpec as P

MESH = pl.DeviceIdType.MESH
BF = jnp.bfloat16
F32 = jnp.float32
HEAD_DIM = 64
PAIR = 2 * HEAD_DIM
EPSILON = 1e-06
NN = (((1,), (0,)), ((), ()))
NT = (((1,), (1,)), ((), ()))
TN = (((0,), (0,)), ((), ()))
MIB = 2**20


def dot(a, b, dims=NN):
    return lax.dot_general(a, b, dims, preferred_element_type=F32)


class Place:
    def __init__(self, shards):
        self.shards = shards
        r, self.z, q = (lax.axis_index(a) for a in ("replica", "shard", "seq"))
        self.x, self.y, self.c = r % 2, q // 2, q % 2
        self.q = q
        self.to_x = {"replica": r + 1 - 2 * self.x}
        self.to_y = {"seq": q + 2 - 4 * self.y}
        self.to_c = {"seq": q + 1 - 2 * self.c}

    def to_z(self, shift):
        return {"shard": (self.z + shift) % self.shards}

    def behind(self, shift):
        return (self.z + self.shards - shift) % self.shards

    def greet(self):
        barrier = pltpu.get_barrier_semaphore()
        peers = [self.to_x, self.to_y, self.to_c]
        peers += [self.to_z(shift) for shift in range(1, self.shards)]
        for peer in peers:
            pl.semaphore_signal(barrier, inc=1, device_id=peer, device_id_type=MESH)
        pl.semaphore_wait(barrier, len(peers))


class Copies:
    def __init__(self, send_sems, recv_sems, local_sems):
        self.send_sems, self.recv_sems, self.local_sems = send_sems, recv_sems, local_sems
        self.remote, self.local = [], []

    def send(self, src, dst, peer):
        at = len(self.remote)
        copy = pltpu.make_async_remote_copy(
            src_ref=src, dst_ref=dst, send_sem=self.send_sems.at[at], recv_sem=self.recv_sems.at[at],
            device_id=peer, device_id_type=MESH,
        )
        copy.start()
        self.remote.append(copy)
        return copy

    def move(self, src, dst):
        at = len(self.local)
        copy = pltpu.make_async_copy(src, dst, self.local_sems.at[at])
        copy.start()
        self.local.append([copy, False])
        return self.local[-1]

    def wait(self, moves):
        for entry in moves:
            if not entry[1]:
                entry[0].wait()
                entry[1] = True

    def finish(self):
        for copy in self.remote:
            copy.wait_send()
        self.wait(self.local)


def normalized(values, gain, shift):
    center = values - jnp.mean(values, axis=-1, keepdims=True)
    spread = jnp.mean(center * center, axis=-1, keepdims=True)
    return center * lax.rsqrt(spread + EPSILON) * gain + shift


def head_masks(rows):
    lane = lax.broadcasted_iota(jnp.int32, (rows, PAIR), 1)
    first = (lane < HEAD_DIM).astype(F32).astype(BF)
    return first, (lane >= HEAD_DIM).astype(F32).astype(BF)


def both_heads(values, masks):
    return jnp.concatenate([values * masks[0], values * masks[1]], axis=0)


N_REMOTE1, N_LOCAL1 = 176, 80
AHEAD = 2
IN_HALVES = (3, 5, 7)


def forward_kernel(
    shards,
    x_in, small_in, wq_in, wo_in, wu_in, wd_in,
    wq_all, wo_all, wu_all, wd_all,
    normed_out, q_out, kv_out, lse_out, att_out, res_out, nm_out, act_out, slope_out, small_out,
    xv, smv, normed, qv, kvb, lsev, att, res, nm, act, slope, wq, wo, wu,
    send_sems, recv_sems, local_sems,
):
    place = Place(shards)
    net = Copies(send_sems, recv_sems, local_sems)
    x, y, z, c = place.x, place.y, place.z, place.c
    slots, length, width = x_in.shape
    tokens = slots * length
    hidden = wu_in.shape[1]
    shard_rows = wq_in.shape[0]
    place.greet()

    small_moves = [net.move(small_in, smv.at[z])]
    small_sends = [net.send(small_in, smv.at[z], place.to_z(s)) for s in range(1, shards)]
    x_moves = [net.move(x_in, xv.at[0])]
    x_sends = [net.send(x_in.at[0], xv.at[1, 0], place.to_y)]

    chunks = [(wq_in, wq_all.at[part], part * width, 0, False) for part in (1, 2, 0)]
    chunks.append((wo_in, wo_all.at[0], 0, 0, False))
    chunks += [(wu_in, wu_all.at[j], j * width, 0, False) for j in range(hidden // width)]
    chunks += [(wd_in, wd_all.at[j], 0, j * shard_rows, True) for j in range(wd_in.shape[0] // shard_rows)]
    chunks = [chunk[:4] + (chunk[4] or i in IN_HALVES,) for i, chunk in enumerate(chunks)]
    state = [dict() for _ in chunks]
    others = pl.ds(1, shards - 1)
    eighth, quarter = shard_rows // 8, shard_rows // 4
    near, far = {"shard": z + 1 - 2 * (z % 2)}, {"shard": z + 2 - 4 * (z // 2)}
    at_near = 1 + 2 * (z % 2)

    def region(i, px, py, pc, side=None, first=0):
        if chunks[i][4]:
            piece = ((px + py) % 2 * 2 + pc) * quarter
            at, n = {None: (0, quarter), "x": (0, eighth), "y": (eighth, eighth)}[side]
        else:
            piece = ((px * 2 + py) * 2 + pc) * eighth
            at, n = {None: (0, eighth), "y": (0, eighth // 2), "x": (eighth // 2, eighth // 2)}[side]
        return pl.ds(pl.multiple_of(first + piece + at, 16), n)

    def start_z(i):
        src, all_, col, row, _ = chunks[i]
        rows = region(i, x, y, c)
        src = src.at[region(i, x, y, c, None, row), pl.ds(col, width)]
        state[i]["far"] = net.send(src, all_.at[2, rows], far)
        state[i]["near"] = net.send(src, all_.at[at_near, rows], near)

    def relay(i):
        all_ = chunks[i][1]
        rows = region(i, x, y, c)
        state[i]["far"].wait_recv()
        state[i]["relay"] = net.send(all_.at[2, rows], all_.at[4 - at_near, rows], near)
        if i + AHEAD < len(chunks):
            start_z(i + AHEAD)

    def pass_piece(i, px, py, pc, peer, side=None):
        ref = chunks[i][1].at[others, region(i, px, py, pc, side)]
        return net.send(ref, ref, peer)

    def plane_one(i):
        st = state[i]
        st["near"].wait_recv()
        st["relay"].wait_recv()
        halves = chunks[i][4]
        st["x"] = pass_piece(i, x, y, c, place.to_x, "x" if halves else None)
        st["y"] = pass_piece(i, x, y, c, place.to_y, "y" if halves else None)
        st["core"] = [pass_piece(i, x, y, c, place.to_c)]

    def plane_two(i):
        st = state[i]
        halves = chunks[i][4]
        st["y"].wait_recv()
        if not halves:
            st["yx"] = pass_piece(i, x, 1 - y, c, place.to_x, "x")
        st["core"].append(pass_piece(i, x, 1 - y, c, place.to_c, "y" if halves else None))
        st["x"].wait_recv()
        if not halves:
            st["xy"] = pass_piece(i, 1 - x, y, c, place.to_y, "y")
        st["core"].append(pass_piece(i, 1 - x, y, c, place.to_c, "x" if halves else None))

    def plane_three(i):
        st = state[i]
        if chunks[i][4]:
            return
        for name, side in (("yx", "x"), ("xy", "y")):
            st[name].wait_recv()
            st["core"].append(pass_piece(i, 1 - x, 1 - y, c, place.to_c, side))

    def arrived(i):
        for copy in state[i]["core"]:
            copy.wait_recv()

    def load(i, dst):
        src, all_, col, *_ = chunks[i]
        moves = []
        for s in range(shards):
            rows = pl.ds(pl.multiple_of(place.behind(s) * shard_rows, shard_rows), shard_rows)
            cs = pl.ds(col, width)
            from_ = src.at[:, cs] if s == 0 else all_.at[s]
            moves.append(net.move(from_, dst.at[rows, cs]))
        return moves

    for i in range(AHEAD):
        start_z(i)

    net.wait(small_moves)
    for copy in small_sends:
        copy.wait_recv()
    small_moves = [net.move(smv, small_out)]

    def small(row, count=1):
        return jnp.concatenate([smv[s] for s in range(shards)], axis=1)[row : row + count].astype(F32)

    def norm_first(which, slot):
        rows = pl.ds(slot * length, length)
        normed[which, rows, :] = normalized(xv[which, slot].astype(F32), small(0), small(1)).astype(BF)

    loads = {}

    def step(i):
        if i + 4 < len(chunks):
            relay(i + 4)
        if i + 2 < len(chunks):
            plane_one(i + 2)
        if 0 <= i + 1 < len(chunks):
            plane_two(i + 1)
        if 0 <= i < len(chunks):
            plane_three(i)
        if 0 <= i - 1:
            arrived(i - 1)
            if i - 1 < len(targets):
                loads[i - 1] = load(i - 1, targets[i - 1])

    targets = [wq] * 3 + [wo] + [wu] * (hidden // width)

    net.wait(x_moves)
    norm_first(0, 0)
    relay(0)
    relay(1)
    step(-2)
    x_sends.append(net.send(x_in.at[1], xv.at[1, 1], place.to_y))
    norm_first(0, 1)
    step(-1)
    x_sends[0].wait_recv()
    norm_first(1, 0)
    step(0)
    x_sends[1].wait_recv()
    norm_first(1, 1)
    moves_out = [net.move(normed, normed_out)]
    step(1)
    v_bias = small(3)

    def project_kv(which, part):
        lanes = pl.ds((part + 1) * width, width)
        rows = normed[which]
        out = dot(rows, wq[:, lanes])
        if part:
            out = out + v_bias
        out = out.astype(BF)
        at = (y if which == 0 else 1 - y) * 2 + c
        for slot in range(slots):
            kvb[slot, part, at] = out[slot * length : (slot + 1) * length]

    shares = []

    def share(part):
        for which in range(2):
            at = (y if which == 0 else 1 - y) * 2 + c
            ref = kvb.at[:, part, at]
            shares.append(net.send(ref, ref, place.to_c))

    net.wait(loads[0])
    project_kv(0, 0)
    project_kv(1, 0)
    share(0)
    step(2)
    net.wait(loads[1])
    project_kv(0, 1)
    project_kv(1, 1)
    share(1)
    step(3)
    net.wait(loads[2])
    qv[...] = (dot(normed[0], wq[:, :width]) + small(2)).astype(BF)
    moves_out.append(net.move(qv, q_out))
    for copy in shares:
        copy.wait_recv()
    moves_out.append(net.move(kvb, kv_out))

    def attend(slot, lo, hi):
        masks = head_masks(length)

        @pl.loop(lo, hi)
        def _(p):
            lanes = pl.ds(pl.multiple_of(p * PAIR, PAIR), PAIR)
            rows = pl.ds(slot * length, length)
            queries = both_heads(qv[rows, lanes] * BF(HEAD_DIM**-0.5), masks)
            keys = kvb[slot, 0, :, :, lanes].reshape(-1, PAIR)
            values = kvb[slot, 1, :, :, lanes].reshape(-1, PAIR)
            scores = dot(keys, queries, NT)
            top = jnp.max(scores, axis=0, keepdims=True)
            terms = jnp.exp(scores - top)
            total = jnp.sum(terms, axis=0, keepdims=True)
            lsev[slot, p] = top + jnp.log(total)
            out = dot(values, terms.astype(BF), TN) * (1.0 / total)
            out = jnp.concatenate([out[:HEAD_DIM, :length], out[HEAD_DIM:, length:]], axis=0)
            att[rows, lanes] = out.T.astype(BF)

    pairs = width // PAIR
    attend(0, 0, pairs // 2)
    step(4)
    attend(0, pairs // 2, pairs)
    step(5)
    attend(1, 0, pairs // 2)
    step(6)
    attend(1, pairs // 2, pairs)
    moves_out += [net.move(lsev, lse_out), net.move(att, att_out)]
    step(7)
    net.wait(loads[3])
    out_bias, mlp_gain, mlp_shift = small(4), small(5), small(6)
    for slot in range(slots):
        rows = pl.ds(slot * length, length)
        value = xv[0, slot].astype(F32) + dot(att[rows], wo[...]) + out_bias
        res[rows] = value
        nm[rows] = normalized(value, mlp_gain, mlp_shift).astype(BF)
    moves_out += [net.move(res, res_out), net.move(nm, nm_out)]

    up_block = 512

    def up(part):
        @pl.loop(part * (width // up_block), (part + 1) * (width // up_block))
        def _(j):
            lanes = pl.ds(pl.multiple_of(j * up_block, up_block), up_block)
            s, inner = j // (wd_in.shape[0] // up_block), j % (wd_in.shape[0] // up_block)
            first = 8 + inner * (up_block // shard_rows)
            sm = smv[s].astype(F32)
            row = jnp.concatenate([sm[8:9], sm[9:10]], axis=1)
            row2 = jnp.concatenate([sm[10:11], sm[11:12]], axis=1)
            bias = jnp.where(inner == 0, row, row2)
            pre = dot(nm[...], wu[:, lanes]) + bias
            phi = 0.5 + 0.5 * lax.erf(pre * (0.5**0.5))
            density = jnp.exp(pre * pre * -0.5) * 0.3989422804014327
            act[:, lanes] = (pre * phi).astype(BF)
            slope[:, lanes] = (phi + pre * density).astype(BF)

    for j in range(hidden // width):
        if 4 + j not in loads:
            step(5 + j)
        net.wait(loads[4 + j])
        up(j)
        if j % 2:
            lanes = pl.ds((j - 1) * width, 2 * width)
            moves_out += [net.move(act.at[:, lanes], act_out.at[:, lanes]), net.move(slope.at[:, lanes], slope_out.at[:, lanes])]
    for i in range(9, len(chunks) + 1):
        step(i)
    net.finish()


def forward(shards, x, small, wq, wo, wu, wd):
    slots, length, width = x.shape
    tokens = slots * length
    hidden = wu.shape[1]
    pairs = width // PAIR
    any_ = pl.BlockSpec(memory_space=pl.ANY)
    sd = jax.ShapeDtypeStruct
    square = (shards, wq.shape[0], width)
    outs = (
        sd((3,) + square, BF), sd((1,) + square, BF), sd((hidden // width,) + square, BF), sd((wd.shape[0] // wq.shape[0],) + square, BF),
        sd((2, tokens, width), BF), sd((tokens, width), BF), sd((slots, 2, 4, length, width), BF),
        sd((slots, pairs, 1, 2 * length), F32), sd((tokens, width), BF), sd((tokens, width), F32),
        sd((tokens, width), BF), sd((tokens, hidden), BF), sd((tokens, hidden), BF), sd((shards,) + small.shape, BF),
    )
    return pl.pallas_call(
        functools.partial(forward_kernel, shards),
        out_shape=outs,
        in_specs=[any_] * 6,
        out_specs=(any_,) * len(outs),
        scratch_shapes=[
            pltpu.VMEM((2, slots, length, width), BF),
            pltpu.VMEM((shards,) + small.shape, BF),
            pltpu.VMEM((2, tokens, width), BF),
            pltpu.VMEM((tokens, width), BF),
            pltpu.VMEM((slots, 2, 4, length, width), BF),
            pltpu.VMEM((slots, pairs, 1, 2 * length), F32),
            pltpu.VMEM((tokens, width), BF),
            pltpu.VMEM((tokens, width), F32),
            pltpu.VMEM((tokens, width), BF),
            pltpu.VMEM((tokens, hidden), BF),
            pltpu.VMEM((tokens, hidden), BF),
            pltpu.VMEM((width, 3 * width), BF),
            pltpu.VMEM((width, width), BF),
            pltpu.VMEM((width, hidden), BF),
            pltpu.SemaphoreType.DMA((N_REMOTE1,)),
            pltpu.SemaphoreType.DMA((N_REMOTE1,)),
            pltpu.SemaphoreType.DMA((N_LOCAL1,)),
        ],
        compiler_params=pltpu.CompilerParams(collective_id=1, has_side_effects=True, vmem_limit_bytes=62 * MIB),
    )(x, small, wq, wo, wu, wd)


N_REMOTE2, N_LOCAL2 = 160, 80
RING_A, RING_B, N_CHUNKS = 3, 3, 12
X_ONLY = (8, 9)
IN_PARTS = (11,)


def norm_back(values, gain, incoming):
    center = values - jnp.mean(values, axis=-1, keepdims=True)
    spread = jnp.mean(center * center, axis=-1, keepdims=True)
    r = lax.rsqrt(spread + EPSILON)
    xhat = center * r
    e = incoming * gain
    back = r * (e - jnp.mean(e, axis=-1, keepdims=True) - xhat * jnp.mean(e * xhat, axis=-1, keepdims=True))
    return back, incoming * xhat


def col_sum(values):
    return jnp.sum(values.astype(F32), axis=0, keepdims=True)


def backward_kernel(
    shards,
    x_in, cot_in, small_in, wq_in, wo_in, wu_in, wd_in, wq_all, wo_all, wu_all, wd_all,
    normed_in, q_in, kv_in, lse_in, att_in, res_in, nm_in, act_in, slope_in,
    layer_out, input_out, gq_out, go_out, gu_out, gd_out, sg_out,
    wa, wb, ad, nm, att, res, dm, dbr, qv, normed, xv, dn, lsev,
    gq, go, gu, gd, sg, ub, sr,
    gbuf, r0, r1, ra, rb, r2, r4, fbuf, gb, tsum, tbuf,
    send_sems, recv_sems, local_sems, free_sems, act_free,
):
    place = Place(shards)
    net = Copies(send_sems, recv_sems, local_sems)
    x, y, z, c = place.x, place.y, place.z, place.c
    slots, length, width = x_in.shape
    tokens = slots * length
    hidden = wu_in.shape[1]
    shard_rows = wq_in.shape[0]
    down_rows = wd_in.shape[0]
    block = 256
    clip = 4 * length

    def span(slot):
        return pl.ds(slot * length, length)

    cot_moves = [net.move(cot_in.at[slot], dm.at[span(slot)]) for slot in range(slots)]
    act_moves = [net.move(act_in, ad.at[0])]

    def blocks_of(own, gathered, dst_of):
        moves = []
        for s in range(shards):
            dst = dst_of(place.behind(s))
            if s == 0:
                moves.append(net.move(own, dst))
                continue
            for j, square in enumerate(gathered):
                at = (pl.ds(j * shard_rows, shard_rows),) if own.shape[0] > shard_rows else (slice(None), pl.ds(j * width, width))
                moves.append(net.move(square.at[s], dst.at[at]))
        return moves

    wd_moves = blocks_of(
        wd_in, [wd_all.at[j] for j in range(down_rows // shard_rows)],
        lambda a: wa.at[pl.ds(pl.multiple_of(a * down_rows, down_rows), down_rows)],
    )
    place.greet()

    def live(slot):
        return jnp.concatenate([small_in[z, 12 + slot : 13 + slot]] * shards, axis=1)

    net.wait(cot_moves)
    for slot in range(slots):
        dm[span(slot)] = dm[span(slot)] * live(slot)
    net.wait(act_moves)

    flights = []

    def first_peer(k, p):
        return place.to_x if p or k in X_ONLY else place.to_y

    def credit(k, p):
        return free_sems.at[2 if p else 3 if k in X_ONLY else 1]

    def advance_zero(st):
        k, rows = st["k"], st["rows"]
        a, b = k % RING_A, k % RING_B
        st["s0"].wait_recv()

        @pl.loop(0, 4)
        def _(i):
            gbuf[a, c, i, :, :, rows, :] = gbuf[a, c, i, :, :, rows, :] + r0[a, i, :, :, rows, :]

        if st["last"]:
            pl.semaphore_signal(free_sems.at[0], inc=1, device_id=place.to_c, device_id_type=MESH)
        st["s1"] = []
        for p in range(2):
            if k >= RING_B and st["first"]:
                pl.semaphore_wait(credit(k, p), 1)
            peer = first_peer(k, p)
            if peer is place.to_x:
                src = gbuf.at[a, c, 2 * p + 1 - x, :, :, rows, :]
            else:
                src = gbuf.at[a, c, pl.ds(2 * p, 2), 1 - y, :, rows, :]
            st["s1"].append(net.send(src, r1.at[b, p, :, :, rows, :], peer))

    def advance_one(st):
        k, rows = st["k"], st["rows"]
        a, b = k % RING_A, k % RING_B
        for p in range(2):
            st["s1"][p].wait_recv()
            for i in range(2):
                if first_peer(k, p) is place.to_x:
                    kept = gbuf[a, c, 2 * p + x, i, :, rows, :]
                else:
                    kept = gbuf[a, c, 2 * p + i, y, :, rows, :]
                value = kept + r1[b, p, i, :, rows, :]
                for zz in range(shards):
                    fbuf[b, zz % 2, zz // 2, 2 * p + i, rows, :] = value[zz]
            if k + RING_B < N_CHUNKS:
                peer = first_peer(k + RING_B, p)
                pl.semaphore_signal(credit(k + RING_B, p), inc=1, device_id=peer, device_id_type=MESH)
        near = {"shard": z + 1 - 2 * (z % 2)}
        st["sa"] = net.send(fbuf.at[b, 1 - z % 2, :, :, rows, :], ra.at[k, :, :, rows, :], near)
        for copy in [st["s0"]] + st["s1"]:
            copy.wait_send()

    def advance_two(st):
        k, rows = st["k"], st["rows"]
        b = k % RING_B
        st["sa"].wait_recv()
        for i in range(2):
            gb[b, i, :, rows, :] = fbuf[b, z % 2, i, :, rows, :] + ra[k, i, :, rows, :]
        far = {"shard": z + 2 - 4 * (z // 2)}
        st["sb"] = net.send(gb.at[b, 1 - z // 2, :, rows, :], rb.at[k, :, rows, :], far)
        st["sa"].wait_send()

    def advance_three(st):
        k, rows = st["k"], st["rows"]
        b = k % RING_B
        st["sb"].wait_recv()
        tsum[b, :, rows, :] = gb[b, z // 2, :, rows, :] + rb[k, :, rows, :]
        st["s2"] = []
        for p in range(2):
            over_y = first_peer(k, p) is place.to_x
            src = tsum.at[b, 2 * p + 1 - (y if over_y else x), rows, :]
            st["s2"].append(net.send(src, r2.at[k, p, rows, :], place.to_y if over_y else place.to_x))
        st["sb"].wait_send()

    def advance_four(st):
        k, rows = st["k"], st["rows"]
        b = k % RING_B
        for p in range(2):
            st["s2"][p].wait_recv()
            at = y if first_peer(k, p) is place.to_x else x
            tbuf[b, p, rows, :] = tsum[b, 2 * p + at, rows, :] + r2[k, p, rows, :]
        st["s4"] = net.send(tbuf.at[b, :, rows, :], r4.at[k, :, rows, :], place.to_x)
        for copy in st["s2"]:
            copy.wait_send()

    def advance_five(st):
        k, rows = st["k"], st["rows"]
        b = k % RING_B
        st["s4"].wait_recv()
        out, kind, col = st["out"]
        for source, slot, at in ((tbuf, b, x), (r4, k, 1 - x)):
            for p in range(2):
                value = source[slot, p, rows, :]
                if kind == "cols":
                    out[rows, pl.ds(pl.multiple_of(col + p * 2 * block + at * block, block), block)] = value
                else:
                    out[pl.ds(pl.multiple_of((p * 2 + at) * 64 + rows.start, 16), rows.size), pl.ds(col, block)] = value
        st["s4"].wait_send()

    stages = (advance_zero, advance_one, advance_two, advance_three, advance_four, advance_five)

    def pump():
        for st in reversed(flights):
            if st["stage"] < len(stages):
                stages[st["stage"]](st)
                st["stage"] += 1

    def next_chunk():
        return flights[-1]["k"] + 1 if flights else 0

    def launch(out, kind, col):
        k = next_chunk()
        a = k % RING_A
        if k >= RING_A:
            pl.semaphore_wait(free_sems.at[0], 1)
        parts = 2 if k in IN_PARTS else 1
        made = []
        for part in range(parts):
            rows = pl.ds(part * (64 // parts), 64 // parts)
            st = {"k": k, "stage": 0, "rows": rows, "out": (out, kind, col)}
            st["first"], st["last"] = part == 0, part == parts - 1
            st["s0"] = net.send(gbuf.at[a, 1 - c, :, :, :, rows, :], r0.at[a, :, :, :, rows, :], place.to_c)
            made.append(st)
        flights.extend(reversed(made))

    def grad_cols(pairs, out, col):
        a = next_chunk() % RING_A

        @pl.loop(0, 2)
        def _(i):
            total = None
            for left, right in pairs:
                term = dot(left[...], right(i), TN)
                total = term if total is None else total + term
            for j in range(2):
                value = total[:, j * block : (j + 1) * block].astype(BF).reshape(shards, 2, 2, 64, block)
                for cc in range(2):
                    for yy in range(2):
                        gbuf[a, cc, i * 2 + j, yy] = value[:, yy, cc]

        launch(out, "cols", col)

    def grad_down(j):
        a = next_chunk() % RING_A
        right = dm[:, pl.ds(j * block, block)]

        @pl.loop(0, shards)
        def _(i):
            left = ad[0, :, pl.ds(pl.multiple_of(i * down_rows, down_rows), down_rows)]
            value = dot(left, right, TN).astype(BF).reshape(2, 2, 4, 64, block)
            for cc in range(2):
                for yy in range(2):
                    gbuf[a, cc, :, yy, i] = value[yy, cc]

        launch(gd, "rows", j * block)

    def lanes_at(start, n=block):
        return pl.ds(pl.multiple_of(start, block), n)

    slope_moves = [net.move(slope_in, ad.at[1])]
    grad_down(0)
    half_rows = width // 2
    per = half_rows // shard_rows
    wu_moves = blocks_of(
        wu_in, [wu_all.at[j] for j in range(hidden // width)],
        lambda a: wb.at[a // per, pl.ds(pl.multiple_of((a % per) * shard_rows, shard_rows), shard_rows)],
    )
    nm_moves = [net.move(res_in, res), net.move(nm_in, nm)]
    wo_moves = blocks_of(
        wo_in, [wo_all.at[0]],
        lambda a: normed.at[a // per, pl.ds(pl.multiple_of((a % per) * shard_rows, shard_rows), shard_rows)],
    )
    late_moves = [net.move(att_in, att), net.move(q_in, qv), net.move(lse_in, lsev)]
    net.wait(wd_moves)
    net.wait(slope_moves)
    wide = 512

    def d_pre(lo, hi):
        @pl.loop(lo, hi)
        def _(j):
            lanes = pl.ds(pl.multiple_of(j * wide, wide), wide)
            value = dot(dm[...], wa[lanes, :], NT) * ad[1, :, lanes].astype(F32)
            value = value.astype(BF)
            ad[1, :, lanes] = value
            ub[j] = col_sum(value)

    def full(row):
        return jnp.concatenate([small_in[s, row : row + 1] for s in range(shards)], axis=1).astype(F32)

    n_wide = hidden // wide
    d_pre(0, n_wide // 4)
    pump()
    grad_down(1)
    d_pre(n_wide // 4, n_wide)
    pump()
    grad_down(2)
    net.wait(wu_moves)
    net.wait(nm_moves)
    down_bias = full(7)
    gain = full(5)
    gain_terms, shift_terms = None, None
    for slot in range(slots):
        rows = span(slot)
        value = res[rows] + dot(ad[0, rows], wa[...]) + down_bias
        xv[slot] = (value * live(slot).astype(F32)).astype(BF)
        incoming = jnp.concatenate([dot(ad[1, rows], wb[i], NT) for i in range(2)], axis=1)
        back, terms = norm_back(res[rows], gain, incoming)
        back = back + dm[rows].astype(F32)
        res[rows] = back
        dbr[rows] = back.astype(BF)
        terms, shifts = col_sum(terms), col_sum(incoming)
        gain_terms = terms if slot == 0 else gain_terms + terms
        shift_terms = shifts if slot == 0 else shift_terms + shifts
        if slot == 0:
            pump()
            grad_down(3)
    layer_moves = [net.move(xv, layer_out)]
    kv_moves = [net.move(kv_in, wa)]
    sg[5:6] = gain_terms
    sg[6:7] = shift_terms
    sg[4:5] = col_sum(dbr[...])
    sg[7:8] = col_sum(dm[...])
    net.wait(wo_moves)
    for i in range(2):
        dm[:, i * half_rows : (i + 1) * half_rows] = dot(dbr[...], normed[i], NT).astype(BF)
    normed_moves = [net.move(normed_in, normed)]
    pl.semaphore_signal(act_free, inc=1, device_id=place.to_c, device_id_type=MESH)

    def up_pairs(j):
        return [(nm, lambda i: ad[1, :, lanes_at(j * width + i * 2 * block, 2 * block)])]

    pump()
    grad_cols(up_pairs(0), gu, 0)
    net.wait(layer_moves)
    late_moves.append(net.move(x_in, xv))
    net.wait(late_moves)
    net.wait(kv_moves)
    scale = HEAD_DIM**-0.5

    def attend(slot, lo, hi):
        masks = head_masks(length)

        @pl.loop(lo, hi)
        def _(p):
            lanes = pl.ds(pl.multiple_of(p * PAIR, PAIR), PAIR)
            rows = span(slot)
            keys = wa[pl.ds(slot * 2 * clip, clip), lanes]
            values = wa[pl.ds((slot * 2 + 1) * clip, clip), lanes]
            queries = qv[rows, lanes] * BF(scale)
            d_out = dm[rows, lanes]
            along = (att[rows, lanes].astype(F32) * d_out.astype(F32)).T
            logs = lsev[slot, p]
            d_k, d_v, d_q = None, None, []
            for h in range(2):
                half = slice(h * HEAD_DIM, (h + 1) * HEAD_DIM)
                q_h, d_h = queries * masks[h], d_out * masks[h]
                probs = jnp.exp(dot(keys, q_h, NT) - logs[:, h * length : (h + 1) * length])
                mean = jnp.sum(along[half], axis=0, keepdims=True)
                d_scores = (probs * (dot(values, d_h, NT) - mean)).astype(BF)
                term_v = dot(probs.astype(BF), d_h)
                term_k = dot(d_scores, q_h)
                d_v = term_v if h == 0 else d_v + term_v
                d_k = term_k if h == 0 else d_k + term_k
                d_q.append(dot(keys, d_scores, TN)[half])
            qv[rows, lanes] = (jnp.concatenate(d_q, axis=0).T * scale).astype(BF)
            for part, value in ((0, d_k), (1, d_v)):
                value = value.astype(BF)
                for yy in range(2):
                    to = pl.ds(pl.multiple_of((yy * 2 + part) * width + p * PAIR, PAIR), PAIR)
                    for cc in range(2):
                        at = (yy * 2 + cc) * length
                        wb[cc, rows, to] = value[at : at + length]

    pairs = width // PAIR

    def share(slot):
        if slot == 0:
            pl.semaphore_wait(act_free, 1)
        return net.send(wb.at[1 - c, span(slot)], ad.at[0, span(slot)], place.to_c)

    attend(0, 0, pairs // 2)
    pump()
    grad_cols(up_pairs(1), gu, width)
    attend(0, pairs // 2, pairs)
    shares = [share(0)]
    pump()
    grad_cols(up_pairs(2), gu, 2 * width)
    attend(1, 0, pairs // 2)
    pump()
    grad_cols(up_pairs(3), gu, 3 * width)
    attend(1, pairs // 2, pairs)
    shares.append(share(1))
    wq_moves = []
    for part in (1, 2, 0):
        wq_moves.append(
            blocks_of(
                wq_in.at[:, pl.ds(part * width, width)], [wq_all.at[part]],
                lambda a: wa.at[pl.ds(pl.multiple_of(part * width + a * shard_rows, shard_rows), shard_rows)],
            )
        )
    pump()
    grad_cols([(att, lambda i: dbr[:, lanes_at(i * 2 * block, 2 * block)])], go, 0)
    sg[2:3] = col_sum(qv[...])

    for slot in range(slots):
        shares[slot].wait_recv()

        @pl.loop(0, 2 * 2)
        def _(i):
            lanes = pl.ds(pl.multiple_of(i * width, width), width)
            wb[c, span(slot), lanes] = wb[c, span(slot), lanes] + ad[0, span(slot), lanes]

    def d_part(part, which, lanes_from=0, n=None):
        side = y if which == 0 else 1 - y
        n = width if n is None else n
        return wb[c, :, lanes_at((side * 2 + part) * width + lanes_from, n)]

    net.wait(wq_moves[0])
    net.wait(wq_moves[1])
    back = dot(d_part(0, 1), wa[pl.ds(width, width)], NT) + dot(d_part(1, 1), wa[pl.ds(2 * width, width)], NT)
    dm[...] = back.astype(BF)
    back_sends = [net.send(dm.at[span(slot)], dn.at[slot], place.to_y) for slot in range(slots)]
    pump()
    net.wait(normed_moves)
    grad_cols([(normed.at[0], lambda i: qv[:, lanes_at(i * 2 * block, 2 * block)])], gq, 0)
    sg[3:4] = col_sum(d_part(1, 0)) + col_sum(d_part(1, 1))
    pump()

    def kv_pairs(part):
        return [
            (normed.at[which], lambda i, which=which: d_part(part, which, i * 2 * block, 2 * block)) for which in range(2)
        ]

    grad_cols(kv_pairs(0), gq, width)
    pump()
    grad_cols(kv_pairs(1), gq, 2 * width)
    pump()
    net.wait(wq_moves[2])
    gain = full(0)
    for slot in range(slots):
        rows = span(slot)
        incoming = dot(qv[rows], wa[pl.ds(0, width)], NT)
        side = [wb[c, rows, lanes_at((y * 2 + part) * width, width)] for part in range(2)]
        incoming = incoming + dot(side[0], wa[pl.ds(width, width)], NT)
        incoming = incoming + dot(side[1], wa[pl.ds(2 * width, width)], NT)
        back_sends[slot].wait_recv()
        incoming = incoming + dn[slot].astype(F32)
        back, terms = norm_back(xv[slot].astype(F32), gain, incoming)
        xv[slot] = (res[rows] + back).astype(BF)
        terms, shifts = col_sum(terms), col_sum(incoming)
        gain_terms = terms if slot == 0 else gain_terms + terms
        shift_terms = shifts if slot == 0 else shift_terms + shifts
        if slot == 0:
            pump()
    out_moves = [net.move(xv, input_out)]
    sg[0:1] = gain_terms
    sg[1:2] = shift_terms
    per_row = width // wide
    for j in range(n_wide):
        sg[8 + j // per_row : 9 + j // per_row, (j % per_row) * wide : (j % per_row + 1) * wide] = ub[j]
    sg[12:16] = jnp.zeros((4, width), F32)

    sums = [net.send(sg, sr.at[0], place.to_c)]
    pump()
    sums[0].wait_recv()
    sr[4] = sg[...] + sr[0]
    sums.append(net.send(sr.at[4], sr.at[1], place.to_y))
    pump()
    sums[1].wait_recv()
    sr[5] = sr[4] + sr[1]
    sums += [net.send(sr.at[5], sr.at[7 + shift], place.to_z(shift)) for shift in range(1, shards)]
    pump()
    for copy in sums[2:]:
        copy.wait_recv()
    total = sr[5]
    for shift in range(1, shards):
        total = total + sr[7 + shift]
    sr[6] = total
    sums.append(net.send(sr.at[6], sr.at[2], place.to_x))
    pump()
    sums[-1].wait_recv()
    sr[3] = sr[6] + sr[2]
    out_moves.append(net.move(sr.at[3], sg_out))
    while any(st["stage"] < len(stages) for st in flights):
        pump()
    for _ in range(RING_A):
        pl.semaphore_wait(free_sems.at[0], 1)
    out_moves += [net.move(a, b) for a, b in ((gq, gq_out), (go, go_out), (gu, gu_out), (gd, gd_out))]
    finish(net, flights)


def finish(net, flights):
    done = set()
    for st in flights:
        for name, value in st.items():
            if name in ("s0", "s1", "sa", "sb", "s2", "s4"):
                done.update(id(copy) for copy in (value if isinstance(value, list) else [value]))
    for copy in net.remote:
        if id(copy) not in done:
            copy.wait_send()
    net.wait(net.local)


def backward(shards, x, cot, small, weights, gathered, kept):
    slots, length, width = x.shape
    tokens = slots * length
    hidden = weights[2].shape[1]
    down_rows = weights[3].shape[0]
    pairs = width // PAIR
    owned = weights[0].shape[0] // 4
    any_ = pl.BlockSpec(memory_space=pl.ANY)
    vmem = pl.BlockSpec(memory_space=pltpu.VMEM)
    sd = jax.ShapeDtypeStruct
    outs = (
        sd((slots, length, width), BF), sd((slots, length, width), BF), sd((owned, 3 * width), BF), sd((owned, width), BF),
        sd((owned, hidden), BF), sd((down_rows // 4, width), BF), sd((16, width), F32),
    )
    tile = (64, 256)
    return pl.pallas_call(
        functools.partial(backward_kernel, shards),
        out_shape=outs,
        in_specs=[any_] * 2 + [vmem] + [any_] * 17,
        out_specs=(any_,) * len(outs),
        scratch_shapes=[
            pltpu.VMEM((hidden, width), BF),
            pltpu.VMEM((2, width // 2, hidden), BF),
            pltpu.VMEM((2, tokens, hidden), BF),
            pltpu.VMEM((tokens, width), BF),
            pltpu.VMEM((tokens, width), BF),
            pltpu.VMEM((tokens, width), F32),
            pltpu.VMEM((tokens, width), BF),
            pltpu.VMEM((tokens, width), BF),
            pltpu.VMEM((tokens, width), BF),
            pltpu.VMEM((2, tokens, width), BF),
            pltpu.VMEM((slots, length, width), BF),
            pltpu.VMEM((slots, length, width), BF),
            pltpu.VMEM((slots, pairs, 1, 2 * length), F32),
            pltpu.VMEM((owned, 3 * width), BF),
            pltpu.VMEM((owned, width), BF),
            pltpu.VMEM((owned, hidden), BF),
            pltpu.VMEM((down_rows // 4, width), BF),
            pltpu.VMEM((16, width), F32),
            pltpu.VMEM((hidden // 512, 1, 512), F32),
            pltpu.VMEM((7 + shards, 16, width), F32),
            pltpu.VMEM((RING_A, 2, 4, 2, shards) + tile, BF),
            pltpu.VMEM((RING_A, 4, 2, shards) + tile, BF),
            pltpu.VMEM((RING_B, 2, 2, shards) + tile, BF),
            pltpu.VMEM((N_CHUNKS, 2, 4) + tile, BF),
            pltpu.VMEM((N_CHUNKS, 4) + tile, BF),
            pltpu.VMEM((N_CHUNKS, 2) + tile, BF),
            pltpu.VMEM((N_CHUNKS, 2) + tile, BF),
            pltpu.VMEM((RING_B, 2, 2, 4) + tile, BF),
            pltpu.VMEM((RING_B, 2, 4) + tile, BF),
            pltpu.VMEM((RING_B, 4) + tile, BF),
            pltpu.VMEM((RING_B, 2) + tile, BF),
            pltpu.SemaphoreType.DMA((N_REMOTE2,)),
            pltpu.SemaphoreType.DMA((N_REMOTE2,)),
            pltpu.SemaphoreType.DMA((N_LOCAL2,)),
            pltpu.SemaphoreType.REGULAR((4,)),
            pltpu.SemaphoreType.REGULAR,
        ],
        compiler_params=pltpu.CompilerParams(collective_id=2, has_side_effects=True, vmem_limit_bytes=63 * MIB),
    )(x, cot, small, *weights, *gathered, *kept)


def place_kernel(n, *refs):
    srcs, dsts = refs[: n + 1], refs[n + 1 : 2 * n + 3]
    small, bufs, wide, sems = refs[2 * n + 3], refs[2 * n + 4 : 3 * n + 4], refs[3 * n + 4 : -1], refs[-1]
    loads = [pltpu.make_async_copy(src, buf, sems.at[i]) for i, (src, buf) in enumerate(zip(srcs, bufs + (small,)))]
    for copy in loads:
        copy.start()
    stores = []
    for i in range(n):
        loads[i].wait()
        buf = bufs[i]
        if i >= 2:
            buf = wide[i - 2]
            buf[...] = bufs[i][...].astype(F32)
        stores.append(pltpu.make_async_copy(buf, dsts[i], sems.at[n + 1 + i]))
        stores[-1].start()
    loads[n].wait()
    at = lax.axis_index("shard") * lax.axis_size("seq") + lax.axis_index("seq")
    vec_out, up_out = dsts[n:]
    pair = small[0:8, pl.ds(pl.multiple_of(at // 2 * 128, 128), 128)]
    vec_out[...] = jnp.where(at % 2 == 0, pair[:, :64], pair[:, 64:])
    up_out[...] = small[pl.ds(8 + at // 4, 1), pl.ds(pl.multiple_of(at % 4 * 256, 256), 256)]
    for copy in stores:
        copy.wait()


def place_results(sums, *arrays):
    any_, vmem = pl.BlockSpec(memory_space=pl.ANY), pl.BlockSpec(memory_space=pltpu.VMEM)
    n = len(arrays)
    outs = tuple(jax.ShapeDtypeStruct(a.shape, F32 if a.ndim == 2 else BF) for a in arrays)
    return pl.pallas_call(
        functools.partial(place_kernel, n),
        out_shape=outs + (jax.ShapeDtypeStruct((8, 64), F32), jax.ShapeDtypeStruct((1, 256), F32)),
        in_specs=[any_] * (n + 1),
        out_specs=(any_,) * n + (vmem, vmem),
        scratch_shapes=[pltpu.VMEM(sums.shape, F32)]
        + [pltpu.VMEM(a.shape, BF) for a in arrays]
        + [pltpu.VMEM(a.shape, F32) for a in arrays[2:]]
        + [pltpu.SemaphoreType.DMA((2 * n + 1,))],
        compiler_params=pltpu.CompilerParams(vmem_limit_bytes=60 * MIB),
    )(*arrays, sums)


def local(
    activations, cotangent, clip_loads, attn_gain, attn_shift, w_qkv, q_bias, v_bias, w_out, out_bias,
    mlp_gain, mlp_shift, w_up, up_bias, w_down, down_bias,
):
    shards = lax.axis_size("shard")
    x, cot = activations[0], cotangent[0]
    slots, length, width = x.shape
    rows = w_qkv.shape[0]
    vectors = [attn_gain, attn_shift, q_bias, v_bias, out_bias, mlp_gain, mlp_shift, down_bias]
    vectors += [up_bias[i * rows : (i + 1) * rows] for i in range(4)]
    row = lax.broadcasted_iota(jnp.int32, (16, rows), 0)
    small = (row - len(vectors) < clip_loads[0]).astype(BF)
    for i, vector in enumerate(vectors):
        small = jnp.where(row == i, vector[None, :], small)
    weights = (w_qkv, w_out, w_up, w_down)
    *gathered, normed, q, kv, lse, att, res, nm, act, slope, small = forward(shards, x, small, *weights)
    kept = (normed, q, kv.reshape(-1, width), lse, att, res, nm, act, slope)
    layer_out, input_grad, gq, go, gu, gd, sums = backward(shards, x, cot, small, weights, gathered, kept)
    pods = lax.axis_size("replica")
    if pods > 2:
        ends = [[p for p in range(pods) if p % 2 == side] for side in range(2)]
        gq, go, gu, gd, sums = (lax.psum(g, "replica", axis_index_groups=ends) for g in (gq, go, gu, gd, sums))
    layer_out, input_grad, gq, go, gu, gd, vec, up = place_results(sums, layer_out, input_grad, gq, go, gu, gd)
    return (
        layer_out[None], input_grad[None], vec[0], vec[1], gq, vec[2], vec[3], go, vec[4], vec[5], vec[6], gu, up[0], gd, vec[7],
    )


def solution(mesh):
    rows = P("shard")
    full = P("shard", None)
    clips = P(("replica", "shard"), None, "seq", None)
    vec = P(("shard", "seq"))
    mat = P(("shard", "seq"), None)
    return jax.shard_map(
        local,
        mesh=mesh,
        in_specs=(
            clips, clips, P(("replica", "shard")), rows, rows, full, rows, rows, full, rows, rows, rows, full, rows, full, rows,
        ),
        out_specs=(clips, clips, vec, vec, mat, vec, vec, mat, vec, vec, vec, mat, vec, mat, vec),
        check_vma=False,
    )
```
